128 devices in a mesh: blk: 32 (over x_hi, z, y), rep: 4 (over x_lo, core).
Axes of the slice: x: 4 (x_hi: 2, x_lo: 2; x = x_hi * 2 + x_lo), y: 4, z: 4, core: 2. Of those that a mesh axis runs over, the one named last changes fastest.
Arguments:
- features: bfloat16 [32768, 512], P('blk', 'rep'), may hold values from -6 to 6
- weight: bfloat16 [512, 512], P('rep'), may hold values from -0.25 to 0.25
- bias_vector: float32 [512], replicated, may hold values from -3 to 3
- cotangent: bfloat16 [32768, 512], P('blk', 'rep'), may hold values from -6 to 6
- tile_masks: int32 [32, 256, 4, 16, 128], P('blk'), may hold values from 0 to 255, as said below
- tile_rows: int32 [32, 256, 4], P('blk'), may hold values from 0 to 7, as said below
- tile_counts: int32 [32, 256], P('blk'), may hold values from 0 to 4, as said below
Outputs:
- activation: float32 [32768, 512], P('blk', 'rep')
- grad_features: float32 [32768, 512], P('blk', 'rep')
- grad_weight: float32 [512, 512], P('rep')
- grad_bias: float32 [512], replicated
The draws below stay inside these ranges and needn't reach their ends.
Inputs may be any that keep to these rules, and one draw needn't show every extreme that they name: `tile_masks`: sparse edge bits. `tile_rows`: within one row block and tile column the live slots name different tile rows. `tile_counts`: each row block has a tile column with all 4 slots live; slots at or beyond the count are ignored.
All inputs are finite; a program needn't handle non-finite values.
Results may differ from the reference program's by a relative error of at most 0.0055.
Values may be sent and summed in bfloat16 or wider, within the bound.
A program may use at most 128 MiB of HBM per device.

```python
import jax
import jax.numpy as jnp
from jax import lax

INPUT_FEATURES = 512
FO = 512
TILE = 128
BLOCK_NODE_COUNT = 1024
BLOCKS = 32
NODES = 32768
ROWTILES = 8
COLTILES = 256
SLOTS = 4
WORDS = 16


def draw_tile_masks(key, part):
    key = jax.random.fold_in(key, 5)
    threshold = max(1, 65536 * 32 * ROWTILES // (COLTILES * SLOTS * TILE * 9 // 16))
    words = jnp.zeros((BLOCKS, COLTILES, SLOTS, WORDS, TILE), jnp.int32)
    for shift in range(8):
        trial = jax.random.randint(jax.random.fold_in(key, shift), (BLOCKS, COLTILES, SLOTS, WORDS, TILE), 0, 65536)
        words = words + (trial < threshold).astype(jnp.int32) * (1 << shift)
    return words


def draw_tile_rows(key, part):
    key = jax.random.fold_in(key, 11)
    scores = jax.random.randint(key, (BLOCKS, COLTILES, ROWTILES), 0, 1 << 20) * ROWTILES
    scores = scores + jnp.arange(ROWTILES, dtype=jnp.int32)
    ordering = jnp.argsort(scores, axis=-1)
    return ordering[..., :SLOTS].astype(jnp.int32)


def draw_tile_counts(key, part):
    key = jax.random.fold_in(key, 23)
    first_key, second_key, third_key = jax.random.split(key, 3)
    levels = jax.random.randint(first_key, (BLOCKS, 1, 1), 1, 9)
    trials = jax.random.randint(second_key, (BLOCKS, COLTILES, SLOTS), 0, 8) < levels
    counted = jnp.sum(trials.astype(jnp.int32), axis=-1)
    picked = jax.random.randint(third_key, (BLOCKS, 1), 0, COLTILES)
    columns = jnp.arange(COLTILES, dtype=jnp.int32)[None, :]
    return jnp.where(columns == picked, SLOTS, counted).astype(jnp.int32)


def block_levels(stream_key, extent, shards, low, top_value):
    def one(axis_at, parts):
        heights = jax.random.uniform(jax.random.fold_in(jax.random.fold_in(stream_key, 6), axis_at), (parts,), jnp.float32, low / len(shards), top_value / len(shards))
        return jnp.repeat(jnp.exp(heights), extent[axis_at] // parts).reshape((-1,) + (1,) * (len(extent) - axis_at - 1))

    loudness = one(*shards[0])
    for cut in shards[1:]:
        loudness = loudness * one(*cut)
    return loudness


def centred(own_key, dims, deviation, most, cuts=(), held_as=jnp.bfloat16):
    entries = deviation * jax.random.normal(own_key, dims, jnp.float32)
    if cuts:
        entries = entries * block_levels(own_key, dims, cuts, -0.22, 0.18)
    return jnp.clip(entries, -most, most).astype(held_as)


def setup_inputs(seed: int = 0) -> dict:
    seeds = jax.random.split(jax.random.key(seed), 8)
    return {
        "features": centred(seeds[0], (NODES, INPUT_FEATURES), 1.0, 6.0, ((0, 32), (1, 4))),
        "weight": centred(seeds[1], (INPUT_FEATURES, FO), INPUT_FEATURES ** -0.5, 0.25, ((0, 4),)),
        "bias_vector": centred(seeds[2], (FO,), 0.5, 3.0, (), jnp.float32),
        "cotangent": centred(seeds[3], (NODES, FO), 1.0, 6.0, ((0, 32), (1, 4))),
        "tile_masks": draw_tile_masks(jax.random.fold_in(seeds[7], 71), 0),
        "tile_rows": draw_tile_rows(jax.random.fold_in(seeds[7], 71), 0),
        "tile_counts": draw_tile_counts(jax.random.fold_in(seeds[7], 71), 0),
    }


def unpack_tiles(mask_words):
    shifts = jnp.arange(8, dtype=jnp.int32)
    bit_values = jnp.bitwise_and(jnp.right_shift(mask_words[..., None], shifts), 1)
    bit_values = jnp.swapaxes(bit_values, -3, -2)
    return bit_values.reshape(bit_values.shape[:-2] + (bit_values.shape[-2] * 8,))

def row_counts(mask_words):
    total = jnp.zeros(mask_words.shape[:-2] + (mask_words.shape[-1],), jnp.int32)
    for shift in range(8):
        total = total + lax.optimization_barrier(jnp.sum(jnp.bitwise_and(jnp.right_shift(mask_words, shift), 1), axis=-2))
    return total

def place_table(slot_rows, slot_counts, row_tiles):
    slot_count = slot_rows.shape[-1]
    is_live = jnp.arange(slot_count, dtype=jnp.int32) < slot_counts[..., None]
    hits = slot_rows[..., None] == jnp.arange(row_tiles, dtype=jnp.int32)
    return jnp.logical_and(hits, is_live[..., None]).astype(jnp.float32)

def reference(features, weight, bias_vector, cotangent, tile_masks, tile_rows, tile_counts):
    highest_precision = lax.Precision.HIGHEST
    row_tiles = BLOCK_NODE_COUNT // TILE

    def degree_block(inputs):
        mask_words, slot_rows, slot_counts = inputs
        tile_placement = place_table(slot_rows, slot_counts, row_tiles)
        counted = row_counts(mask_words).astype(jnp.float32)
        return jnp.einsum('gst,gsr->tr', tile_placement, counted, precision=highest_precision).reshape(BLOCK_NODE_COUNT)
    degrees = 1.0 + lax.map(degree_block, (tile_masks, tile_rows, tile_counts)).reshape(NODES)
    inv_root = lax.rsqrt(degrees)
    scaled = (features.astype(jnp.float32) * inv_root[:, None]).astype(jnp.bfloat16)
    scaled_tiles = scaled.astype(jnp.float32).reshape(COLTILES, TILE, INPUT_FEATURES)

    def gather_block(inputs):
        mask_words, slot_rows, slot_counts = inputs
        dense = unpack_tiles(mask_words).astype(jnp.float32)
        tile_products = jnp.einsum('gsrc,gcf->gsrf', dense, scaled_tiles, precision=highest_precision)
        tile_placement = place_table(slot_rows, slot_counts, row_tiles)
        return jnp.einsum('odu,odzy->uzy', tile_placement, tile_products, precision=highest_precision).reshape(BLOCK_NODE_COUNT, INPUT_FEATURES)
    neighbour_sums = lax.map(gather_block, (tile_masks, tile_rows, tile_counts)).reshape(NODES, INPUT_FEATURES)
    aggregate = (neighbour_sums * inv_root[:, None]).astype(jnp.bfloat16)
    hidden = jnp.dot(aggregate, weight, preferred_element_type=jnp.float32) + bias_vector
    logistic = jax.nn.sigmoid(hidden)
    activation = hidden * logistic
    slope_grad = (cotangent.astype(jnp.float32) * logistic * (1.0 + hidden * (1.0 - logistic))).astype(jnp.bfloat16)
    grad_weight = jnp.dot(aggregate.T, slope_grad, preferred_element_type=jnp.float32)
    grad_bias = lax.optimization_barrier(jnp.sum(slope_grad.astype(jnp.float32), axis=0))
    back_input = (jnp.dot(slope_grad, weight.T, preferred_element_type=jnp.float32) * inv_root[:, None]).astype(jnp.bfloat16)
    back_tiles = back_input.astype(jnp.float32).reshape(BLOCKS, row_tiles, TILE, INPUT_FEATURES)

    def scatter_block(running, inputs):
        mask_words, slot_rows, slot_counts, source_node = inputs
        dense = unpack_tiles(mask_words).astype(jnp.float32)
        tile_placement = place_table(slot_rows, slot_counts, row_tiles)
        selected_tile = jnp.einsum('qnz,zhb->qnhb', tile_placement, source_node, precision=highest_precision)
        return (running + jnp.einsum('gsrc,gsrf->gcf', dense, selected_tile, precision=highest_precision), None)
    initial = jnp.zeros((COLTILES, TILE, INPUT_FEATURES), jnp.float32)
    back_sums, _ = lax.scan(scatter_block, initial, (tile_masks, tile_rows, tile_counts, back_tiles))
    grad_features = back_sums.reshape(NODES, INPUT_FEATURES) * inv_root[:, None]
    return (activation, grad_features, grad_weight, grad_bias)
```

```python
import functools

import jax
import jax.numpy as jnp
import numpy as np
from jax import lax
from jax.experimental import pallas as pl
from jax.experimental.pallas import tpu as pltpu
from jax.sharding import PartitionSpec as P

MESH = pl.DeviceIdType.MESH
BF16 = jnp.bfloat16
F32 = jnp.float32
VMEM = pl.BlockSpec(memory_space=pltpu.VMEM)
SMEM = pl.BlockSpec(memory_space=pltpu.SMEM)
ANY = pl.BlockSpec(memory_space=pl.ANY)
DMA = pltpu.SemaphoreType.DMA
MIB = 2**20


class Place:
    def __init__(self):
        blk = lax.axis_index("blk")
        rep = lax.axis_index("rep")
        self.x, self.z, self.y = blk // 16, lax.rem(blk // 4, 4), lax.rem(blk, 4)
        self.xl, self.c = rep // 2, lax.rem(rep, 2)
        self.rep = rep
        self.xz = self.x * 4 + self.z

    def at(self, x=None, z=None, y=None, xl=None, c=None):
        x = self.x if x is None else x
        z = self.z if z is None else z
        y = self.y if y is None else y
        xl = self.xl if xl is None else xl
        c = self.c if c is None else c
        return (x * 16 + z * 4 + y, xl * 2 + c)

    def dy(self, n):
        return lax.rem(self.y + n, 4)

    def dz(self, n):
        return lax.rem(self.z + n, 4)


def greet(peers):
    barrier = pltpu.get_barrier_semaphore()
    for peer in peers:
        pl.semaphore_signal(barrier, inc=1, device_id=peer, device_id_type=MESH)
    pl.semaphore_wait(barrier, len(peers))


class Copies:
    def __init__(self, send, recv):
        self.send, self.recv, self.used = send, recv, []

    def start(self, src, dst, peer):
        n = len(self.used)
        copy = pltpu.make_async_remote_copy(
            src_ref=src, dst_ref=dst, send_sem=self.send.at[n], recv_sem=self.recv.at[n],
            device_id=peer, device_id_type=MESH,
        )
        copy.start()
        self.used.append(copy)
        return copy

    def wait_sends(self):
        for copy in self.used:
            copy.wait_send()


def prepare_kernel(meta_ref, masks_ref, feat_ref, perm_ref, m16_ref, xt_ref, row_ref, col_ref, d0, d1, d2, d3):
    step = pl.program_id(0)
    degs = (d0, d1, d2, d3)

    @pl.when(step == 0)
    def _():
        for d in degs:
            d[...] = jnp.zeros_like(d)

    group = masks_ref.shape[0]
    for g in range(group):
        for s in range(4):
            words = masks_ref[g, s]
            m16_ref[g, s * 16:(s + 1) * 16, :] = words.astype(jnp.int16)
            joined = jnp.bitwise_or(words[:8], jnp.left_shift(words[8:], 8))
            t = meta_ref[(step * group + g) * 4 + s]
            degs[s][t] += lax.population_count(joined)

    @pl.when(step == pl.num_programs(0) - 1)
    def _():
        total = (d0[0:8] + d1[0:8]) + (d2[0:8] + d3[0:8])
        degrees = 1.0 + jnp.sum(total, axis=1).astype(F32)
        inv = lax.rsqrt(degrees)
        for t in range(8):
            lanes = inv[t:t + 1, :]
            row_ref[:, t * 128:(t + 1) * 128] = jnp.broadcast_to(lanes, (8, 128))
            spread = jnp.broadcast_to(lanes, (128, 128))
            col_ref[t * 128:(t + 1) * 128, :] = spread.T
            feat = feat_ref[t * 128:(t + 1) * 128, :].astype(F32).T
            scaled = (feat * spread).astype(BF16)
            moved = jnp.dot(scaled, perm_ref[...], preferred_element_type=F32).astype(BF16)
            xt_ref[t // 4, :, (t % 4) * 128:(t % 4 + 1) * 128] = moved


def prepare(meta, masks, features, perm):
    group = 16
    steps = 256 // group
    fixed = lambda *shape: pl.BlockSpec(shape, lambda i: (0,) * len(shape))
    return pl.pallas_call(
        prepare_kernel,
        grid=(steps,),
        out_shape=(
            jax.ShapeDtypeStruct((256, 64, 128), jnp.int16),
            jax.ShapeDtypeStruct((2, 128, 512), BF16),
            jax.ShapeDtypeStruct((8, 1024), F32),
            jax.ShapeDtypeStruct((1024, 128), F32),
        ),
        in_specs=[
            SMEM,
            pl.BlockSpec((group, 4, 16, 128), lambda i: (i, 0, 0, 0)),
            fixed(1024, 128),
            fixed(128, 128),
        ],
        out_specs=(
            pl.BlockSpec((group, 64, 128), lambda i: (i, 0, 0)),
            fixed(2, 128, 512),
            fixed(8, 1024),
            fixed(1024, 128),
        ),
        scratch_shapes=[pltpu.VMEM((9, 8, 128), jnp.int32)] * 4,
        compiler_params=pltpu.CompilerParams(
            dimension_semantics=("arbitrary",), vmem_limit_bytes=24 * MIB
        ),
        name="prepare",
    )(meta, masks, features, perm)


def spread_kernel(m16, meta, xt, w, rm, rmeta, g, wc, send, recv, local):
    me = Place()
    sibling = me.at(c=1 - me.c)
    x_peer = me.at(x=1 - me.x)
    z_peers = [me.at(z=me.dz(n)) for n in (1, 2, 3)]
    y_peers = [me.at(y=me.dy(n)) for n in (1, 2, 3)]
    rep_peers = [sibling, me.at(xl=1 - me.xl), me.at(xl=1 - me.xl, c=1 - me.c)]
    greet(z_peers + y_peers + rep_peers + [x_peer])

    copies = Copies(send, recv)
    own, other = me.c, 1 - me.c
    to_sibling = copies.start(xt.at[other], g.at[me.xz, own], sibling)
    first = [copies.start(xt.at[own], g.at[me.xz, own], p) for p in z_peers]
    across = copies.start(xt.at[own], g.at[me.xz, own], x_peer)
    masks = []
    for n in (1, 2, 3):
        there = me.dy(n)
        peer = y_peers[n - 1]
        masks.append(copies.start(meta.at[there, own], rmeta.at[me.y], peer))
        masks.append(copies.start(m16.at[:, there, own], rm.at[me.y], peer))
    stays = [
        pltpu.make_async_copy(m16.at[:, me.y, own], rm.at[me.y], local.at[0]),
        pltpu.make_async_copy(meta.at[me.y, own], rmeta.at[me.y], local.at[1]),
        pltpu.make_async_copy(xt.at[own], g.at[me.xz, own], local.at[2]),
        pltpu.make_async_copy(w.at[me.rep], wc.at[me.rep], local.at[3]),
    ]
    for copy in stays:
        copy.start()
    weights = []
    for peer in rep_peers:
        weights.append(copies.start(w.at[peer[1]], wc.at[me.rep], peer))

    to_sibling.wait_recv()
    other_x = copies.start(g.at[me.xz, other], g.at[me.xz, other], x_peer)
    second = [copies.start(g.at[me.xz, other], g.at[me.xz, other], p) for p in z_peers]
    last = []
    for n in (1, 2, 3):
        first[n - 1].wait_recv()
        source = me.x * 4 + me.dz(4 - n)
        last.append(copies.start(g.at[source, own], g.at[source, own], x_peer))
    other_x.wait_recv()
    far = (1 - me.x) * 4 + me.z
    last += [copies.start(g.at[far, other], g.at[far, other], p) for p in z_peers]
    for copy in [across] + masks + weights + second + last:
        copy.wait_recv()
    copies.wait_sends()
    for copy in stays:
        copy.wait()


def spread(m16, meta, xt, w):
    return pl.pallas_call(
        spread_kernel,
        out_shape=(
            jax.ShapeDtypeStruct((4, 8, 4, 64, 128), jnp.int16),
            jax.ShapeDtypeStruct((4, 8, 128), jnp.int32),
            jax.ShapeDtypeStruct((8, 2, 128, 512), BF16),
            jax.ShapeDtypeStruct((4, 128, 128), BF16),
        ),
        in_specs=[ANY, VMEM, VMEM, VMEM],
        out_specs=(VMEM, VMEM, VMEM, VMEM),
        scratch_shapes=[DMA((24,)), DMA((24,)), DMA((4,))],
        compiler_params=pltpu.CompilerParams(
            collective_id=0, has_side_effects=True, vmem_limit_bytes=24 * MIB
        ),
        name="spread",
    )(m16, meta, xt, w)


def unpack_chunk(i, j, masks_ref, meta_ref, dense_ref, out_ref):
    one, zero = jnp.asarray(1, BF16), jnp.asarray(0, BF16)
    for tc in range(4):
        dense_ref[tc, 0:8] = jnp.zeros((8, 16, 128), jnp.int16)
        for s in range(4):
            t = meta_ref[i, 0, (j * 4 + tc) * 4 + s]
            dense_ref[tc, t] = masks_ref[i, j, tc, s * 16:(s + 1) * 16, :]
    for tc in range(4):
        for t in range(8):
            words = dense_ref[tc, t]
            for k in range(8):
                bits = jnp.where(jnp.bitwise_and(words, jnp.int16(1 << k)) != 0, one, zero)
                row = tc * 128 + k * 16
                out_ref[row:row + 16, t * 128:(t + 1) * 128] = bits


def forward_kernel(meta_ref, masks_ref, g_ref, o_ref, dense, a0, a1, acc):
    bufs = (a0, a1)
    unpack_chunk(0, 0, masks_ref, meta_ref, dense, a0)

    def step(n, _):
        i, pair = n // 4, lax.rem(n, 4)
        for h in range(2):
            later = jnp.minimum(n * 2 + h + 1, 31)
            unpack_chunk(later // 8, lax.rem(later, 8), masks_ref, meta_ref, dense, bufs[1 - h])
            prod = jnp.dot(g_ref[pair * 2 + h], bufs[h][...], preferred_element_type=F32)
            if h == 0:
                acc[...] = jnp.where(pair == 0, 0.0, acc[...]) + prod
            else:
                acc[...] += prod

        @pl.when(pair == 3)
        def _():
            o_ref[i] = acc[...].astype(BF16)

        return 0

    lax.fori_loop(0, 16, step, 0)


def backward_kernel(meta_ref, masks_ref, b_ref, o_ref, dense, a0, a1, acc):
    bufs = (a0, a1)
    unpack_chunk(0, 0, masks_ref, meta_ref, dense, a0)

    def step(n, _):
        j, pair = n // 2, lax.rem(n, 2)
        for h in range(2):
            later = jnp.minimum(n * 2 + h + 1, 31)
            unpack_chunk(lax.rem(later, 4), later // 4, masks_ref, meta_ref, dense, bufs[1 - h])
            prod = jnp.dot(bufs[h][...], b_ref[pair * 2 + h], preferred_element_type=F32)
            if h == 0:
                acc[...] = jnp.where(pair == 0, 0.0, acc[...]) + prod
            else:
                acc[...] += prod

        @pl.when(pair == 1)
        def _():
            o_ref[j] = acc[...].astype(BF16)

        return 0

    lax.fori_loop(0, 16, step, 0)


def product(kernel, name, out_shape, acc_shape, meta, masks, dense):
    return pl.pallas_call(
        kernel,
        out_shape=jax.ShapeDtypeStruct(out_shape, BF16),
        in_specs=[SMEM, VMEM, VMEM],
        out_specs=VMEM,
        scratch_shapes=[
            pltpu.VMEM((4, 9, 16, 128), jnp.int16),
            pltpu.VMEM((512, 1024), BF16),
            pltpu.VMEM((512, 1024), BF16),
            pltpu.VMEM(acc_shape, F32),
        ],
        compiler_params=pltpu.CompilerParams(vmem_limit_bytes=24 * MIB),
        name=name,
    )(meta, masks, dense)


def middle_kernel(part, row, col, wc, w, bias, cot, act, ball, gwx,
                  rc, snd, ry, agg, agg_t, slope, send, recv):
    me = Place()
    sibling = me.at(c=1 - me.c)
    xl_peer = me.at(xl=1 - me.xl)
    y_peers = [me.at(y=me.dy(n)) for n in (1, 2, 3)]
    greet([sibling, xl_peer] + y_peers)
    copies = Copies(send, recv)
    own, other = me.c, 1 - me.c

    halves = {}
    for n in (2, 1, 3, 0):
        halves[n] = copies.start(part.at[me.dy(n), other], rc.at[n], sibling)
    sums = {}
    for n in (2, 1, 3):
        halves[n].wait_recv()
        snd[n - 1] = (part[me.dy(n), own].astype(F32) + rc[n].astype(F32)).astype(BF16)
        sums[n] = copies.start(snd.at[n - 1], ry.at[n - 1], y_peers[n - 1])
    halves[0].wait_recv()
    for n in (1, 3, 2):
        sums[n].wait_recv()
    for t in range(8):
        lanes = slice(t * 128, (t + 1) * 128)
        total = part[me.y, own, :, lanes].astype(F32) + rc[0, :, lanes].astype(F32)
        for n in range(3):
            total = total + ry[n, :, lanes].astype(F32)
        total = total * row[0:1, lanes]
        agg_t[:, lanes] = total.astype(BF16)
        agg[me.rep, lanes, :] = total.T.astype(BF16)

    def gather_rep(buf):
        near = copies.start(buf.at[me.rep], buf.at[me.rep], sibling)
        far = copies.start(buf.at[me.rep], buf.at[me.rep], xl_peer)
        far.wait_recv()
        theirs = (1 - me.xl) * 2 + me.c
        passed = copies.start(buf.at[theirs], buf.at[theirs], sibling)
        near.wait_recv()
        passed.wait_recv()

    gather_rep(agg)

    def rows_forward(m, _):
        rows = pl.ds(pl.multiple_of(m * 256, 256), 256)
        hidden = jnp.dot(agg[0, rows, :], wc[0], preferred_element_type=F32)
        for q in range(1, 4):
            hidden = hidden + jnp.dot(agg[q, rows, :], wc[q], preferred_element_type=F32)
        hidden = hidden + bias[me.rep, 0:1, :]
        logistic = jax.nn.sigmoid(hidden)
        act[rows, :] = hidden * logistic
        value = cot[rows, :].astype(F32) * logistic * (1.0 + hidden * (1.0 - logistic))
        slope[me.rep, rows, :] = value.astype(BF16)
        return 0

    lax.fori_loop(0, 4, rows_forward, 0)
    gather_rep(slope)

    mine = pl.ds(pl.multiple_of(own * 128, 128), 128)

    def rows_backward(m, _):
        rows = pl.ds(pl.multiple_of(m * 256, 256), 256)
        total = jnp.zeros((256, 128), F32)
        for q in range(4):
            total = total + lax.dot_general(
                slope[q, rows, :], w[q], (((1,), (1,)), ((), ())), preferred_element_type=F32
            )
        ball[me.y, rows, mine] = (total * col[rows, :]).astype(BF16)
        return 0

    lax.fori_loop(0, 4, rows_backward, 0)
    block = ball.at[me.y, :, mine]
    gathered = [copies.start(block, block, p) for p in y_peers]
    shared = [copies.start(block, block, sibling)]
    ones = jnp.ones((8, 1024), BF16)
    for q in range(4):
        lanes = slice(q * 128, (q + 1) * 128)
        grad = jnp.dot(agg_t[...], slope[q], preferred_element_type=F32)
        gb = jnp.dot(ones, slope[q], preferred_element_type=F32)
        for n in range(4):
            gwx[n, 0:32, lanes] = grad[n * 32:(n + 1) * 32]
            gwx[n, 32:40, lanes] = gb
    for n in (1, 3, 2):
        gathered[n - 1].wait_recv()
        block = ball.at[me.dy(4 - n), :, mine]
        shared.append(copies.start(block, block, sibling))
    for copy in shared:
        copy.wait_recv()
    copies.wait_sends()


def middle(part, row, col, wc, w, bias, cot):
    return pl.pallas_call(
        middle_kernel,
        out_shape=(
            jax.ShapeDtypeStruct((1024, 128), F32),
            jax.ShapeDtypeStruct((4, 1024, 256), BF16),
            jax.ShapeDtypeStruct((4, 40, 512), F32),
        ),
        in_specs=[VMEM] * 7,
        out_specs=(VMEM, VMEM, VMEM),
        scratch_shapes=[
            pltpu.VMEM((4, 128, 1024), BF16),
            pltpu.VMEM((3, 128, 1024), BF16),
            pltpu.VMEM((3, 128, 1024), BF16),
            pltpu.VMEM((4, 1024, 128), BF16),
            pltpu.VMEM((128, 1024), BF16),
            pltpu.VMEM((4, 1024, 128), BF16),
            DMA((24,)),
            DMA((24,)),
        ],
        compiler_params=pltpu.CompilerParams(
            collective_id=1, has_side_effects=True, vmem_limit_bytes=32 * MIB
        ),
        name="middle",
    )(part, row, col, wc, w, bias, cot)


def settle_kernel(part, gwx, out, gw, az, a_sum, ax, bx, b_sum, bz, final,
                  wy, wz, wx_send, wx, send, recv, local):
    me = Place()
    sibling = me.at(c=1 - me.c)
    x_peer = me.at(x=1 - me.x)
    z_peers = [me.at(z=me.dz(n)) for n in (1, 2, 3)]
    y_peers = [me.at(y=me.dy(n)) for n in (1, 2, 3)]
    greet(z_peers + y_peers + [x_peer, sibling])
    copies = Copies(send, recv)
    own_x, other_x = me.x, 1 - me.x

    to_x = [copies.start(part.at[other_x, me.dz(n), 1], bx.at[n], x_peer) for n in (2, 1, 3, 0)]
    to_x = dict(zip((2, 1, 3, 0), to_x))
    weights = [copies.start(gwx.at[me.dy(n)], wy.at[me.y], y_peers[n - 1]) for n in (1, 2, 3)]
    to_z = {}
    for side in (1, 0):
        for n in (2, 1, 3):
            x_at = other_x if side else own_x
            to_z[side, n] = copies.start(part.at[x_at, me.dz(n), 0], az.at[side, n - 1], z_peers[n - 1])
    wy[me.y] = gwx[me.y]

    for copy in weights:
        copy.wait_recv()
    wz[me.z] = (wy[0] + wy[1]) + (wy[2] + wy[3])
    weights = [copies.start(wz.at[me.z], wz.at[me.z], p) for p in z_peers]

    b_out = {}
    for n in (2, 1, 3):
        to_x[n].wait_recv()
        b_sum[n - 1] = (part[own_x, me.dz(n), 1].astype(F32) + bx[n].astype(F32)).astype(BF16)
        b_out[n] = copies.start(b_sum.at[n - 1], bz.at[n - 1], z_peers[n - 1])
    for n in (1, 3, 2):
        to_z[1, n].wait_recv()
    total = part[other_x, me.z, 0].astype(F32)
    for n in range(3):
        total = total + az[1, n].astype(F32)
    a_sum[...] = total.astype(BF16)
    a_out = copies.start(a_sum, ax, x_peer)

    for copy in weights:
        copy.wait_recv()
    wx_send[...] = (wz[0] + wz[1]) + (wz[2] + wz[3])
    weight_x = copies.start(wx_send, wx, x_peer)

    to_x[0].wait_recv()
    for n in (1, 3, 2):
        b_out[n].wait_recv()
    total = part[own_x, me.z, 1].astype(F32) + bx[0].astype(F32)
    for n in range(3):
        total = total + bz[n].astype(F32)
    final[0, 256:512, :] = total[:, 0:128]
    final[1, 256:512, :] = total[:, 128:256]

    weight_x.wait_recv()
    gw[me.y] = wx_send[...] + wx[...]
    weights = [copies.start(gw.at[me.y], gw.at[me.y], p) for p in y_peers]

    for n in (1, 3, 2):
        to_z[0, n].wait_recv()
    a_out.wait_recv()
    total = part[own_x, me.z, 0].astype(F32) + ax[...].astype(F32)
    for n in range(3):
        total = total + az[0, n].astype(F32)
    final[0, 0:256, :] = total[:, 0:128]
    final[1, 0:256, :] = total[:, 128:256]
    swap = copies.start(final.at[1 - me.c], out.at[me.c], sibling)
    keep = pltpu.make_async_copy(final.at[me.c], out.at[me.c], local)
    keep.start()
    swap.wait_recv()
    for copy in weights:
        copy.wait_recv()
    keep.wait()
    copies.wait_sends()


def settle(part, gwx):
    half = (256, 256)
    return pl.pallas_call(
        settle_kernel,
        out_shape=(
            jax.ShapeDtypeStruct((2, 512, 128), F32),
            jax.ShapeDtypeStruct((4, 40, 512), F32),
        ),
        in_specs=[VMEM, VMEM],
        out_specs=(VMEM, VMEM),
        scratch_shapes=[
            pltpu.VMEM((2, 3) + half, BF16),
            pltpu.VMEM(half, BF16),
            pltpu.VMEM(half, BF16),
            pltpu.VMEM((4,) + half, BF16),
            pltpu.VMEM((3,) + half, BF16),
            pltpu.VMEM((3,) + half, BF16),
            pltpu.VMEM((2, 512, 128), F32),
            pltpu.VMEM((4, 40, 512), F32),
            pltpu.VMEM((4, 40, 512), F32),
            pltpu.VMEM((40, 512), F32),
            pltpu.VMEM((40, 512), F32),
            DMA((28,)),
            DMA((28,)),
            DMA,
        ],
        compiler_params=pltpu.CompilerParams(
            collective_id=2, has_side_effects=True, vmem_limit_bytes=32 * MIB
        ),
        name="settle",
    )(part, gwx)


def body(features, weight, bias_vector, cotangent, tile_masks, tile_rows, tile_counts):
    perm = np.zeros((128, 128), np.float32)
    for w in range(16):
        for k in range(8):
            perm[8 * w + k, 16 * k + w] = 1.0
    live = jnp.arange(4, dtype=jnp.int32) < tile_counts[0][:, None]
    place = jnp.where(live, tile_rows[0], 8).astype(jnp.int32)
    meta = place.reshape(8, 4, 2, 16).transpose(1, 2, 0, 3).reshape(4, 2, 1, 128)
    meta = jnp.broadcast_to(meta, (4, 2, 8, 128))
    weight_q = weight.reshape(128, 4, 128).transpose(1, 0, 2)

    m16, xt, row, col = prepare(place.reshape(1024), tile_masks[0], features, jnp.asarray(perm, BF16))
    rm, rmeta, g, wc = spread(m16.reshape(8, 4, 2, 4, 64, 128), meta, xt, weight_q)
    part = product(forward_kernel, "forward", (4, 256, 1024), (256, 1024), rmeta, rm, g.reshape(8, 256, 512))
    bias = jnp.broadcast_to(bias_vector.reshape(4, 1, 128), (4, 8, 128))
    act, ball, gwx = middle(part.reshape(4, 2, 128, 1024), row, col, wc, weight_q, bias, cotangent)
    back = product(backward_kernel, "backward", (8, 512, 256), (512, 256), rmeta, rm, ball)
    out, gw = settle(back.reshape(2, 4, 2, 256, 256), gwx)
    out = out.reshape(8, 8, 16, 128).transpose(0, 2, 1, 3).reshape(1024, 128) * col
    return act, out, gw[:, :32].reshape(128, 512), gw[0, 32]


def solution(mesh):
    return jax.shard_map(
        body,
        mesh=mesh,
        in_specs=(
            P("blk", "rep"),
            P("rep", None),
            P(),
            P("blk", "rep"),
            P("blk", None, None, None, None),
            P("blk", None, None),
            P("blk", None),
        ),
        out_specs=(P("blk", "rep"), P("blk", "rep"), P("rep", None), P()),
        check_vma=False,
    )
```

```python
import functools

import jax
import jax.numpy as jnp
import numpy as np
from jax import lax
from jax.experimental import pallas as pl
from jax.experimental.pallas import tpu as pltpu
from jax.sharding import PartitionSpec as P

MESH = pl.DeviceIdType.MESH
BF16 = jnp.bfloat16
F32 = jnp.float32
VMEM = pl.BlockSpec(memory_space=pltpu.VMEM)
SMEM = pl.BlockSpec(memory_space=pltpu.SMEM)
DMA = pltpu.SemaphoreType.DMA
MIB = 2**20


class Place:
    def __init__(self):
        blk = lax.axis_index("blk")
        rep = lax.axis_index("rep")
        self.x, self.z, self.y = blk // 16, lax.rem(blk // 4, 4), lax.rem(blk, 4)
        self.xl, self.c = rep // 2, lax.rem(rep, 2)
        self.rep = rep
        self.xz = self.x * 4 + self.z

    def at(self, x=None, z=None, y=None, xl=None, c=None):
        x = self.x if x is None else x
        z = self.z if z is None else z
        y = self.y if y is None else y
        xl = self.xl if xl is None else xl
        c = self.c if c is None else c
        return (x * 16 + z * 4 + y, xl * 2 + c)

    def dy(self, n):
        return lax.rem(self.y + n, 4)

    def dz(self, n):
        return lax.rem(self.z + n, 4)


def greet(peers):
    barrier = pltpu.get_barrier_semaphore()
    for peer in peers:
        pl.semaphore_signal(barrier, inc=1, device_id=peer, device_id_type=MESH)
    pl.semaphore_wait(barrier, len(peers))


class Copies:
    def __init__(self, send, recv):
        self.send, self.recv, self.used = send, recv, []

    def start(self, src, dst, peer):
        n = len(self.used)
        copy = pltpu.make_async_remote_copy(
            src_ref=src, dst_ref=dst, send_sem=self.send.at[n], recv_sem=self.recv.at[n],
            device_id=peer, device_id_type=MESH,
        )
        copy.start()
        self.used.append(copy)
        return copy

    def wait_sends(self):
        for copy in self.used:
            copy.wait_send()


def prepare_kernel(meta_ref, masks_ref, feat_ref, perm_ref, m16_ref, xt_ref, row_ref, col_ref, d0, d1, d2, d3):
    step = pl.program_id(0)
    degs = (d0, d1, d2, d3)

    @pl.when(step == 0)
    def _():
        for d in degs:
            d[...] = jnp.zeros_like(d)

    group = masks_ref.shape[0]
    for g in range(group):
        for s in range(4):
            words = masks_ref[g, s]
            m16_ref[g, s * 16:(s + 1) * 16, :] = words.astype(jnp.int16)
            joined = jnp.bitwise_or(words[:8], jnp.left_shift(words[8:], 8))
            t = meta_ref[(step * group + g) * 4 + s]
            degs[s][t] += lax.population_count(joined)

    @pl.when(step == pl.num_programs(0) - 1)
    def _():
        total = (d0[0:8] + d1[0:8]) + (d2[0:8] + d3[0:8])
        degrees = 1.0 + jnp.sum(total, axis=1).astype(F32)
        inv = lax.rsqrt(degrees)
        for t in range(8):
            lanes = inv[t:t + 1, :]
            row_ref[:, t * 128:(t + 1) * 128] = jnp.broadcast_to(lanes, (8, 128))
            spread = jnp.broadcast_to(lanes, (128, 128))
            col_ref[t * 128:(t + 1) * 128, :] = spread.T
            feat = feat_ref[t * 128:(t + 1) * 128, :].astype(F32).T
            scaled = (feat * spread).astype(BF16)
            moved = jnp.dot(scaled, perm_ref[...], preferred_element_type=F32).astype(BF16)
            xt_ref[t // 4, :, (t % 4) * 128:(t % 4 + 1) * 128] = moved


def prepare(meta, masks, features, perm):
    group = 16
    steps = 256 // group
    fixed = lambda *shape: pl.BlockSpec(shape, lambda i: (0,) * len(shape))
    return pl.pallas_call(
        prepare_kernel,
        grid=(steps,),
        out_shape=(
            jax.ShapeDtypeStruct((256, 64, 128), jnp.int16),
            jax.ShapeDtypeStruct((2, 128, 512), BF16),
            jax.ShapeDtypeStruct((8, 1024), F32),
            jax.ShapeDtypeStruct((1024, 128), F32),
        ),
        in_specs=[
            SMEM,
            pl.BlockSpec((group, 4, 16, 128), lambda i: (i, 0, 0, 0)),
            fixed(1024, 128),
            fixed(128, 128),
        ],
        out_specs=(
            pl.BlockSpec((group, 64, 128), lambda i: (i, 0, 0)),
            fixed(2, 128, 512),
            fixed(8, 1024),
            fixed(1024, 128),
        ),
        scratch_shapes=[pltpu.VMEM((9, 8, 128), jnp.int32)] * 4,
        compiler_params=pltpu.CompilerParams(
            dimension_semantics=("arbitrary",), vmem_limit_bytes=24 * MIB
        ),
        name="prepare",
    )(meta, masks, features, perm)


def spread_kernel(m16, meta, xt, w, rm, rmeta, g, wc, send, recv, local):
    me = Place()
    sibling = me.at(c=1 - me.c)
    x_peer = me.at(x=1 - me.x)
    z_peers = [me.at(z=me.dz(n)) for n in (1, 2, 3)]
    y_peers = [me.at(y=me.dy(n)) for n in (1, 2, 3)]
    rep_peers = [sibling, me.at(xl=1 - me.xl), me.at(xl=1 - me.xl, c=1 - me.c)]
    greet(z_peers + y_peers + rep_peers + [x_peer])

    copies = Copies(send, recv)
    own, other = me.c, 1 - me.c

    def at(core, xz):
        return g.at[core, :, pl.ds(pl.multiple_of(xz * 512, 512), 512)]

    to_sibling = copies.start(xt.at[other], at(own, me.xz), sibling)
    first = [copies.start(xt.at[own], at(own, me.xz), p) for p in z_peers]
    across = copies.start(xt.at[own], at(own, me.xz), x_peer)
    masks = []
    for n in (1, 2, 3):
        there = me.dy(n)
        peer = y_peers[n - 1]
        masks.append(copies.start(meta.at[there, own], rmeta.at[me.y], peer))
        masks.append(copies.start(m16.at[:, there, own], rm.at[me.y], peer))
    stays = [
        pltpu.make_async_copy(m16.at[:, me.y, own], rm.at[me.y], local.at[0]),
        pltpu.make_async_copy(meta.at[me.y, own], rmeta.at[me.y], local.at[1]),
        pltpu.make_async_copy(xt.at[own], at(own, me.xz), local.at[2]),
        pltpu.make_async_copy(w.at[me.rep], wc.at[me.rep], local.at[3]),
    ]
    for copy in stays:
        copy.start()
    weights = []
    for peer in rep_peers:
        weights.append(copies.start(w.at[peer[1]], wc.at[me.rep], peer))

    to_sibling.wait_recv()
    other_x = copies.start(at(other, me.xz), at(other, me.xz), x_peer)
    second = [copies.start(at(other, me.xz), at(other, me.xz), p) for p in z_peers]
    last = []
    for n in (1, 2, 3):
        first[n - 1].wait_recv()
        source = me.x * 4 + me.dz(4 - n)
        last.append(copies.start(at(own, source), at(own, source), x_peer))
    other_x.wait_recv()
    far = (1 - me.x) * 4 + me.z
    last += [copies.start(at(other, far), at(other, far), p) for p in z_peers]
    for copy in [across] + masks + weights + second + last:
        copy.wait_recv()
    copies.wait_sends()
    for copy in stays:
        copy.wait()


def spread(m16, meta, xt, w):
    return pl.pallas_call(
        spread_kernel,
        out_shape=(
            jax.ShapeDtypeStruct((4, 8, 4, 64, 128), jnp.int16),
            jax.ShapeDtypeStruct((4, 8, 128), jnp.int32),
            jax.ShapeDtypeStruct((2, 128, 4096), BF16),
            jax.ShapeDtypeStruct((4, 128, 128), BF16),
        ),
        in_specs=[VMEM] * 4,
        out_specs=(VMEM, VMEM, VMEM, VMEM),
        scratch_shapes=[DMA((24,)), DMA((24,)), DMA((4,))],
        compiler_params=pltpu.CompilerParams(
            collective_id=0, has_side_effects=True, vmem_limit_bytes=24 * MIB
        ),
        name="spread",
    )(m16, meta, xt, w)


def place_kernel(meta_ref, masks_ref, dense_ref):
    def chunk(n, _):
        i, j = n // 8, lax.rem(n, 8)
        for tc in range(4):
            dense_ref[n, tc, 0:8] = jnp.zeros((8, 16, 128), jnp.int16)
            for s in range(4):
                t = meta_ref[i, 0, (j * 4 + tc) * 4 + s]
                dense_ref[n, tc, t] = masks_ref[i, j, tc, s * 16:(s + 1) * 16, :]
        return 0

    lax.fori_loop(0, 32, chunk, 0)


def place_tiles(meta, masks):
    return pl.pallas_call(
        place_kernel,
        out_shape=jax.ShapeDtypeStruct((32, 4, 9, 16, 128), jnp.int16),
        in_specs=[SMEM, VMEM],
        out_specs=VMEM,
        compiler_params=pltpu.CompilerParams(vmem_limit_bytes=16 * MIB),
        name="place",
    )(meta, masks)


def table(values, step):
    found = values[-1]
    for n in range(len(values) - 1):
        found = jnp.where(step == n, values[n], found)
    return found


def put_bits(words, out_ref, row, lane):
    one, zero = jnp.asarray(1, BF16), jnp.asarray(0, BF16)
    for k in range(8):
        bits = jnp.where(jnp.bitwise_and(words, jnp.int16(1 << k)) != 0, one, zero)
        out_ref[row + k * 16:row + (k + 1) * 16, lane:lane + 128] = bits


def layer_kernel(dense, g, row, col, wc, w, bias, cot, act, ball, gwx,
                 a0, a1, part, rc, snd, ry, agg, agg_t, slope,
                 core_s, core_r, sum_s, sum_r, send, recv):
    me = Place()
    sibling = me.at(c=1 - me.c)
    xl_peer = me.at(xl=1 - me.xl)
    y_peers = [me.at(y=me.dy(n)) for n in (1, 2, 3)]
    greet([sibling, xl_peer] + y_peers)
    copies = Copies(send, recv)
    own, other = me.c, 1 - me.c

    def unpack(s, out):
        i, pair = me.dy(table((2, 1, 3, 0), s // 4)), lax.rem(s, 4)
        for j in range(8):
            for tc in range(4):
                for t in range(2):
                    words = dense[i * 8 + j, tc, pair * 2 + t]
                    put_bits(words, out, j * 512 + tc * 128, t * 128)

    def to_sibling(s):
        return pltpu.make_async_remote_copy(
            src_ref=part.at[s, other], dst_ref=rc.at[s], send_sem=core_s.at[s], recv_sem=core_r.at[s],
            device_id=sibling, device_id_type=MESH,
        )

    def to_owner(s):
        return pltpu.make_async_remote_copy(
            src_ref=snd.at[s], dst_ref=ry.at[s], send_sem=sum_s.at[s], recv_sem=sum_r.at[s],
            device_id=me.at(y=me.dy(table((2, 1, 3), s // 4))), device_id_type=MESH,
        )

    def pass_on(s):
        to_sibling(s).wait_recv()
        snd[s] = (part[s, own].astype(F32) + rc[s].astype(F32)).astype(BF16)
        to_owner(s).start()

    def rows_of(m):
        return pl.ds(pl.multiple_of(m * 256, 256), 256)

    def rep_copy(buf, base, m, kind):
        theirs = (1 - me.xl) * 2 + me.c
        src = buf.at[theirs if kind == 2 else me.rep, rows_of(m), :]
        n = base + kind * 4 + m
        return pltpu.make_async_remote_copy(
            src_ref=src, dst_ref=src, send_sem=send.at[n], recv_sem=recv.at[n],
            device_id=xl_peer if kind == 1 else sibling, device_id_type=MESH,
        )

    def share(buf, base, m):
        rep_copy(buf, base, m, 1).start()
        rep_copy(buf, base, m, 0).start()

    def finish_sum(m):
        to_sibling(12 + m).wait_recv()
        for k in range(3):
            to_owner(4 * k + m).wait_recv()
        rows = rows_of(m)
        total = part[12 + m, own].astype(F32) + rc[12 + m].astype(F32)
        for k in range(3):
            total = total + ry[4 * k + m].astype(F32)
        total = total * row[0:1, rows]
        agg_t[:, rows] = total.astype(BF16)
        agg[me.rep, rows, :] = total.T.astype(BF16)
        share(agg, 0, m)

    bufs = (a0, a1)
    unpack(0, a0)

    def two_chunks(half, _):
        for h in range(2):
            s = half * 2 + h
            unpack(jnp.minimum(s + 1, 15), bufs[1 - h])
            prod = jnp.dot(g[...], bufs[h][...], preferred_element_type=F32).astype(BF16)
            part[s, 0] = prod[0:128]
            part[s, 1] = prod[128:256]
            to_sibling(s).start()

            @pl.when(jnp.logical_and(s >= 1, s <= 12))
            def _():
                pass_on(s - 1)

            @pl.when(s >= 13)
            def _():
                finish_sum(s - 13)

        return 0

    lax.fori_loop(0, 8, two_chunks, 0)
    finish_sum(3)

    def relay(buf, base, m):
        rep_copy(buf, base, m, 1).wait_recv()
        rep_copy(buf, base, m, 2).start()

    def settled(buf, base, m):
        rep_copy(buf, base, m, 0).wait_recv()
        rep_copy(buf, base, m, 2).wait_recv()

    def rows_forward(m):
        rows = rows_of(m)
        hidden = jnp.dot(agg[0, rows, :], wc[0], preferred_element_type=F32)
        for q in range(1, 4):
            hidden = hidden + jnp.dot(agg[q, rows, :], wc[q], preferred_element_type=F32)
        hidden = hidden + bias[me.rep, 0:1, :]
        logistic = jax.nn.sigmoid(hidden)
        act[rows, :] = hidden * logistic
        value = cot[rows, :].astype(F32) * logistic * (1.0 + hidden * (1.0 - logistic))
        slope[me.rep, rows, :] = value.astype(BF16)

    mine = pl.ds(pl.multiple_of(own * 128, 128), 128)

    def block(n, m):
        start = me.dy(n) * 1024 + m * 256
        return ball.at[pl.ds(pl.multiple_of(start, 256), 256), mine]

    def y_copy(n, m):
        k = 24 + (n - 1) * 4 + m
        return pltpu.make_async_remote_copy(
            src_ref=block(0, m), dst_ref=block(0, m), send_sem=send.at[k], recv_sem=recv.at[k],
            device_id=y_peers[n - 1], device_id_type=MESH,
        )

    def core_copy(n, m):
        k = 36 + n * 4 + m
        return pltpu.make_async_remote_copy(
            src_ref=block(n, m), dst_ref=block(n, m), send_sem=send.at[k], recv_sem=recv.at[k],
            device_id=sibling, device_id_type=MESH,
        )

    def rows_backward(m):
        rows = rows_of(m)
        total = jnp.zeros((256, 128), F32)
        for q in range(4):
            total = total + lax.dot_general(
                slope[q, rows, :], w[q], (((1,), (1,)), ((), ())), preferred_element_type=F32
            )
        here = pl.ds(pl.multiple_of(me.y * 1024 + m * 256, 256), 256)
        ball[here, mine] = (total * col[rows, :]).astype(BF16)
        for n in (2, 1, 3):
            y_copy(n, m).start()
        core_copy(0, m).start()

    def layer_step(m, _):
        @pl.when(m < 4)
        def _():
            relay(agg, 0, m)

        @pl.when(jnp.logical_and(m >= 1, m < 5))
        def _():
            settled(agg, 0, m - 1)
            rows_forward(m - 1)
            share(slope, 12, m - 1)

        @pl.when(jnp.logical_and(m >= 2, m < 6))
        def _():
            relay(slope, 12, m - 2)

        @pl.when(m >= 3)
        def _():
            settled(slope, 12, m - 3)
            rows_backward(m - 3)

        return 0

    lax.fori_loop(0, 7, layer_step, 0)

    ones = jnp.ones((8, 1024), BF16)
    for q in range(4):
        lanes = slice(q * 128, (q + 1) * 128)
        grad = jnp.dot(agg_t[...], slope[q], preferred_element_type=F32)
        gb = jnp.dot(ones, slope[q], preferred_element_type=F32)
        for n in range(4):
            gwx[n, 0:32, lanes] = grad[n * 32:(n + 1) * 32]
            gwx[n, 32:40, lanes] = gb

    def pass_blocks(m, _):
        for n in (1, 3, 2):
            y_copy(n, m).wait_recv()
            core_copy(4 - n, m).start()
        return 0

    lax.fori_loop(0, 4, pass_blocks, 0)

    def finish(m, _):
        for n in range(4):
            core_copy(n, m).wait()
        for n in (1, 2, 3):
            y_copy(n, m).wait_send()
            to_owner((n - 1) * 4 + m).wait_send()
        for kind in range(3):
            rep_copy(agg, 0, m, kind).wait_send()
            rep_copy(slope, 12, m, kind).wait_send()
        for n in range(4):
            to_sibling(n * 4 + m).wait_send()
        return 0

    lax.fori_loop(0, 4, finish, 0)


def layer(dense, g, row, col, wc, w, bias, cot):
    return pl.pallas_call(
        layer_kernel,
        out_shape=(
            jax.ShapeDtypeStruct((1024, 128), F32),
            jax.ShapeDtypeStruct((4096, 256), BF16),
            jax.ShapeDtypeStruct((4, 40, 512), F32),
        ),
        in_specs=[VMEM] * 8,
        out_specs=(VMEM, VMEM, VMEM),
        scratch_shapes=[
            pltpu.VMEM((4096, 256), BF16),
            pltpu.VMEM((4096, 256), BF16),
            pltpu.VMEM((16, 2, 128, 256), BF16),
            pltpu.VMEM((16, 128, 256), BF16),
            pltpu.VMEM((12, 128, 256), BF16),
            pltpu.VMEM((12, 128, 256), BF16),
            pltpu.VMEM((4, 1024, 128), BF16),
            pltpu.VMEM((128, 1024), BF16),
            pltpu.VMEM((4, 1024, 128), BF16),
            DMA((16,)),
            DMA((16,)),
            DMA((12,)),
            DMA((12,)),
            DMA((52,)),
            DMA((52,)),
        ],
        compiler_params=pltpu.CompilerParams(
            collective_id=1, has_side_effects=True, vmem_limit_bytes=36 * MIB
        ),
        name="layer",
    )(dense, g, row, col, wc, w, bias, cot)


STEPS = (
    (1, 1, 2), (0, 1, 2), (1, 1, 1), (0, 1, 1), (1, 1, 3), (0, 1, 3), (1, 1, 0), (0, 1, 0),
    (1, 0, 2), (1, 0, 1), (1, 0, 3), (0, 0, 2), (0, 0, 1), (0, 0, 3), (1, 0, 0), (0, 0, 0),
)
ORDER = {key: n for n, key in enumerate(STEPS)}


def settle_kernel(dense, ball, gwx, out, gw, a0, a1, part, az, a_sum, ax, bx, b_sum, bz, final,
                  wy, wz, wx_send, wx, send, recv, local):
    me = Place()
    sibling = me.at(c=1 - me.c)
    x_peer = me.at(x=1 - me.x)
    z_peers = [me.at(z=me.dz(n)) for n in (1, 2, 3)]
    y_peers = [me.at(y=me.dy(n)) for n in (1, 2, 3)]
    greet(z_peers + y_peers + [x_peer, sibling])

    def remote(n, src, dst, peer):
        return pltpu.make_async_remote_copy(
            src_ref=src, dst_ref=dst, send_sem=send.at[n], recv_sem=recv.at[n],
            device_id=peer, device_id_type=MESH,
        )

    x_first = {n: remote(n, part.at[ORDER[1, 1, n]], bx.at[n], x_peer) for n in range(4)}
    z_first = {
        (side, n): remote(4 + side * 3 + n - 1, part.at[ORDER[0, side, n]], az.at[side, n - 1], z_peers[n - 1])
        for side in range(2) for n in (1, 2, 3)
    }
    z_second = {n: remote(9 + n, b_sum.at[n - 1], bz.at[n - 1], z_peers[n - 1]) for n in (1, 2, 3)}
    x_second = remote(13, a_sum, ax, x_peer)
    w_y = [remote(13 + n, gwx.at[me.dy(n)], wy.at[me.y], y_peers[n - 1]) for n in (1, 2, 3)]
    w_z = [remote(16 + n, wz.at[me.z], wz.at[me.z], z_peers[n - 1]) for n in (1, 2, 3)]
    w_x = remote(20, wx_send, wx, x_peer)
    w_back = [remote(20 + n, gw.at[me.y], gw.at[me.y], y_peers[n - 1]) for n in (1, 2, 3)]

    def unpack(s, out_ref):
        half = table([step[0] for step in STEPS], s)
        side = table([step[1] for step in STEPS], s)
        dist = table([step[2] for step in STEPS], s)
        x = lax.rem(me.x + side, 2)
        j = x * 4 + lax.rem(me.z + dist, 4)
        for i in range(4):
            for tc in range(2):
                for t in range(8):
                    put_bits(dense[i * 8 + j, half * 2 + tc, t], out_ref, tc * 128, i * 1024 + t * 128)

    def pass_b(n):
        x_first[n].wait_recv()
        b_sum[n - 1] = (part[ORDER[1, 0, n]].astype(F32) + bx[n].astype(F32)).astype(BF16)
        z_second[n].start()

    def pass_a():
        total = part[ORDER[0, 1, 0]].astype(F32)
        for n in (1, 2, 3):
            z_first[1, n].wait_recv()
            total = total + az[1, n - 1].astype(F32)
        a_sum[...] = total.astype(BF16)
        x_second.start()

    def weights_z():
        for copy in w_y:
            copy.wait_recv()
        wz[me.z] = (wy[0] + wy[1]) + (wy[2] + wy[3])
        for copy in w_z:
            copy.start()

    def weights_x():
        for copy in w_z:
            copy.wait_recv()
        wx_send[...] = (wz[0] + wz[1]) + (wz[2] + wz[3])
        w_x.start()

    def weights_back():
        w_x.wait_recv()
        gw[me.y] = wx_send[...] + wx[...]
        for copy in w_back:
            copy.start()

    actions = {}
    for n in range(4):
        actions.setdefault(ORDER[1, 1, n], []).append(x_first[n].start)
    for key, copy in z_first.items():
        actions.setdefault(ORDER[(0,) + key], []).append(copy.start)
    actions.setdefault(6, []).append(weights_z)
    for n in (2, 1, 3):
        actions.setdefault(ORDER[1, 0, n] + 1, []).append(functools.partial(pass_b, n))
    actions.setdefault(11, []).append(pass_a)
    actions.setdefault(12, []).append(weights_x)
    actions.setdefault(14, []).append(weights_back)

    for copy in w_y:
        copy.start()
    wy[me.y] = gwx[me.y]
    bufs = (a0, a1)
    unpack(0, a0)

    def two_chunks(pair, _):
        for h in range(2):
            s = pair * 2 + h
            unpack(jnp.minimum(s + 1, 15), bufs[1 - h])
            part[s] = jnp.dot(bufs[h][...], ball[...], preferred_element_type=F32).astype(BF16)
            for at in sorted(actions):
                if at % 2 == h:
                    @pl.when(s == at)
                    def _():
                        for action in actions[at]:
                            action()
        return 0

    lax.fori_loop(0, 8, two_chunks, 0)

    total = part[ORDER[1, 0, 0]].astype(F32)
    x_first[0].wait_recv()
    total = total + bx[0].astype(F32)
    for n in (1, 2, 3):
        z_second[n].wait_recv()
        total = total + bz[n - 1].astype(F32)
    final[0, 256:512, :] = total[:, 0:128]
    final[1, 256:512, :] = total[:, 128:256]
    total = part[ORDER[0, 0, 0]].astype(F32)
    for n in (1, 2, 3):
        z_first[0, n].wait_recv()
        total = total + az[0, n - 1].astype(F32)
    x_second.wait_recv()
    total = total + ax[...].astype(F32)
    final[0, 0:256, :] = total[:, 0:128]
    final[1, 0:256, :] = total[:, 128:256]
    swap = remote(24, final.at[1 - me.c], out.at[me.c], sibling)
    swap.start()
    keep = pltpu.make_async_copy(final.at[me.c], out.at[me.c], local)
    keep.start()
    for copy in w_back:
        copy.wait_recv()
    swap.wait_recv()
    keep.wait()
    for copy in list(x_first.values()) + list(z_first.values()) + list(z_second.values()):
        copy.wait_send()
    for copy in [x_second, w_x, swap] + w_y + w_z + w_back:
        copy.wait_send()


def settle(dense, ball, gwx):
    half = (256, 256)
    return pl.pallas_call(
        settle_kernel,
        out_shape=(
            jax.ShapeDtypeStruct((2, 512, 128), F32),
            jax.ShapeDtypeStruct((4, 40, 512), F32),
        ),
        in_specs=[VMEM] * 3,
        out_specs=(VMEM, VMEM),
        scratch_shapes=[
            pltpu.VMEM((256, 4096), BF16),
            pltpu.VMEM((256, 4096), BF16),
            pltpu.VMEM((16,) + half, BF16),
            pltpu.VMEM((2, 3) + half, BF16),
            pltpu.VMEM(half, BF16),
            pltpu.VMEM(half, BF16),
            pltpu.VMEM((4,) + half, BF16),
            pltpu.VMEM((3,) + half, BF16),
            pltpu.VMEM((3,) + half, BF16),
            pltpu.VMEM((2, 512, 128), F32),
            pltpu.VMEM((4, 40, 512), F32),
            pltpu.VMEM((4, 40, 512), F32),
            pltpu.VMEM((40, 512), F32),
            pltpu.VMEM((40, 512), F32),
            DMA((25,)),
            DMA((25,)),
            DMA,
        ],
        compiler_params=pltpu.CompilerParams(
            collective_id=2, has_side_effects=True, vmem_limit_bytes=36 * MIB
        ),
        name="settle",
    )(dense, ball, gwx)


def body(features, weight, bias_vector, cotangent, tile_masks, tile_rows, tile_counts):
    perm = np.zeros((128, 128), np.float32)
    for w in range(16):
        for k in range(8):
            perm[8 * w + k, 16 * k + w] = 1.0
    live = jnp.arange(4, dtype=jnp.int32) < tile_counts[0][:, None]
    place = jnp.where(live, tile_rows[0], 8).astype(jnp.int32)
    meta = place.reshape(8, 4, 2, 16).transpose(1, 2, 0, 3).reshape(4, 2, 1, 128)
    meta = jnp.broadcast_to(meta, (4, 2, 8, 128))
    weight_q = weight.reshape(128, 4, 128).transpose(1, 0, 2)

    m16, xt, row, col = prepare(place.reshape(1024), tile_masks[0], features, jnp.asarray(perm, BF16))
    rm, rmeta, g, wc = spread(m16.reshape(8, 4, 2, 4, 64, 128), meta, xt, weight_q)
    dense = place_tiles(rmeta, rm)
    bias = jnp.broadcast_to(bias_vector.reshape(4, 1, 128), (4, 8, 128))
    act, ball, gwx = layer(dense, g.reshape(256, 4096), row, col, wc, weight_q, bias, cotangent)
    out, gw = settle(dense, ball, gwx)
    out = out.reshape(8, 8, 16, 128).transpose(0, 2, 1, 3).reshape(1024, 128) * col
    return act, out, gw[:, :32].reshape(128, 512), gw[0, 32]


def solution(mesh):
    return jax.shard_map(
        body,
        mesh=mesh,
        in_specs=(
            P("blk", "rep"),
            P("rep", None),
            P(),
            P("blk", "rep"),
            P("blk", None, None, None, None),
            P("blk", None, None),
            P("blk", None),
        ),
        out_specs=(P("blk", "rep"), P("blk", "rep"), P("rep", None), P()),
        check_vma=False,
    )
```

```python
import functools

import jax
import jax.numpy as jnp
from jax import lax
from jax.experimental import pallas as pl
from jax.experimental.pallas import tpu as pltpu
from jax.sharding import PartitionSpec as P

MESH = pl.DeviceIdType.MESH
BF16 = jnp.bfloat16
F32 = jnp.float32
VMEM = pl.BlockSpec(memory_space=pltpu.VMEM)
SMEM = pl.BlockSpec(memory_space=pltpu.SMEM)
DMA = pltpu.SemaphoreType.DMA
MIB = 2**20


class Place:
    def __init__(self):
        blk = lax.axis_index("blk")
        rep = lax.axis_index("rep")
        self.x, self.z, self.y = blk // 16, lax.rem(blk // 4, 4), lax.rem(blk, 4)
        self.xl, self.c = rep // 2, lax.rem(rep, 2)
        self.rep = rep
        self.xz = self.x * 4 + self.z

    def at(self, x=None, z=None, y=None, xl=None, c=None):
        x = self.x if x is None else x
        z = self.z if z is None else z
        y = self.y if y is None else y
        xl = self.xl if xl is None else xl
        c = self.c if c is None else c
        return (x * 16 + z * 4 + y, xl * 2 + c)

    def dy(self, n):
        return lax.rem(self.y + n, 4)

    def dz(self, n):
        return lax.rem(self.z + n, 4)


def greet(peers):
    barrier = pltpu.get_barrier_semaphore()
    for peer in peers:
        pl.semaphore_signal(barrier, inc=1, device_id=peer, device_id_type=MESH)
    pl.semaphore_wait(barrier, len(peers))


class Copies:
    def __init__(self, send, recv):
        self.send, self.recv, self.used = send, recv, []

    def start(self, src, dst, peer):
        n = len(self.used)
        copy = pltpu.make_async_remote_copy(
            src_ref=src, dst_ref=dst, send_sem=self.send.at[n], recv_sem=self.recv.at[n],
            device_id=peer, device_id_type=MESH,
        )
        copy.start()
        self.used.append(copy)
        return copy

    def wait_sends(self):
        for copy in self.used:
            copy.wait_send()


Y_ORDER = (2, 1, 3, 0)


def spread_kernel(rows_ref, counts_ref, masks, feat, w, dense, row, col, g, wc,
                  words, m16, rm, slots_s, slots_v, landed_v, landed_s, xt, send, recv, load, local):
    me = Place()
    own, other = me.c, 1 - me.c
    loads = []
    for q in range(8):
        half = own if q < 4 else other
        loads.append(pltpu.make_async_copy(masks.at[:, me.dy(Y_ORDER[q % 4]), half], words.at[q], load.at[q]))
        loads[q].start()

    sibling = me.at(c=1 - me.c)
    x_peer = me.at(x=1 - me.x)
    z_peers = [me.at(z=me.dz(n)) for n in (1, 2, 3)]
    y_peers = [me.at(y=me.dy(n)) for n in (1, 2, 3)]
    rep_peers = [sibling, me.at(xl=1 - me.xl), me.at(xl=1 - me.xl, c=1 - me.c)]
    greet(z_peers + y_peers + rep_peers + [x_peer])
    copies = Copies(send, recv)

    tile_row = lax.broadcasted_iota(jnp.int32, (8, 128), 0)

    def scan(q, degrees):
        n = Y_ORDER[q % 4]
        half = own if q < 4 else other
        loads[q].wait()

        def tiles(xz, degrees):
            first = ((xz * 4 + me.dy(n)) * 2 + half) * 4
            for tc in range(4):
                count = counts_ref[first + tc]
                for s in range(4):
                    slot = tc * 4 + s
                    t = jnp.where(s < count, rows_ref[s, first + tc], 8)
                    tile = words[q, xz, slot]
                    if q < 3:
                        m16[q, xz, slot] = tile.astype(jnp.int16)
                    elif q == 3:
                        rm[me.y, xz, slot] = tile.astype(jnp.int16)
                    if q < 4:
                        slots_s[q, 0, xz * 16 + slot] = t
                    joined = jnp.bitwise_or(tile[:8], jnp.left_shift(tile[8:], 8))
                    counted = jnp.sum(lax.population_count(joined), axis=0, keepdims=True)
                    degrees = degrees + jnp.where(tile_row == t, counted, 0)
            return degrees

        return lax.fori_loop(0, 8, tiles, degrees)

    degrees = jnp.zeros((8, 128), jnp.int32)
    mask_copies = []
    for q in range(3):
        degrees = scan(q, degrees)
        mask_copies.append(copies.start(m16.at[q], rm.at[me.y], y_peers[Y_ORDER[q] - 1]))
    for q in range(3, 8):
        degrees = scan(q, degrees)

    inv = lax.rsqrt(1.0 + degrees.astype(F32))
    place = lax.broadcasted_iota(jnp.int32, (128, 128), 1)
    source = 8 * jnp.bitwise_and(place, 15) + jnp.right_shift(place, 4)
    perm = jnp.where(lax.broadcasted_iota(jnp.int32, (128, 128), 0) == source, 1.0, 0.0).astype(BF16)
    for t in range(8):
        lanes = inv[t:t + 1, :]
        row[:, t * 128:(t + 1) * 128] = jnp.broadcast_to(lanes, (8, 128))
        spread = jnp.broadcast_to(lanes, (128, 128))
        col[t * 128:(t + 1) * 128, :] = spread.T
        scaled = (feat[t * 128:(t + 1) * 128, :].astype(F32).T * spread).astype(BF16)
        moved = jnp.dot(scaled, perm, preferred_element_type=F32).astype(BF16)
        xt[t // 4, :, (t % 4) * 128:(t % 4 + 1) * 128] = moved

    def at(core, xz):
        return g.at[xz, core]

    def weight_to(rep):
        return w.at[:, pl.ds(pl.multiple_of(rep * 128, 128), 128)]

    to_sibling = copies.start(xt.at[other], at(own, me.xz), sibling)
    first = [copies.start(xt.at[own], at(own, me.xz), p) for p in z_peers]
    across = copies.start(xt.at[own], at(own, me.xz), x_peer)
    stays = [
        pltpu.make_async_copy(xt.at[own], at(own, me.xz), local.at[0]),
        pltpu.make_async_copy(weight_to(me.rep), wc.at[me.rep], local.at[1]),
    ]
    for copy in stays:
        copy.start()
    to_vmem = pltpu.make_async_copy(slots_s, slots_v, local.at[2])
    to_vmem.start()
    to_vmem.wait()
    slot_copies = [copies.start(slots_v.at[q], landed_v.at[me.y], y_peers[Y_ORDER[q] - 1]) for q in range(3)]
    kept = pltpu.make_async_copy(slots_v.at[3], landed_v.at[me.y], local.at[3])
    kept.start()

    to_sibling.wait_recv()
    other_x = copies.start(at(other, me.xz), at(other, me.xz), x_peer)
    second = [copies.start(at(other, me.xz), at(other, me.xz), p) for p in z_peers]
    weights = [copies.start(weight_to(peer[1]), wc.at[me.rep], peer) for peer in rep_peers]

    kept.wait()
    for copy in slot_copies:
        copy.wait_recv()
    to_smem = pltpu.make_async_copy(landed_v, landed_s, local.at[4])
    to_smem.start()
    to_smem.wait()

    def put_tiles(n):
        i = me.dy(n)

        def column(j, _):
            for tc in range(4):
                rows = [landed_s[i, 0, j * 16 + tc * 4 + s] for s in range(4)]
                tiles = [rm[i, j, tc * 4 + s] for s in range(4)]
                for t in range(8):
                    found = jnp.zeros((16, 128), jnp.int16)
                    for s in range(4):
                        found = jnp.where(rows[s] == t, tiles[s], found)
                    dense[i * 8 + j, tc, t] = found
            return 0

        lax.fori_loop(0, 8, column, 0)

    put_tiles(0)
    last = []
    for n in (1, 2, 3):
        first[n - 1].wait_recv()
        source = me.x * 4 + me.dz(4 - n)
        last.append(copies.start(at(own, source), at(own, source), x_peer))
    other_x.wait_recv()
    far = (1 - me.x) * 4 + me.z
    last += [copies.start(at(other, far), at(other, far), p) for p in z_peers]
    for q in range(3):
        mask_copies[q].wait_recv()
        put_tiles(4 - Y_ORDER[q])
    for copy in [across] + weights + second + last:
        copy.wait_recv()
    copies.wait_sends()
    for copy in stays:
        copy.wait()


def spread(rows, counts, masks, features, w):
    return pl.pallas_call(
        spread_kernel,
        out_shape=(
            jax.ShapeDtypeStruct((32, 4, 8, 16, 128), jnp.int16),
            jax.ShapeDtypeStruct((8, 1024), F32),
            jax.ShapeDtypeStruct((1024, 128), F32),
            jax.ShapeDtypeStruct((8, 2, 128, 512), BF16),
            jax.ShapeDtypeStruct((4, 128, 128), BF16),
        ),
        in_specs=[SMEM, SMEM, pl.BlockSpec(memory_space=pltpu.HBM), VMEM, VMEM],
        out_specs=(VMEM,) * 5,
        scratch_shapes=[
            pltpu.VMEM((8, 8, 16, 16, 128), jnp.int32),
            pltpu.VMEM((3, 8, 16, 16, 128), jnp.int16),
            pltpu.VMEM((4, 8, 16, 16, 128), jnp.int16),
            pltpu.SMEM((4, 1, 128), jnp.int32),
            pltpu.VMEM((4, 1, 128), jnp.int32),
            pltpu.VMEM((4, 1, 128), jnp.int32),
            pltpu.SMEM((4, 1, 128), jnp.int32),
            pltpu.VMEM((2, 128, 512), BF16),
            DMA((24,)),
            DMA((24,)),
            DMA((8,)),
            DMA((5,)),
        ],
        compiler_params=pltpu.CompilerParams(
            collective_id=0, has_side_effects=True, vmem_limit_bytes=32 * MIB
        ),
        name="spread",
    )(rows, counts, masks, features, w)


def table(values, step):
    found = values[-1]
    for n in range(len(values) - 1):
        found = jnp.where(step == n, values[n], found)
    return found


def unpack(dense, i, j, out_ref):
    one, zero = jnp.asarray(1, BF16), jnp.asarray(0, BF16)
    for tc in range(4):
        for t in range(8):
            words = dense[i * 8 + j, tc, t]
            for k in range(8):
                bits = jnp.where(jnp.bitwise_and(words, jnp.int16(1 << k)) != 0, one, zero)
                first = tc * 128 + k * 16
                out_ref[first:first + 16, t * 128:(t + 1) * 128] = bits


def layer_kernel(dense, g, row, col, wc, w, bias, cot, act, ball, gwx,
                 a0, a1, acc, part, rc, snd, ry, agg, agg_t, slope,
                 core_s, core_r, sum_s, sum_r, send, recv):
    me = Place()
    sibling = me.at(c=1 - me.c)
    xl_peer = me.at(xl=1 - me.xl)
    y_peers = [me.at(y=me.dy(n)) for n in (1, 2, 3)]
    greet([sibling, xl_peer] + y_peers)
    copies = Copies(send, recv)
    own, other = me.c, 1 - me.c

    def to_sibling(s):
        return pltpu.make_async_remote_copy(
            src_ref=part.at[s, other], dst_ref=rc.at[s], send_sem=core_s.at[s], recv_sem=core_r.at[s],
            device_id=sibling, device_id_type=MESH,
        )

    def to_owner(s):
        return pltpu.make_async_remote_copy(
            src_ref=snd.at[s], dst_ref=ry.at[s], send_sem=sum_s.at[s], recv_sem=sum_r.at[s],
            device_id=me.at(y=me.dy(table((2, 1, 3), s))), device_id_type=MESH,
        )

    def pass_on(s):
        to_sibling(s).wait_recv()
        snd[s] = (part[s, own].astype(F32) + rc[s].astype(F32)).astype(BF16)
        to_owner(s).start()

    def rows_of(m):
        return pl.ds(pl.multiple_of(m * 256, 256), 256)

    def rep_copy(buf, base, m, kind):
        theirs = (1 - me.xl) * 2 + me.c
        src = buf.at[theirs if kind == 2 else me.rep, rows_of(m), :]
        n = base + kind * 4 + m
        return pltpu.make_async_remote_copy(
            src_ref=src, dst_ref=src, send_sem=send.at[n], recv_sem=recv.at[n],
            device_id=xl_peer if kind == 1 else sibling, device_id_type=MESH,
        )

    def share(buf, base, m):
        rep_copy(buf, base, m, 1).start()
        rep_copy(buf, base, m, 0).start()

    def finish_sum(m):
        rows = rows_of(m)
        total = part[3, own, :, rows].astype(F32) + rc[3, :, rows].astype(F32)
        for k in range(3):
            total = total + ry[k, :, rows].astype(F32)
        total = total * row[0:1, rows]
        agg_t[:, rows] = total.astype(BF16)
        agg[me.rep, rows, :] = total.T.astype(BF16)
        share(agg, 0, m)

    def chunk(c):
        return me.dy(table((2, 1, 3, 0), c // 8)), lax.rem(c, 8)

    bufs = (a0, a1)
    unpack(dense, *chunk(0), a0)

    def two_chunks(n, _):
        k, pair = n // 4, lax.rem(n, 4)
        for h in range(2):
            unpack(dense, *chunk(jnp.minimum(n * 2 + h + 1, 31)), bufs[1 - h])
            prod = jnp.dot(g[pair * 2 + h], bufs[h][...], preferred_element_type=F32)
            if h == 0:
                acc[...] = jnp.where(pair == 0, 0.0, acc[...]) + prod
            else:
                acc[...] += prod

        @pl.when(pair == 3)
        def _():
            part[k, 0] = acc[0:128].astype(BF16)
            part[k, 1] = acc[128:256].astype(BF16)
            to_sibling(k).start()

        @pl.when(jnp.logical_and(pair == 0, k >= 1))
        def _():
            pass_on(k - 1)

        return 0

    lax.fori_loop(0, 16, two_chunks, 0)
    to_sibling(3).wait_recv()
    for k in range(3):
        to_owner(k).wait_recv()
    for m in range(4):
        finish_sum(m)

    def relay(buf, base, m):
        rep_copy(buf, base, m, 1).wait_recv()
        rep_copy(buf, base, m, 2).start()

    def settled(buf, base, m):
        rep_copy(buf, base, m, 0).wait_recv()
        rep_copy(buf, base, m, 2).wait_recv()

    def rows_forward(m):
        rows = rows_of(m)
        hidden = jnp.dot(agg[0, rows, :], wc[0], preferred_element_type=F32)
        for q in range(1, 4):
            hidden = hidden + jnp.dot(agg[q, rows, :], wc[q], preferred_element_type=F32)
        hidden = hidden + bias[pl.ds(me.rep, 1), :]
        logistic = jax.nn.sigmoid(hidden)
        act[rows, :] = hidden * logistic
        value = cot[rows, :].astype(F32) * logistic * (1.0 + hidden * (1.0 - logistic))
        slope[me.rep, rows, :] = value.astype(BF16)

    mine = pl.ds(pl.multiple_of(own * 128, 128), 128)

    def block(n, m):
        start = me.dy(n) * 1024 + m * 256
        return ball.at[pl.ds(pl.multiple_of(start, 256), 256), mine]

    def y_copy(n, m):
        k = 24 + (n - 1) * 4 + m
        return pltpu.make_async_remote_copy(
            src_ref=block(0, m), dst_ref=block(0, m), send_sem=send.at[k], recv_sem=recv.at[k],
            device_id=y_peers[n - 1], device_id_type=MESH,
        )

    def core_copy(n, m):
        k = 36 + n * 4 + m
        return pltpu.make_async_remote_copy(
            src_ref=block(n, m), dst_ref=block(n, m), send_sem=send.at[k], recv_sem=recv.at[k],
            device_id=sibling, device_id_type=MESH,
        )

    def rows_backward(m):
        rows = rows_of(m)
        total = jnp.zeros((256, 128), F32)
        for q in range(4):
            total = total + lax.dot_general(
                slope[q, rows, :], w[:, q * 128:(q + 1) * 128], (((1,), (1,)), ((), ())), preferred_element_type=F32
            )
        here = pl.ds(pl.multiple_of(me.y * 1024 + m * 256, 256), 256)
        ball[here, mine] = (total * col[rows, :]).astype(BF16)
        for n in (2, 1, 3):
            y_copy(n, m).start()
        core_copy(0, m).start()

    def layer_step(m, _):
        @pl.when(m < 4)
        def _():
            relay(agg, 0, m)

        @pl.when(jnp.logical_and(m >= 1, m < 5))
        def _():
            settled(agg, 0, m - 1)
            rows_forward(m - 1)
            share(slope, 12, m - 1)

        @pl.when(jnp.logical_and(m >= 2, m < 6))
        def _():
            relay(slope, 12, m - 2)

        @pl.when(m >= 3)
        def _():
            settled(slope, 12, m - 3)
            rows_backward(m - 3)

        return 0

    lax.fori_loop(0, 7, layer_step, 0)

    ones = jnp.ones((8, 1024), BF16)
    for q in range(4):
        lanes = slice(q * 128, (q + 1) * 128)
        grad = jnp.dot(agg_t[...], slope[q], preferred_element_type=F32)
        gb = jnp.dot(ones, slope[q], preferred_element_type=F32)
        for n in range(4):
            gwx[n, 0:32, lanes] = grad[n * 32:(n + 1) * 32]
            gwx[n, 32:40, lanes] = gb

    def pass_blocks(m, _):
        for n in (1, 3, 2):
            y_copy(n, m).wait_recv()
            core_copy(4 - n, m).start()
        return 0

    lax.fori_loop(0, 4, pass_blocks, 0)

    def finish(m, _):
        for n in range(4):
            core_copy(n, m).wait()
        for n in (1, 2, 3):
            y_copy(n, m).wait_send()
        for kind in range(3):
            rep_copy(agg, 0, m, kind).wait_send()
            rep_copy(slope, 12, m, kind).wait_send()
        to_sibling(m).wait_send()
        return 0

    lax.fori_loop(0, 4, finish, 0)
    for k in range(3):
        to_owner(k).wait_send()


def layer(dense, g, row, col, wc, w, bias, cot):
    return pl.pallas_call(
        layer_kernel,
        out_shape=(
            jax.ShapeDtypeStruct((1024, 128), F32),
            jax.ShapeDtypeStruct((4096, 256), BF16),
            jax.ShapeDtypeStruct((4, 40, 512), F32),
        ),
        in_specs=[VMEM] * 8,
        out_specs=(VMEM, VMEM, VMEM),
        scratch_shapes=[
            pltpu.VMEM((512, 1024), BF16),
            pltpu.VMEM((512, 1024), BF16),
            pltpu.VMEM((256, 1024), F32),
            pltpu.VMEM((4, 2, 128, 1024), BF16),
            pltpu.VMEM((4, 128, 1024), BF16),
            pltpu.VMEM((3, 128, 1024), BF16),
            pltpu.VMEM((3, 128, 1024), BF16),
            pltpu.VMEM((4, 1024, 128), BF16),
            pltpu.VMEM((128, 1024), BF16),
            pltpu.VMEM((4, 1024, 128), BF16),
            DMA((4,)),
            DMA((4,)),
            DMA((3,)),
            DMA((3,)),
            DMA((52,)),
            DMA((52,)),
        ],
        compiler_params=pltpu.CompilerParams(
            collective_id=1, has_side_effects=True, vmem_limit_bytes=36 * MIB
        ),
        name="layer",
    )(dense, g, row, col, wc, w, bias, cot)


BLOCKS = ((1, 2), (1, 1), (1, 3), (1, 0), (0, 2), (0, 1), (0, 3), (0, 0))
ORDER = {key: n for n, key in enumerate(BLOCKS)}


def settle_kernel(dense, ball, gwx, out, gw, a0, a1, acc, part, az, a_sum, ax, bx, b_sum, bz, final,
                  wy, wz, wx_send, wx, send, recv, local):
    me = Place()
    sibling = me.at(c=1 - me.c)
    x_peer = me.at(x=1 - me.x)
    z_peers = [me.at(z=me.dz(n)) for n in (1, 2, 3)]
    y_peers = [me.at(y=me.dy(n)) for n in (1, 2, 3)]
    greet(z_peers + y_peers + [x_peer, sibling])

    def remote(n, src, dst, peer):
        return pltpu.make_async_remote_copy(
            src_ref=src, dst_ref=dst, send_sem=send.at[n], recv_sem=recv.at[n],
            device_id=peer, device_id_type=MESH,
        )

    x_first = {n: remote(n, part.at[ORDER[1, n], 1], bx.at[n], x_peer) for n in range(4)}
    z_first = {
        (side, n): remote(4 + side * 3 + n - 1, part.at[ORDER[side, n], 0], az.at[side, n - 1], z_peers[n - 1])
        for side in range(2) for n in (1, 2, 3)
    }
    z_second = {n: remote(9 + n, b_sum.at[n - 1], bz.at[n - 1], z_peers[n - 1]) for n in (1, 2, 3)}
    x_second = remote(13, a_sum, ax, x_peer)
    w_y = [remote(13 + n, gwx.at[me.dy(n)], wy.at[me.y], y_peers[n - 1]) for n in (1, 2, 3)]
    w_z = [remote(16 + n, wz.at[me.z], wz.at[me.z], z_peers[n - 1]) for n in (1, 2, 3)]
    w_x = remote(20, wx_send, wx, x_peer)
    w_back = [remote(20 + n, gw.at[me.y], gw.at[me.y], y_peers[n - 1]) for n in (1, 2, 3)]

    def pass_b(n):
        x_first[n].wait_recv()
        b_sum[n - 1] = (part[ORDER[0, n], 1].astype(F32) + bx[n].astype(F32)).astype(BF16)
        z_second[n].start()

    def pass_a():
        total = part[ORDER[1, 0], 0].astype(F32)
        for n in (1, 2, 3):
            z_first[1, n].wait_recv()
            total = total + az[1, n - 1].astype(F32)
        a_sum[...] = total.astype(BF16)
        x_second.start()

    def weights_z():
        for copy in w_y:
            copy.wait_recv()
        wz[me.z] = (wy[0] + wy[1]) + (wy[2] + wy[3])
        for copy in w_z:
            copy.start()

    def weights_x():
        for copy in w_z:
            copy.wait_recv()
        wx_send[...] = (wz[0] + wz[1]) + (wz[2] + wz[3])
        w_x.start()

    def weights_back():
        w_x.wait_recv()
        gw[me.y] = wx_send[...] + wx[...]
        for copy in w_back:
            copy.start()

    actions = {n: [] for n in range(8)}
    for n in range(4):
        actions[ORDER[1, n]].append(x_first[n].start)
    for n in (2, 1, 3):
        actions[ORDER[0, n]].append(functools.partial(pass_b, n))
    for key, copy in z_first.items():
        actions[ORDER[key]].append(copy.start)
    actions[3].append(weights_z)
    actions[4].append(pass_a)
    actions[5].append(weights_x)
    actions[6].append(weights_back)

    for copy in w_y:
        copy.start()
    wy[me.y] = gwx[me.y]

    def chunk(c):
        at = c // 4
        x = lax.rem(me.x + table([block[0] for block in BLOCKS], at), 2)
        z = lax.rem(me.z + table([block[1] for block in BLOCKS], at), 4)
        return lax.rem(c, 4), x * 4 + z

    bufs = (a0, a1)
    unpack(dense, *chunk(0), a0)

    def two_chunks(step, _):
        block, pair = step // 2, lax.rem(step, 2)
        for h in range(2):
            unpack(dense, *chunk(jnp.minimum(step * 2 + h + 1, 31)), bufs[1 - h])
            prod = jnp.dot(bufs[h][...], ball[pair * 2 + h], preferred_element_type=F32)
            if h == 0:
                acc[...] = jnp.where(pair == 0, 0.0, acc[...]) + prod
            else:
                acc[...] += prod

        @pl.when(pair == 1)
        def _():
            part[block, 0] = acc[0:256].astype(BF16)
            part[block, 1] = acc[256:512].astype(BF16)

        for at, calls in actions.items():
            if calls:
                @pl.when(step == at * 2 + 1)
                def _():
                    for call in calls:
                        call()

        return 0

    lax.fori_loop(0, 16, two_chunks, 0)

    total = part[ORDER[0, 0], 1].astype(F32)
    x_first[0].wait_recv()
    total = total + bx[0].astype(F32)
    for n in (1, 2, 3):
        z_second[n].wait_recv()
        total = total + bz[n - 1].astype(F32)
    final[0, 256:512, :] = total[:, 0:128]
    final[1, 256:512, :] = total[:, 128:256]
    total = part[ORDER[0, 0], 0].astype(F32)
    for n in (1, 2, 3):
        z_first[0, n].wait_recv()
        total = total + az[0, n - 1].astype(F32)
    x_second.wait_recv()
    total = total + ax[...].astype(F32)
    final[0, 0:256, :] = total[:, 0:128]
    final[1, 0:256, :] = total[:, 128:256]
    swap = remote(24, final.at[1 - me.c], out.at[me.c], sibling)
    swap.start()
    keep = pltpu.make_async_copy(final.at[me.c], out.at[me.c], local)
    keep.start()
    for copy in w_back:
        copy.wait_recv()
    swap.wait_recv()
    keep.wait()
    for copy in list(x_first.values()) + list(z_first.values()) + list(z_second.values()):
        copy.wait_send()
    for copy in [x_second, w_x, swap] + w_y + w_z + w_back:
        copy.wait_send()


def settle(dense, ball, gwx):
    half = (256, 256)
    return pl.pallas_call(
        settle_kernel,
        out_shape=(
            jax.ShapeDtypeStruct((2, 512, 128), F32),
            jax.ShapeDtypeStruct((4, 40, 512), F32),
        ),
        in_specs=[VMEM] * 3,
        out_specs=(VMEM, VMEM),
        scratch_shapes=[
            pltpu.VMEM((512, 1024), BF16),
            pltpu.VMEM((512, 1024), BF16),
            pltpu.VMEM((512, 256), F32),
            pltpu.VMEM((8, 2) + half, BF16),
            pltpu.VMEM((2, 3) + half, BF16),
            pltpu.VMEM(half, BF16),
            pltpu.VMEM(half, BF16),
            pltpu.VMEM((4,) + half, BF16),
            pltpu.VMEM((3,) + half, BF16),
            pltpu.VMEM((3,) + half, BF16),
            pltpu.VMEM((2, 512, 128), F32),
            pltpu.VMEM((4, 40, 512), F32),
            pltpu.VMEM((4, 40, 512), F32),
            pltpu.VMEM((40, 512), F32),
            pltpu.VMEM((40, 512), F32),
            DMA((25,)),
            DMA((25,)),
            DMA,
        ],
        compiler_params=pltpu.CompilerParams(
            collective_id=2, has_side_effects=True, vmem_limit_bytes=36 * MIB
        ),
        name="settle",
    )(dense, ball, gwx)


def body(features, weight, bias_vector, cotangent, tile_masks, tile_rows, tile_counts):
    masks = tile_masks.reshape(8, 4, 2, 16, 16, 128)
    dense, row, col, g, wc = spread(tile_rows[0].T, tile_counts.reshape(256), masks, features, weight)
    act, ball, gwx = layer(
        dense, g.reshape(8, 256, 512), row, col, wc, weight, bias_vector.reshape(4, 128), cotangent
    )
    out, gw = settle(dense, ball.reshape(4, 1024, 256), gwx)
    out = out.reshape(8, 8, 16, 128).transpose(0, 2, 1, 3).reshape(1024, 128) * col
    return act, out, gw[:, :32].reshape(128, 512), gw[0, 32]


def solution(mesh):
    return jax.shard_map(
        body,
        mesh=mesh,
        in_specs=(
            P("blk", "rep"),
            P("rep", None),
            P(),
            P("blk", "rep"),
            P("blk", None, None, None, None),
            P("blk", None, None),
            P("blk", None),
        ),
        out_specs=(P("blk", "rep"), P("blk", "rep"), P("rep", None), P()),
        check_vma=False,
    )
```

```python
import functools

import jax
import jax.numpy as jnp
from jax import lax
from jax.experimental import pallas as pl
from jax.experimental.pallas import tpu as pltpu
from jax.sharding import PartitionSpec as P

MESH = pl.DeviceIdType.MESH
BF16 = jnp.bfloat16
F32 = jnp.float32
VMEM = pl.BlockSpec(memory_space=pltpu.VMEM)
SMEM = pl.BlockSpec(memory_space=pltpu.SMEM)
DMA = pltpu.SemaphoreType.DMA
MIB = 2**20


class Place:
    def __init__(self):
        blk = lax.axis_index("blk")
        rep = lax.axis_index("rep")
        self.x, self.z, self.y = blk // 16, lax.rem(blk // 4, 4), lax.rem(blk, 4)
        self.xl, self.c = rep // 2, lax.rem(rep, 2)
        self.rep = rep
        self.xz = self.x * 4 + self.z

    def at(self, x=None, z=None, y=None, xl=None, c=None):
        x = self.x if x is None else x
        z = self.z if z is None else z
        y = self.y if y is None else y
        xl = self.xl if xl is None else xl
        c = self.c if c is None else c
        return (x * 16 + z * 4 + y, xl * 2 + c)

    def dy(self, n):
        return lax.rem(self.y + n, 4)

    def dz(self, n):
        return lax.rem(self.z + n, 4)


def greet(peers):
    barrier = pltpu.get_barrier_semaphore()
    for peer in peers:
        pl.semaphore_signal(barrier, inc=1, device_id=peer, device_id_type=MESH)
    pl.semaphore_wait(barrier, len(peers))


class Copies:
    def __init__(self, send, recv):
        self.send, self.recv, self.used = send, recv, []

    def start(self, src, dst, peer):
        n = len(self.used)
        copy = pltpu.make_async_remote_copy(
            src_ref=src, dst_ref=dst, send_sem=self.send.at[n], recv_sem=self.recv.at[n],
            device_id=peer, device_id_type=MESH,
        )
        copy.start()
        self.used.append(copy)
        return copy

    def wait_sends(self):
        for copy in self.used:
            copy.wait_send()


Y_ORDER = (2, 1, 3, 0)


def spread_kernel(rows_ref, counts_ref, masks, feat, w, dense, row, col, g, wc,
                  words, m16, rm, slots_s, slots_v, landed_v, landed_s, xt, send, recv, load, local):
    me = Place()
    own, other = me.c, 1 - me.c
    loads = []
    for q in range(8):
        half = own if q < 4 else other
        loads.append(pltpu.make_async_copy(masks.at[:, me.dy(Y_ORDER[q % 4]), half], words.at[q], load.at[q]))
        loads[q].start()

    sibling = me.at(c=1 - me.c)
    x_peer = me.at(x=1 - me.x)
    z_peers = [me.at(z=me.dz(n)) for n in (1, 2, 3)]
    y_peers = [me.at(y=me.dy(n)) for n in (1, 2, 3)]
    rep_peers = [sibling, me.at(xl=1 - me.xl), me.at(xl=1 - me.xl, c=1 - me.c)]
    greet(z_peers + y_peers + rep_peers + [x_peer])
    copies = Copies(send, recv)

    tile_row = lax.broadcasted_iota(jnp.int32, (8, 128), 0)

    def scan(q, degrees):
        n = Y_ORDER[q % 4]
        half = own if q < 4 else other
        loads[q].wait()

        def tiles(xz, degrees):
            first = ((xz * 4 + me.dy(n)) * 2 + half) * 4
            for tc in range(4):
                count = counts_ref[first + tc]
                for s in range(4):
                    slot = tc * 4 + s
                    t = jnp.where(s < count, rows_ref[s, first + tc], 8)
                    tile = words[q, xz, slot]
                    if q < 3:
                        m16[q, xz, slot] = tile.astype(jnp.int16)
                    elif q == 3:
                        rm[me.y, xz, slot] = tile.astype(jnp.int16)
                    if q < 4:
                        slots_s[q, 0, xz * 16 + slot] = t
                    joined = jnp.bitwise_or(tile[:8], jnp.left_shift(tile[8:], 8))
                    counted = jnp.sum(lax.population_count(joined), axis=0, keepdims=True)
                    degrees = degrees + jnp.where(tile_row == t, counted, 0)
            return degrees

        return lax.fori_loop(0, 8, tiles, degrees)

    degrees = jnp.zeros((8, 128), jnp.int32)
    mask_copies = []
    for q in range(3):
        degrees = scan(q, degrees)
        mask_copies.append(copies.start(m16.at[q], rm.at[me.y], y_peers[Y_ORDER[q] - 1]))
    for q in range(3, 8):
        degrees = scan(q, degrees)

    inv = lax.rsqrt(1.0 + degrees.astype(F32))
    place = lax.broadcasted_iota(jnp.int32, (128, 128), 1)
    source = 8 * jnp.bitwise_and(place, 15) + jnp.right_shift(place, 4)
    perm = jnp.where(lax.broadcasted_iota(jnp.int32, (128, 128), 0) == source, 1.0, 0.0).astype(BF16)
    for t in range(8):
        lanes = inv[t:t + 1, :]
        row[:, t * 128:(t + 1) * 128] = jnp.broadcast_to(lanes, (8, 128))
        spread = jnp.broadcast_to(lanes, (128, 128))
        col[t * 128:(t + 1) * 128, :] = spread.T
        scaled = (feat[t * 128:(t + 1) * 128, :].astype(F32).T * spread).astype(BF16)
        moved = jnp.dot(scaled, perm, preferred_element_type=F32).astype(BF16)
        xt[t // 4, :, (t % 4) * 128:(t % 4 + 1) * 128] = moved

    def at(core, xz):
        return g.at[xz, core]

    def weight_to(rep):
        return w.at[:, pl.ds(pl.multiple_of(rep * 128, 128), 128)]

    to_sibling = copies.start(xt.at[other], at(own, me.xz), sibling)
    first = [copies.start(xt.at[own], at(own, me.xz), p) for p in z_peers]
    across = copies.start(xt.at[own], at(own, me.xz), x_peer)
    stays = [
        pltpu.make_async_copy(xt.at[own], at(own, me.xz), local.at[0]),
        pltpu.make_async_copy(weight_to(me.rep), wc.at[me.rep], local.at[1]),
    ]
    for copy in stays:
        copy.start()
    to_vmem = pltpu.make_async_copy(slots_s, slots_v, local.at[2])
    to_vmem.start()
    to_vmem.wait()
    slot_copies = [copies.start(slots_v.at[q], landed_v.at[me.y], y_peers[Y_ORDER[q] - 1]) for q in range(3)]
    kept = pltpu.make_async_copy(slots_v.at[3], landed_v.at[me.y], local.at[3])
    kept.start()

    to_sibling.wait_recv()
    other_x = copies.start(at(other, me.xz), at(other, me.xz), x_peer)
    second = [copies.start(at(other, me.xz), at(other, me.xz), p) for p in z_peers]
    weights = [copies.start(weight_to(peer[1]), wc.at[me.rep], peer) for peer in rep_peers]

    def put_tiles(n, slot_rows, at):
        i = me.dy(n)

        def column(j, _):
            for tc in range(4):
                rows = [slot_rows[at, 0, j * 16 + tc * 4 + s] for s in range(4)]
                tiles = [rm[i, j, tc * 4 + s] for s in range(4)]
                for t in range(8):
                    found = jnp.zeros((16, 128), jnp.int16)
                    for s in range(4):
                        found = jnp.where(rows[s] == t, tiles[s], found)
                    dense[i * 8 + j, tc, t] = found
            return 0

        lax.fori_loop(0, 8, column, 0)

    last = []
    for n in (1, 2, 3):
        first[n - 1].wait_recv()
        source = me.x * 4 + me.dz(4 - n)
        last.append(copies.start(at(own, source), at(own, source), x_peer))
    other_x.wait_recv()
    far = (1 - me.x) * 4 + me.z
    last += [copies.start(at(other, far), at(other, far), p) for p in z_peers]
    put_tiles(0, slots_s, 3)
    kept.wait()
    for copy in slot_copies:
        copy.wait_recv()
    to_smem = pltpu.make_async_copy(landed_v, landed_s, local.at[4])
    to_smem.start()
    to_smem.wait()
    for q in range(3):
        mask_copies[q].wait_recv()
        put_tiles(4 - Y_ORDER[q], landed_s, me.dy(4 - Y_ORDER[q]))
    for copy in [across] + weights + second + last:
        copy.wait_recv()
    copies.wait_sends()
    for copy in stays:
        copy.wait()


def spread(rows, counts, masks, features, w):
    return pl.pallas_call(
        spread_kernel,
        out_shape=(
            jax.ShapeDtypeStruct((32, 4, 8, 16, 128), jnp.int16),
            jax.ShapeDtypeStruct((8, 1024), F32),
            jax.ShapeDtypeStruct((1024, 128), F32),
            jax.ShapeDtypeStruct((8, 2, 128, 512), BF16),
            jax.ShapeDtypeStruct((4, 128, 128), BF16),
        ),
        in_specs=[SMEM, SMEM, pl.BlockSpec(memory_space=pltpu.HBM), VMEM, VMEM],
        out_specs=(VMEM,) * 5,
        scratch_shapes=[
            pltpu.VMEM((8, 8, 16, 16, 128), jnp.int32),
            pltpu.VMEM((3, 8, 16, 16, 128), jnp.int16),
            pltpu.VMEM((4, 8, 16, 16, 128), jnp.int16),
            pltpu.SMEM((4, 1, 128), jnp.int32),
            pltpu.VMEM((4, 1, 128), jnp.int32),
            pltpu.VMEM((4, 1, 128), jnp.int32),
            pltpu.SMEM((4, 1, 128), jnp.int32),
            pltpu.VMEM((2, 128, 512), BF16),
            DMA((24,)),
            DMA((24,)),
            DMA((8,)),
            DMA((5,)),
        ],
        compiler_params=pltpu.CompilerParams(
            collective_id=0, has_side_effects=True, vmem_limit_bytes=44 * MIB
        ),
        name="spread",
    )(rows, counts, masks, features, w)


def table(values, step):
    found = values[-1]
    for n in range(len(values) - 1):
        found = jnp.where(step == n, values[n], found)
    return found


def unpack(dense, i, j, out_ref):
    one, zero = jnp.asarray(1, BF16), jnp.asarray(0, BF16)
    for tc in range(4):
        for t in range(8):
            words = dense[i * 8 + j, tc, t]
            for k in range(8):
                bits = jnp.where(jnp.bitwise_and(words, jnp.int16(1 << k)) != 0, one, zero)
                first = tc * 128 + k * 16
                out_ref[first:first + 16, t * 128:(t + 1) * 128] = bits


def layer_kernel(dense, g, row, col, wc, w, bias, cot, act, ball, gwx,
                 a0, a1, acc, part, rc, snd, ry, agg, agg_t, slope,
                 core_s, core_r, sum_s, sum_r, send, recv):
    me = Place()
    sibling = me.at(c=1 - me.c)
    xl_peer = me.at(xl=1 - me.xl)
    y_peers = [me.at(y=me.dy(n)) for n in (1, 2, 3)]
    greet([sibling, xl_peer] + y_peers)
    copies = Copies(send, recv)
    own, other = me.c, 1 - me.c

    def to_sibling(s):
        return pltpu.make_async_remote_copy(
            src_ref=part.at[s, other], dst_ref=rc.at[s], send_sem=core_s.at[s], recv_sem=core_r.at[s],
            device_id=sibling, device_id_type=MESH,
        )

    def rows_of(m):
        return pl.ds(pl.multiple_of(m * 256, 256), 256)

    def to_owner(k, m):
        return pltpu.make_async_remote_copy(
            src_ref=snd.at[k, m], dst_ref=ry.at[k, m], send_sem=sum_s.at[k * 4 + m], recv_sem=sum_r.at[k * 4 + m],
            device_id=me.at(y=me.dy(table((2, 1, 3), k))), device_id_type=MESH,
        )

    def pass_on(k):
        to_sibling(k).wait_recv()
        for m in range(4):
            rows = slice(m * 256, (m + 1) * 256)
            snd[k, m] = (part[k, own, :, rows].astype(F32) + rc[k, :, rows].astype(F32)).astype(BF16)
            to_owner(k, m).start()

    def rep_copy(buf, base, m, kind):
        theirs = (1 - me.xl) * 2 + me.c
        src = buf.at[theirs if kind == 2 else me.rep, rows_of(m), :]
        n = base + kind * 4 + m
        return pltpu.make_async_remote_copy(
            src_ref=src, dst_ref=src, send_sem=send.at[n], recv_sem=recv.at[n],
            device_id=xl_peer if kind == 1 else sibling, device_id_type=MESH,
        )

    def share(buf, base, m):
        rep_copy(buf, base, m, 1).start()
        rep_copy(buf, base, m, 0).start()

    def finish_sum(m):
        for k in range(3):
            to_owner(k, m).wait_recv()
        rows = slice(m * 256, (m + 1) * 256)
        total = part[3, own, :, rows].astype(F32) + rc[3, :, rows].astype(F32)
        for k in range(3):
            total = total + ry[k, m].astype(F32)
        total = total * row[0:1, rows]
        agg_t[:, rows] = total.astype(BF16)
        agg[me.rep, rows, :] = total.T.astype(BF16)
        share(agg, 0, m)

    def chunk(c):
        return me.dy(table((2, 1, 3, 0), c // 8)), lax.rem(c, 8)

    bufs = (a0, a1)
    unpack(dense, *chunk(0), a0)

    def two_chunks(n, _):
        k, pair = n // 4, lax.rem(n, 4)
        for h in range(2):
            unpack(dense, *chunk(jnp.minimum(n * 2 + h + 1, 31)), bufs[1 - h])
            prod = jnp.dot(g[pair * 2 + h], bufs[h][...], preferred_element_type=F32)
            if h == 0:
                acc[...] = jnp.where(pair == 0, 0.0, acc[...]) + prod
            else:
                acc[...] += prod

        @pl.when(pair == 3)
        def _():
            part[k, 0] = acc[0:128].astype(BF16)
            part[k, 1] = acc[128:256].astype(BF16)
            to_sibling(k).start()

        @pl.when(jnp.logical_and(pair == 0, k >= 1))
        def _():
            pass_on(k - 1)

        return 0

    lax.fori_loop(0, 16, two_chunks, 0)
    to_sibling(3).wait_recv()
    for m in range(4):
        finish_sum(m)

    def relay(buf, base, m):
        rep_copy(buf, base, m, 1).wait_recv()
        rep_copy(buf, base, m, 2).start()

    def settled(buf, base, m):
        rep_copy(buf, base, m, 0).wait_recv()
        rep_copy(buf, base, m, 2).wait_recv()

    def rows_forward(m):
        rows = rows_of(m)
        hidden = jnp.dot(agg[0, rows, :], wc[0], preferred_element_type=F32)
        for q in range(1, 4):
            hidden = hidden + jnp.dot(agg[q, rows, :], wc[q], preferred_element_type=F32)
        hidden = hidden + bias[pl.ds(me.rep, 1), :]
        logistic = jax.nn.sigmoid(hidden)
        act[rows, :] = hidden * logistic
        value = cot[rows, :].astype(F32) * logistic * (1.0 + hidden * (1.0 - logistic))
        slope[me.rep, rows, :] = value.astype(BF16)

    mine = pl.ds(pl.multiple_of(own * 128, 128), 128)

    def block(n, m):
        start = me.dy(n) * 1024 + m * 256
        return ball.at[pl.ds(pl.multiple_of(start, 256), 256), mine]

    def y_copy(n, m):
        k = 24 + (n - 1) * 4 + m
        return pltpu.make_async_remote_copy(
            src_ref=block(0, m), dst_ref=block(0, m), send_sem=send.at[k], recv_sem=recv.at[k],
            device_id=y_peers[n - 1], device_id_type=MESH,
        )

    def core_copy(n, m):
        k = 36 + n * 4 + m
        return pltpu.make_async_remote_copy(
            src_ref=block(n, m), dst_ref=block(n, m), send_sem=send.at[k], recv_sem=recv.at[k],
            device_id=sibling, device_id_type=MESH,
        )

    def rows_backward(m):
        rows = rows_of(m)
        total = jnp.zeros((256, 128), F32)
        for q in range(4):
            total = total + lax.dot_general(
                slope[q, rows, :], w[:, q * 128:(q + 1) * 128], (((1,), (1,)), ((), ())), preferred_element_type=F32
            )
        here = pl.ds(pl.multiple_of(me.y * 1024 + m * 256, 256), 256)
        ball[here, mine] = (total * col[rows, :]).astype(BF16)
        for n in (2, 1, 3):
            y_copy(n, m).start()
        core_copy(0, m).start()

    def layer_step(m, _):
        @pl.when(m < 4)
        def _():
            relay(agg, 0, m)

        @pl.when(jnp.logical_and(m >= 1, m < 5))
        def _():
            settled(agg, 0, m - 1)
            rows_forward(m - 1)
            share(slope, 12, m - 1)

        @pl.when(jnp.logical_and(m >= 2, m < 6))
        def _():
            relay(slope, 12, m - 2)

        @pl.when(m >= 3)
        def _():
            settled(slope, 12, m - 3)
            rows_backward(m - 3)

        return 0

    lax.fori_loop(0, 7, layer_step, 0)

    ones = jnp.ones((8, 1024), BF16)
    for q in range(4):
        lanes = slice(q * 128, (q + 1) * 128)
        grad = jnp.dot(agg_t[...], slope[q], preferred_element_type=F32)
        gb = jnp.dot(ones, slope[q], preferred_element_type=F32)
        for n in range(4):
            gwx[n, 0:32, lanes] = grad[n * 32:(n + 1) * 32]
            gwx[n, 32:40, lanes] = gb

    def pass_blocks(m, _):
        for n in (1, 3, 2):
            y_copy(n, m).wait_recv()
            core_copy(4 - n, m).start()
        return 0

    lax.fori_loop(0, 4, pass_blocks, 0)

    def finish(m, _):
        for n in range(4):
            core_copy(n, m).wait()
        for n in (1, 2, 3):
            y_copy(n, m).wait_send()
            to_owner(n - 1, m).wait_send()
        for kind in range(3):
            rep_copy(agg, 0, m, kind).wait_send()
            rep_copy(slope, 12, m, kind).wait_send()
        to_sibling(m).wait_send()
        return 0

    lax.fori_loop(0, 4, finish, 0)


def layer(dense, g, row, col, wc, w, bias, cot):
    return pl.pallas_call(
        layer_kernel,
        out_shape=(
            jax.ShapeDtypeStruct((1024, 128), F32),
            jax.ShapeDtypeStruct((4096, 256), BF16),
            jax.ShapeDtypeStruct((4, 40, 512), F32),
        ),
        in_specs=[VMEM] * 8,
        out_specs=(VMEM, VMEM, VMEM),
        scratch_shapes=[
            pltpu.VMEM((512, 1024), BF16),
            pltpu.VMEM((512, 1024), BF16),
            pltpu.VMEM((256, 1024), F32),
            pltpu.VMEM((4, 2, 128, 1024), BF16),
            pltpu.VMEM((4, 128, 1024), BF16),
            pltpu.VMEM((3, 4, 128, 256), BF16),
            pltpu.VMEM((3, 4, 128, 256), BF16),
            pltpu.VMEM((4, 1024, 128), BF16),
            pltpu.VMEM((128, 1024), BF16),
            pltpu.VMEM((4, 1024, 128), BF16),
            DMA((4,)),
            DMA((4,)),
            DMA((12,)),
            DMA((12,)),
            DMA((52,)),
            DMA((52,)),
        ],
        compiler_params=pltpu.CompilerParams(
            collective_id=1, has_side_effects=True, vmem_limit_bytes=36 * MIB
        ),
        name="layer",
    )(dense, g, row, col, wc, w, bias, cot)


BLOCKS = ((1, 2), (1, 1), (1, 3), (1, 0), (0, 2), (0, 1), (0, 3), (0, 0))
ORDER = {key: n for n, key in enumerate(BLOCKS)}


def settle_kernel(dense, ball, gwx, out, gw, a0, a1, acc, part, az, a_sum, ax, bx, b_sum, bz, final,
                  wy, wz, wx_send, wx, send, recv, local):
    me = Place()
    sibling = me.at(c=1 - me.c)
    x_peer = me.at(x=1 - me.x)
    z_peers = [me.at(z=me.dz(n)) for n in (1, 2, 3)]
    y_peers = [me.at(y=me.dy(n)) for n in (1, 2, 3)]
    greet(z_peers + y_peers + [x_peer, sibling])

    def remote(n, src, dst, peer):
        return pltpu.make_async_remote_copy(
            src_ref=src, dst_ref=dst, send_sem=send.at[n], recv_sem=recv.at[n],
            device_id=peer, device_id_type=MESH,
        )

    x_first = {n: remote(n, part.at[ORDER[1, n], 1], bx.at[n], x_peer) for n in range(4)}
    z_first = {
        (side, n): remote(4 + side * 3 + n - 1, part.at[ORDER[side, n], 0], az.at[side, n - 1], z_peers[n - 1])
        for side in range(2) for n in (1, 2, 3)
    }
    z_second = {n: remote(9 + n, b_sum.at[n - 1], bz.at[n - 1], z_peers[n - 1]) for n in (1, 2, 3)}
    x_second = remote(13, a_sum, ax, x_peer)
    w_y = [remote(13 + n, gwx.at[me.dy(n)], wy.at[me.y], y_peers[n - 1]) for n in (1, 2, 3)]
    w_z = [remote(16 + n, wz.at[me.z], wz.at[me.z], z_peers[n - 1]) for n in (1, 2, 3)]
    w_x = remote(20, wx_send, wx, x_peer)
    w_back = [remote(20 + n, gw.at[me.y], gw.at[me.y], y_peers[n - 1]) for n in (1, 2, 3)]

    def pass_b(n):
        x_first[n].wait_recv()
        b_sum[n - 1] = (part[ORDER[0, n], 1].astype(F32) + bx[n].astype(F32)).astype(BF16)
        z_second[n].start()

    def pass_a():
        total = part[ORDER[1, 0], 0].astype(F32)
        for n in (1, 2, 3):
            z_first[1, n].wait_recv()
            total = total + az[1, n - 1].astype(F32)
        a_sum[...] = total.astype(BF16)
        x_second.start()

    def weights_z():
        for copy in w_y:
            copy.wait_recv()
        wz[me.z] = (wy[0] + wy[1]) + (wy[2] + wy[3])
        for copy in w_z:
            copy.start()

    def weights_x():
        for copy in w_z:
            copy.wait_recv()
        wx_send[...] = (wz[0] + wz[1]) + (wz[2] + wz[3])
        w_x.start()

    def weights_back():
        w_x.wait_recv()
        gw[me.y] = wx_send[...] + wx[...]
        for copy in w_back:
            copy.start()

    actions = {n: [] for n in range(8)}
    for n in range(4):
        actions[ORDER[1, n]].append(x_first[n].start)
    for n in (2, 1, 3):
        actions[ORDER[0, n]].append(functools.partial(pass_b, n))
    for key, copy in z_first.items():
        actions[ORDER[key]].append(copy.start)
    actions[3].append(weights_z)
    actions[4].append(pass_a)
    actions[5].append(weights_x)
    actions[6].append(weights_back)

    for copy in w_y:
        copy.start()
    wy[me.y] = gwx[me.y]

    def chunk(c):
        at = c // 4
        x = lax.rem(me.x + table([block[0] for block in BLOCKS], at), 2)
        z = lax.rem(me.z + table([block[1] for block in BLOCKS], at), 4)
        return lax.rem(c, 4), x * 4 + z

    bufs = (a0, a1)
    unpack(dense, *chunk(0), a0)

    def two_chunks(step, _):
        block, pair = step // 2, lax.rem(step, 2)
        for h in range(2):
            unpack(dense, *chunk(jnp.minimum(step * 2 + h + 1, 31)), bufs[1 - h])
            prod = jnp.dot(bufs[h][...], ball[pair * 2 + h], preferred_element_type=F32)
            if h == 0:
                acc[...] = jnp.where(pair == 0, 0.0, acc[...]) + prod
            else:
                acc[...] += prod

        @pl.when(pair == 1)
        def _():
            part[block, 0] = acc[0:256].astype(BF16)
            part[block, 1] = acc[256:512].astype(BF16)

        for at, calls in actions.items():
            if calls:
                @pl.when(step == at * 2 + 1)
                def _():
                    for call in calls:
                        call()

        return 0

    lax.fori_loop(0, 16, two_chunks, 0)

    total = part[ORDER[0, 0], 1].astype(F32)
    x_first[0].wait_recv()
    total = total + bx[0].astype(F32)
    for n in (1, 2, 3):
        z_second[n].wait_recv()
        total = total + bz[n - 1].astype(F32)
    final[0, 256:512, :] = total[:, 0:128]
    final[1, 256:512, :] = total[:, 128:256]
    total = part[ORDER[0, 0], 0].astype(F32)
    for n in (1, 2, 3):
        z_first[0, n].wait_recv()
        total = total + az[0, n - 1].astype(F32)
    x_second.wait_recv()
    total = total + ax[...].astype(F32)
    final[0, 0:256, :] = total[:, 0:128]
    final[1, 0:256, :] = total[:, 128:256]
    swap = remote(24, final.at[1 - me.c], out.at[me.c], sibling)
    swap.start()
    keep = pltpu.make_async_copy(final.at[me.c], out.at[me.c], local)
    keep.start()
    for copy in w_back:
        copy.wait_recv()
    swap.wait_recv()
    keep.wait()
    for copy in list(x_first.values()) + list(z_first.values()) + list(z_second.values()):
        copy.wait_send()
    for copy in [x_second, w_x, swap] + w_y + w_z + w_back:
        copy.wait_send()


def settle(dense, ball, gwx):
    half = (256, 256)
    return pl.pallas_call(
        settle_kernel,
        out_shape=(
            jax.ShapeDtypeStruct((2, 512, 128), F32),
            jax.ShapeDtypeStruct((4, 40, 512), F32),
        ),
        in_specs=[VMEM] * 3,
        out_specs=(VMEM, VMEM),
        scratch_shapes=[
            pltpu.VMEM((512, 1024), BF16),
            pltpu.VMEM((512, 1024), BF16),
            pltpu.VMEM((512, 256), F32),
            pltpu.VMEM((8, 2) + half, BF16),
            pltpu.VMEM((2, 3) + half, BF16),
            pltpu.VMEM(half, BF16),
            pltpu.VMEM(half, BF16),
            pltpu.VMEM((4,) + half, BF16),
            pltpu.VMEM((3,) + half, BF16),
            pltpu.VMEM((3,) + half, BF16),
            pltpu.VMEM((2, 512, 128), F32),
            pltpu.VMEM((4, 40, 512), F32),
            pltpu.VMEM((4, 40, 512), F32),
            pltpu.VMEM((40, 512), F32),
            pltpu.VMEM((40, 512), F32),
            DMA((25,)),
            DMA((25,)),
            DMA,
        ],
        compiler_params=pltpu.CompilerParams(
            collective_id=2, has_side_effects=True, vmem_limit_bytes=36 * MIB
        ),
        name="settle",
    )(dense, ball, gwx)


def body(features, weight, bias_vector, cotangent, tile_masks, tile_rows, tile_counts):
    masks = tile_masks.reshape(8, 4, 2, 16, 16, 128)
    dense, row, col, g, wc = spread(tile_rows[0].T, tile_counts.reshape(256), masks, features, weight)
    act, ball, gwx = layer(
        dense, g.reshape(8, 256, 512), row, col, wc, weight, bias_vector.reshape(4, 128), cotangent
    )
    out, gw = settle(dense, ball.reshape(4, 1024, 256), gwx)
    out = out.reshape(8, 8, 16, 128).transpose(0, 2, 1, 3).reshape(1024, 128) * col
    return act, out, gw[:, :32].reshape(128, 512), gw[0, 32]


def solution(mesh):
    return jax.shard_map(
        body,
        mesh=mesh,
        in_specs=(
            P("blk", "rep"),
            P("rep", None),
            P(),
            P("blk", "rep"),
            P("blk", None, None, None, None),
            P("blk", None, None),
            P("blk", None),
        ),
        out_specs=(P("blk", "rep"), P("blk", "rep"), P("rep", None), P()),
        check_vma=False,
    )
```

```python
import functools

import jax
import jax.numpy as jnp
from jax import lax
from jax.experimental import pallas as pl
from jax.experimental.pallas import tpu as pltpu
from jax.sharding import PartitionSpec as P

MESH = pl.DeviceIdType.MESH
BF16 = jnp.bfloat16
F32 = jnp.float32
VMEM = pl.BlockSpec(memory_space=pltpu.VMEM)
SMEM = pl.BlockSpec(memory_space=pltpu.SMEM)
DMA = pltpu.SemaphoreType.DMA
MIB = 2**20


class Place:
    def __init__(self):
        blk = lax.axis_index("blk")
        rep = lax.axis_index("rep")
        self.x, self.z, self.y = blk // 16, lax.rem(blk // 4, 4), lax.rem(blk, 4)
        self.xl, self.c = rep // 2, lax.rem(rep, 2)
        self.rep = rep
        self.xz = self.x * 4 + self.z

    def at(self, x=None, z=None, y=None, xl=None, c=None):
        x = self.x if x is None else x
        z = self.z if z is None else z
        y = self.y if y is None else y
        xl = self.xl if xl is None else xl
        c = self.c if c is None else c
        return (x * 16 + z * 4 + y, xl * 2 + c)

    def dy(self, n):
        return lax.rem(self.y + n, 4)

    def dz(self, n):
        return lax.rem(self.z + n, 4)


def greet(peers):
    barrier = pltpu.get_barrier_semaphore()
    for peer in peers:
        pl.semaphore_signal(barrier, inc=1, device_id=peer, device_id_type=MESH)
    pl.semaphore_wait(barrier, len(peers))


class Copies:
    def __init__(self, send, recv):
        self.send, self.recv, self.used = send, recv, []

    def start(self, src, dst, peer):
        n = len(self.used)
        copy = pltpu.make_async_remote_copy(
            src_ref=src, dst_ref=dst, send_sem=self.send.at[n], recv_sem=self.recv.at[n],
            device_id=peer, device_id_type=MESH,
        )
        copy.start()
        self.used.append(copy)
        return copy

    def wait_sends(self):
        for copy in self.used:
            copy.wait_send()


Y_ORDER = (2, 1, 3, 0)


def spread_kernel(rows_ref, counts_ref, masks, feat, w, cot, dense, row, col, g, wc, cotr,
                  words, m16, rm, slots_s, slots_v, landed_v, landed_s, xt, send, recv, load, local):
    me = Place()
    own, other = me.c, 1 - me.c
    loads = []
    for q in range(8):
        half = own if q < 4 else other
        loads.append(pltpu.make_async_copy(masks.at[:, me.dy(Y_ORDER[q % 4]), half], words.at[q], load.at[q]))
        loads[q].start()

    sibling = me.at(c=1 - me.c)
    x_peer = me.at(x=1 - me.x)
    z_peers = [me.at(z=me.dz(n)) for n in (1, 2, 3)]
    y_peers = [me.at(y=me.dy(n)) for n in (1, 2, 3)]
    rep_peers = [sibling, me.at(xl=1 - me.xl), me.at(xl=1 - me.xl, c=1 - me.c)]
    greet(z_peers + y_peers + rep_peers + [x_peer])
    copies = Copies(send, recv)

    def cot_rows(rep):
        return cot.at[pl.ds(pl.multiple_of(rep * 256, 256), 256), :]

    early = []
    for peer in rep_peers:
        early.append(copies.start(cot_rows(peer[1]), cotr.at[me.rep], peer))
        early.append(copies.start(w, wc.at[me.rep], peer))
    tile_row = lax.broadcasted_iota(jnp.int32, (8, 128), 0)

    def scan(q, degrees):
        n = Y_ORDER[q % 4]
        half = own if q < 4 else other
        loads[q].wait()

        def tiles(xz, degrees):
            first = ((xz * 4 + me.dy(n)) * 2 + half) * 4
            for tc in range(4):
                count = counts_ref[first + tc]
                for s in range(4):
                    slot = tc * 4 + s
                    t = jnp.where(s < count, rows_ref[s, first + tc], 8)
                    tile = words[q, xz, slot]
                    if q < 3:
                        m16[q, xz, slot] = tile.astype(jnp.int16)
                    elif q == 3:
                        rm[me.y, xz, slot] = tile.astype(jnp.int16)
                    if q < 4:
                        slots_s[q, 0, xz * 16 + slot] = t
                    joined = jnp.bitwise_or(tile[:8], jnp.left_shift(tile[8:], 8))
                    counted = jnp.sum(lax.population_count(joined), axis=0, keepdims=True)
                    degrees = degrees + jnp.where(tile_row == t, counted, 0)
            return degrees

        return lax.fori_loop(0, 8, tiles, degrees)

    degrees = jnp.zeros((8, 128), jnp.int32)
    mask_copies = []
    for q in range(3):
        degrees = scan(q, degrees)
        mask_copies.append(copies.start(m16.at[q], rm.at[me.y], y_peers[Y_ORDER[q] - 1]))
    for q in range(3, 8):
        degrees = scan(q, degrees)

    inv = lax.rsqrt(1.0 + degrees.astype(F32))
    place = lax.broadcasted_iota(jnp.int32, (128, 128), 1)
    source = 8 * jnp.bitwise_and(place, 15) + jnp.right_shift(place, 4)
    perm = jnp.where(lax.broadcasted_iota(jnp.int32, (128, 128), 0) == source, 1.0, 0.0).astype(BF16)
    for t in range(8):
        lanes = inv[t:t + 1, :]
        row[:, t * 128:(t + 1) * 128] = jnp.broadcast_to(lanes, (8, 128))
        spread = jnp.broadcast_to(lanes, (128, 128))
        col[t * 128:(t + 1) * 128, :] = spread.T
        scaled = (feat[t * 128:(t + 1) * 128, :].astype(F32).T * spread).astype(BF16)
        moved = jnp.dot(scaled, perm, preferred_element_type=F32).astype(BF16)
        xt[t // 4, :, (t % 4) * 128:(t % 4 + 1) * 128] = moved

    def at(core, xz):
        return g.at[xz, core]

    to_sibling = copies.start(xt.at[other], at(own, me.xz), sibling)
    first = [copies.start(xt.at[own], at(own, me.xz), p) for p in z_peers]
    across = copies.start(xt.at[own], at(own, me.xz), x_peer)
    stays = [
        pltpu.make_async_copy(xt.at[own], at(own, me.xz), local.at[0]),
        pltpu.make_async_copy(w, wc.at[me.rep], local.at[1]),
        pltpu.make_async_copy(cot_rows(me.rep), cotr.at[me.rep], local.at[5]),
    ]
    for copy in stays:
        copy.start()
    to_vmem = pltpu.make_async_copy(slots_s, slots_v, local.at[2])
    to_vmem.start()
    to_vmem.wait()
    slot_copies = [copies.start(slots_v.at[q], landed_v.at[me.y], y_peers[Y_ORDER[q] - 1]) for q in range(3)]
    kept = pltpu.make_async_copy(slots_v.at[3], landed_v.at[me.y], local.at[3])
    kept.start()

    to_sibling.wait_recv()
    other_x = copies.start(at(other, me.xz), at(other, me.xz), x_peer)
    second = [copies.start(at(other, me.xz), at(other, me.xz), p) for p in z_peers]

    def put_tiles(n, slot_rows, at):
        i = me.dy(n)

        def column(j, _):
            for tc in range(4):
                rows = [slot_rows[at, 0, j * 16 + tc * 4 + s] for s in range(4)]
                tiles = [rm[i, j, tc * 4 + s] for s in range(4)]
                for t in range(8):
                    found = jnp.zeros((16, 128), jnp.int16)
                    for s in range(4):
                        found = jnp.where(rows[s] == t, tiles[s], found)
                    dense[i * 8 + j, tc, t] = found
            return 0

        lax.fori_loop(0, 8, column, 0)

    last = []
    for n in (1, 2, 3):
        first[n - 1].wait_recv()
        source = me.x * 4 + me.dz(4 - n)
        last.append(copies.start(at(own, source), at(own, source), x_peer))
    other_x.wait_recv()
    far = (1 - me.x) * 4 + me.z
    last += [copies.start(at(other, far), at(other, far), p) for p in z_peers]
    put_tiles(0, slots_s, 3)
    kept.wait()
    for copy in slot_copies:
        copy.wait_recv()
    to_smem = pltpu.make_async_copy(landed_v, landed_s, local.at[4])
    to_smem.start()
    to_smem.wait()
    for q in range(3):
        mask_copies[q].wait_recv()
        put_tiles(4 - Y_ORDER[q], landed_s, me.dy(4 - Y_ORDER[q]))
    for copy in [across] + early + second + last:
        copy.wait_recv()
    copies.wait_sends()
    for copy in stays:
        copy.wait()


def spread(rows, counts, masks, features, w, cot):
    return pl.pallas_call(
        spread_kernel,
        out_shape=(
            jax.ShapeDtypeStruct((32, 4, 8, 16, 128), jnp.int16),
            jax.ShapeDtypeStruct((8, 1024), F32),
            jax.ShapeDtypeStruct((1024, 128), F32),
            jax.ShapeDtypeStruct((8, 2, 128, 512), BF16),
            jax.ShapeDtypeStruct((4, 128, 512), BF16),
            jax.ShapeDtypeStruct((4, 256, 128), BF16),
        ),
        in_specs=[SMEM, SMEM, pl.BlockSpec(memory_space=pltpu.HBM), VMEM, VMEM, VMEM],
        out_specs=(VMEM,) * 6,
        scratch_shapes=[
            pltpu.VMEM((8, 8, 16, 16, 128), jnp.int32),
            pltpu.VMEM((3, 8, 16, 16, 128), jnp.int16),
            pltpu.VMEM((4, 8, 16, 16, 128), jnp.int16),
            pltpu.SMEM((4, 1, 128), jnp.int32),
            pltpu.VMEM((4, 1, 128), jnp.int32),
            pltpu.VMEM((4, 1, 128), jnp.int32),
            pltpu.SMEM((4, 1, 128), jnp.int32),
            pltpu.VMEM((2, 128, 512), BF16),
            DMA((27,)),
            DMA((27,)),
            DMA((8,)),
            DMA((6,)),
        ],
        compiler_params=pltpu.CompilerParams(
            collective_id=0, has_side_effects=True, vmem_limit_bytes=44 * MIB
        ),
        name="spread",
    )(rows, counts, masks, features, w, cot)


def table(values, step):
    found = values[-1]
    for n in range(len(values) - 1):
        found = jnp.where(step == n, values[n], found)
    return found


def unpack(dense, i, j, out_ref):
    one, zero = jnp.asarray(1, BF16), jnp.asarray(0, BF16)
    for tc in range(4):
        for t in range(8):
            words = dense[i * 8 + j, tc, t]
            for k in range(8):
                bits = jnp.where(jnp.bitwise_and(words, jnp.int16(1 << k)) != 0, one, zero)
                first = tc * 128 + k * 16
                out_ref[first:first + 16, t * 128:(t + 1) * 128] = bits


def layer_kernel(dense, g, row, col, wc, bias, cotr, act, ball, gwx,
                 a0, a1, acc, part, rc, snd, ry, agg_s, agg, agg_t, slope, act_s, back_s,
                 core_s, core_r, sum_s, sum_r, send, recv):
    me = Place()
    sibling = me.at(c=1 - me.c)
    xl_peer = me.at(xl=1 - me.xl)
    xl_other = me.at(xl=1 - me.xl, c=1 - me.c)
    y_peers = [me.at(y=me.dy(n)) for n in (1, 2, 3)]
    greet([sibling, xl_peer, xl_other] + y_peers)
    copies = Copies(send, recv)
    own, other = me.c, 1 - me.c

    def to_sibling(s):
        return pltpu.make_async_remote_copy(
            src_ref=part.at[s, other], dst_ref=rc.at[s], send_sem=core_s.at[s], recv_sem=core_r.at[s],
            device_id=sibling, device_id_type=MESH,
        )

    def rows_of(m):
        return pl.ds(pl.multiple_of(m * 256, 256), 256)

    def to_owner(k, m):
        return pltpu.make_async_remote_copy(
            src_ref=snd.at[k, m], dst_ref=ry.at[k, m], send_sem=sum_s.at[k * 4 + m], recv_sem=sum_r.at[k * 4 + m],
            device_id=me.at(y=me.dy(table((2, 1, 3), k))), device_id_type=MESH,
        )

    def pass_on(k):
        to_sibling(k).wait_recv()
        for m in range(4):
            rows = slice(m * 256, (m + 1) * 256)
            snd[k, m] = (part[k, own, :, rows].astype(F32) + rc[k, :, rows].astype(F32)).astype(BF16)
            to_owner(k, m).start()

    def chunk(c):
        return me.dy(table((2, 1, 3, 0), c // 8)), lax.rem(c, 8)

    bufs = (a0, a1)
    unpack(dense, *chunk(0), a0)

    def two_chunks(n, _):
        k, pair = n // 4, lax.rem(n, 4)
        for h in range(2):
            unpack(dense, *chunk(jnp.minimum(n * 2 + h + 1, 31)), bufs[1 - h])
            prod = jnp.dot(g[pair * 2 + h], bufs[h][...], preferred_element_type=F32)
            if h == 0:
                acc[...] = jnp.where(pair == 0, 0.0, acc[...]) + prod
            else:
                acc[...] += prod

        @pl.when(pair == 3)
        def _():
            part[k, 0] = acc[0:128].astype(BF16)
            part[k, 1] = acc[128:256].astype(BF16)
            to_sibling(k).start()

        @pl.when(jnp.logical_and(pair == 0, k >= 1))
        def _():
            pass_on(k - 1)

        return 0

    lax.fori_loop(0, 16, two_chunks, 0)
    to_sibling(3).wait_recv()

    def finish_sum(m, out):
        for k in range(3):
            to_owner(k, m).wait_recv()
        rows = rows_of(m)
        total = part[3, own, :, rows].astype(F32) + rc[3, :, rows].astype(F32)
        for k in range(3):
            total = total + ry[k, m].astype(F32)
        total = total * row[0:1, rows]
        agg_t[:, rows] = total.astype(BF16)
        out[...] = total.T.astype(BF16)

    swaps = []
    peers = (xl_peer, xl_other, sibling)
    for n in range(3):
        finish_sum(peers[n][1], agg_s.at[n])
        swaps.append(copies.start(agg_s.at[n], agg.at[me.rep], peers[n]))
    finish_sum(me.rep, agg.at[me.rep])
    for copy in reversed(swaps):
        copy.wait_recv()

    for half in range(2):
        rows = slice(half * 128, (half + 1) * 128)
        hidden = jnp.dot(agg[0, rows, :], wc[0], preferred_element_type=F32)
        for q in range(1, 4):
            hidden = hidden + jnp.dot(agg[q, rows, :], wc[q], preferred_element_type=F32)
        hidden = hidden + bias[...]
        logistic = jax.nn.sigmoid(hidden)
        value = hidden * logistic
        factor = logistic * (1.0 + hidden * (1.0 - logistic))
        for q in range(4):
            lanes = slice(q * 128, (q + 1) * 128)
            act_s[q, rows, :] = value[:, lanes]
            slope[me.rep, rows, lanes] = (cotr[q, rows, :].astype(F32) * factor[:, lanes]).astype(BF16)

    def block(y, rep):
        return ball.at[pl.ds(pl.multiple_of(y * 1024 + rep * 256, 256), 256), :]

    def back_into(xl, out):
        for core in range(2):
            value = lax.dot_general(
                slope[me.rep], wc[xl * 2 + core], (((1,), (1,)), ((), ())), preferred_element_type=F32
            )
            out[:, core * 128:(core + 1) * 128] = (value * col[rows_of(me.rep), :]).astype(BF16)

    theirs = (1 - me.xl) * 2 + me.c
    back_into(1 - me.xl, back_s)
    from_xl = copies.start(back_s, block(me.y, me.rep), xl_peer)
    back_into(me.xl, block(me.y, me.rep))

    def send_block(rep):
        here = block(me.y, rep)
        return [copies.start(here, here, y_peers[n - 1]) for n in (2, 1, 3)] + [copies.start(here, here, sibling)]

    mine = send_block(me.rep)
    slope_far = copies.start(slope.at[me.rep], slope.at[me.rep], xl_peer)
    slope_near = copies.start(slope.at[me.rep], slope.at[me.rep], sibling)
    from_xl.wait_recv()
    passed = send_block(theirs)
    acts = [
        copies.start(act_s.at[peer[1]], act.at[rows_of(me.rep), :], peer)
        for peer in (xl_peer, xl_other, sibling)
    ]
    act[rows_of(me.rep), :] = act_s[me.rep]
    slope_far.wait_recv()
    slope_relay = copies.start(slope.at[theirs], slope.at[theirs], sibling)

    relays = []
    for sent, rep in ((mine, me.rep), (passed, theirs)):
        if rep is theirs:
            slope_near.wait_recv()
            slope_relay.wait_recv()
            ones = jnp.ones((8, 256), BF16)
            grad = jnp.zeros((128, 512), F32)
            gb = jnp.zeros((8, 512), F32)
            for q in range(4):
                grad = grad + jnp.dot(agg_t[:, q * 256:(q + 1) * 256], slope[q], preferred_element_type=F32)
                gb = gb + jnp.dot(ones, slope[q], preferred_element_type=F32)
            for n in range(4):
                gwx[n, 0:32, :] = grad[n * 32:(n + 1) * 32]
                gwx[n, 32:40, :] = gb
        for n, copy in zip((2, 1, 3), sent):
            copy.wait_recv()
            here = block(me.dy(4 - n), rep)
            relays.append(copies.start(here, here, sibling))
    for copy in [mine[3], passed[3]] + relays + acts:
        copy.wait_recv()
    copies.wait_sends()
    for k in range(3):
        for m in range(4):
            to_owner(k, m).wait_send()
    for k in range(4):
        to_sibling(k).wait_send()


def layer(dense, g, row, col, wc, bias, cotr):
    return pl.pallas_call(
        layer_kernel,
        out_shape=(
            jax.ShapeDtypeStruct((1024, 128), F32),
            jax.ShapeDtypeStruct((4096, 256), BF16),
            jax.ShapeDtypeStruct((4, 40, 512), F32),
        ),
        in_specs=[VMEM] * 7,
        out_specs=(VMEM, VMEM, VMEM),
        scratch_shapes=[
            pltpu.VMEM((512, 1024), BF16),
            pltpu.VMEM((512, 1024), BF16),
            pltpu.VMEM((256, 1024), F32),
            pltpu.VMEM((4, 2, 128, 1024), BF16),
            pltpu.VMEM((4, 128, 1024), BF16),
            pltpu.VMEM((3, 4, 128, 256), BF16),
            pltpu.VMEM((3, 4, 128, 256), BF16),
            pltpu.VMEM((3, 256, 128), BF16),
            pltpu.VMEM((4, 256, 128), BF16),
            pltpu.VMEM((128, 1024), BF16),
            pltpu.VMEM((4, 256, 512), BF16),
            pltpu.VMEM((4, 256, 128), F32),
            pltpu.VMEM((256, 256), BF16),
            DMA((4,)),
            DMA((4,)),
            DMA((12,)),
            DMA((12,)),
            DMA((24,)),
            DMA((24,)),
        ],
        compiler_params=pltpu.CompilerParams(
            collective_id=1, has_side_effects=True, vmem_limit_bytes=36 * MIB
        ),
        name="layer",
    )(dense, g, row, col, wc, bias, cotr)


BLOCKS = ((1, 2), (1, 1), (1, 3), (1, 0), (0, 2), (0, 1), (0, 3), (0, 0))
ORDER = {key: n for n, key in enumerate(BLOCKS)}


def settle_kernel(dense, ball, gwx, out, gw, a0, a1, acc, part, az, a_sum, ax, bx, b_sum, bz, final,
                  wy, wz, wx_send, wx, send, recv, local):
    me = Place()
    sibling = me.at(c=1 - me.c)
    x_peer = me.at(x=1 - me.x)
    z_peers = [me.at(z=me.dz(n)) for n in (1, 2, 3)]
    y_peers = [me.at(y=me.dy(n)) for n in (1, 2, 3)]
    greet(z_peers + y_peers + [x_peer, sibling])

    def remote(n, src, dst, peer):
        return pltpu.make_async_remote_copy(
            src_ref=src, dst_ref=dst, send_sem=send.at[n], recv_sem=recv.at[n],
            device_id=peer, device_id_type=MESH,
        )

    x_first = {n: remote(n, part.at[ORDER[1, n], 1], bx.at[n], x_peer) for n in range(4)}
    z_first = {
        (side, n): remote(4 + side * 3 + n - 1, part.at[ORDER[side, n], 0], az.at[side, n - 1], z_peers[n - 1])
        for side in range(2) for n in (1, 2, 3)
    }
    z_second = {n: remote(9 + n, b_sum.at[n - 1], bz.at[n - 1], z_peers[n - 1]) for n in (1, 2, 3)}
    x_second = remote(13, a_sum, ax, x_peer)
    w_y = [remote(13 + n, gwx.at[me.dy(n)], wy.at[me.y], y_peers[n - 1]) for n in (1, 2, 3)]
    w_z = [remote(16 + n, wz.at[me.z], wz.at[me.z], z_peers[n - 1]) for n in (1, 2, 3)]
    w_x = remote(20, wx_send, wx, x_peer)
    w_back = [remote(20 + n, gw.at[me.y], gw.at[me.y], y_peers[n - 1]) for n in (1, 2, 3)]

    def pass_b(n):
        x_first[n].wait_recv()
        b_sum[n - 1] = (part[ORDER[0, n], 1].astype(F32) + bx[n].astype(F32)).astype(BF16)
        z_second[n].start()

    def pass_a():
        total = part[ORDER[1, 0], 0].astype(F32)
        for n in (1, 2, 3):
            z_first[1, n].wait_recv()
            total = total + az[1, n - 1].astype(F32)
        a_sum[...] = total.astype(BF16)
        x_second.start()

    def weights_z():
        for copy in w_y:
            copy.wait_recv()
        wz[me.z] = (wy[0] + wy[1]) + (wy[2] + wy[3])
        for copy in w_z:
            copy.start()

    def weights_x():
        for copy in w_z:
            copy.wait_recv()
        wx_send[...] = (wz[0] + wz[1]) + (wz[2] + wz[3])
        w_x.start()

    def weights_back():
        w_x.wait_recv()
        gw[me.y] = wx_send[...] + wx[...]
        for copy in w_back:
            copy.start()

    actions = {n: [] for n in range(8)}
    for n in range(4):
        actions[ORDER[1, n]].append(x_first[n].start)
    for n in (2, 1, 3):
        actions[ORDER[0, n]].append(functools.partial(pass_b, n))
    for key, copy in z_first.items():
        actions[ORDER[key]].append(copy.start)
    actions[3].append(weights_z)
    actions[4].append(pass_a)
    actions[5].append(weights_x)
    actions[6].append(weights_back)

    for copy in w_y:
        copy.start()
    wy[me.y] = gwx[me.y]

    def chunk(c):
        at = c // 4
        x = lax.rem(me.x + table([block[0] for block in BLOCKS], at), 2)
        z = lax.rem(me.z + table([block[1] for block in BLOCKS], at), 4)
        return lax.rem(c, 4), x * 4 + z

    bufs = (a0, a1)
    unpack(dense, *chunk(0), a0)

    def two_chunks(step, _):
        block, pair = step // 2, lax.rem(step, 2)
        for h in range(2):
            unpack(dense, *chunk(jnp.minimum(step * 2 + h + 1, 31)), bufs[1 - h])
            prod = jnp.dot(bufs[h][...], ball[pair * 2 + h], preferred_element_type=F32)
            if h == 0:
                acc[...] = jnp.where(pair == 0, 0.0, acc[...]) + prod
            else:
                acc[...] += prod

        @pl.when(pair == 1)
        def _():
            part[block, 0] = acc[0:256].astype(BF16)
            part[block, 1] = acc[256:512].astype(BF16)

        for at, calls in actions.items():
            if calls:
                @pl.when(step == at * 2 + 1)
                def _():
                    for call in calls:
                        call()

        return 0

    lax.fori_loop(0, 16, two_chunks, 0)

    total = part[ORDER[0, 0], 1].astype(F32)
    x_first[0].wait_recv()
    total = total + bx[0].astype(F32)
    for n in (1, 2, 3):
        z_second[n].wait_recv()
        total = total + bz[n - 1].astype(F32)
    final[0, 256:512, :] = total[:, 0:128]
    final[1, 256:512, :] = total[:, 128:256]
    total = part[ORDER[0, 0], 0].astype(F32)
    for n in (1, 2, 3):
        z_first[0, n].wait_recv()
        total = total + az[0, n - 1].astype(F32)
    x_second.wait_recv()
    total = total + ax[...].astype(F32)
    final[0, 0:256, :] = total[:, 0:128]
    final[1, 0:256, :] = total[:, 128:256]
    swap = remote(24, final.at[1 - me.c], out.at[me.c], sibling)
    swap.start()
    keep = pltpu.make_async_copy(final.at[me.c], out.at[me.c], local)
    keep.start()
    for copy in w_back:
        copy.wait_recv()
    swap.wait_recv()
    keep.wait()
    for copy in list(x_first.values()) + list(z_first.values()) + list(z_second.values()):
        copy.wait_send()
    for copy in [x_second, w_x, swap] + w_y + w_z + w_back:
        copy.wait_send()


def settle(dense, ball, gwx):
    half = (256, 256)
    return pl.pallas_call(
        settle_kernel,
        out_shape=(
            jax.ShapeDtypeStruct((2, 512, 128), F32),
            jax.ShapeDtypeStruct((4, 40, 512), F32),
        ),
        in_specs=[VMEM] * 3,
        out_specs=(VMEM, VMEM),
        scratch_shapes=[
            pltpu.VMEM((512, 1024), BF16),
            pltpu.VMEM((512, 1024), BF16),
            pltpu.VMEM((512, 256), F32),
            pltpu.VMEM((8, 2) + half, BF16),
            pltpu.VMEM((2, 3) + half, BF16),
            pltpu.VMEM(half, BF16),
            pltpu.VMEM(half, BF16),
            pltpu.VMEM((4,) + half, BF16),
            pltpu.VMEM((3,) + half, BF16),
            pltpu.VMEM((3,) + half, BF16),
            pltpu.VMEM((2, 512, 128), F32),
            pltpu.VMEM((4, 40, 512), F32),
            pltpu.VMEM((4, 40, 512), F32),
            pltpu.VMEM((40, 512), F32),
            pltpu.VMEM((40, 512), F32),
            DMA((25,)),
            DMA((25,)),
            DMA,
        ],
        compiler_params=pltpu.CompilerParams(
            collective_id=2, has_side_effects=True, vmem_limit_bytes=36 * MIB
        ),
        name="settle",
    )(dense, ball, gwx)


def body(features, weight, bias_vector, cotangent, tile_masks, tile_rows, tile_counts):
    masks = tile_masks.reshape(8, 4, 2, 16, 16, 128)
    dense, row, col, g, wc, cotr = spread(
        tile_rows[0].T, tile_counts.reshape(256), masks, features, weight, cotangent
    )
    act, ball, gwx = layer(dense, g.reshape(8, 256, 512), row, col, wc, bias_vector.reshape(1, 512), cotr)
    out, gw = settle(dense, ball.reshape(4, 1024, 256), gwx)
    out = out.reshape(8, 8, 16, 128).transpose(0, 2, 1, 3).reshape(1024, 128) * col
    return act, out, gw[:, :32].reshape(128, 512), gw[0, 32]


def solution(mesh):
    return jax.shard_map(
        body,
        mesh=mesh,
        in_specs=(
            P("blk", "rep"),
            P("rep", None),
            P(),
            P("blk", "rep"),
            P("blk", None, None, None, None),
            P("blk", None, None),
            P("blk", None),
        ),
        out_specs=(P("blk", "rep"), P("blk", "rep"), P("rep", None), P()),
        check_vma=False,
    )
```

```python
import functools

import jax
import jax.numpy as jnp
from jax import lax
from jax.experimental import pallas as pl
from jax.experimental.pallas import tpu as pltpu
from jax.sharding import PartitionSpec as P

MESH = pl.DeviceIdType.MESH
BF16 = jnp.bfloat16
F32 = jnp.float32
HBM = pl.BlockSpec(memory_space=pltpu.HBM)
DMA = pltpu.SemaphoreType.DMA
MIB = 2**20
VMEM_MIB = 60


class Place:
    def __init__(self):
        blk = lax.axis_index("blk")
        rep = lax.axis_index("rep")
        self.x, self.z, self.y = blk // 16, lax.rem(blk // 4, 4), lax.rem(blk, 4)
        self.xl, self.c = rep // 2, lax.rem(rep, 2)
        self.rep = rep
        self.xz = self.x * 4 + self.z

    def at(self, x=None, z=None, y=None, xl=None, c=None):
        x = self.x if x is None else x
        z = self.z if z is None else z
        y = self.y if y is None else y
        xl = self.xl if xl is None else xl
        c = self.c if c is None else c
        return (x * 16 + z * 4 + y, xl * 2 + c)

    def dy(self, n):
        return lax.rem(self.y + n, 4)

    def dz(self, n):
        return lax.rem(self.z + n, 4)


class Copies:
    def __init__(self, send, recv):
        self.send, self.recv, self.used = send, recv, []

    def start(self, src, dst, peer):
        n = len(self.used)
        copy = pltpu.make_async_remote_copy(
            src_ref=src, dst_ref=dst, send_sem=self.send.at[n], recv_sem=self.recv.at[n],
            device_id=peer, device_id_type=MESH,
        )
        copy.start()
        self.used.append(copy)
        return copy

    def wait_sends(self):
        for copy in self.used:
            copy.wait_send()


Y_ORDER = (2, 1, 3, 0)


def spread(me, rows_hbm, counts_hbm, masks, feat_hbm, w, bias_hbm, cot, dense, row, col, g, wc, cotr, bias,
           rows_ref, counts_ref, feat, words, m16, rm, slots_s, slots_v, landed_v, landed_s, xt, send, recv, load, local):
    own, other = me.c, 1 - me.c
    small = [
        pltpu.make_async_copy(rows_hbm, rows_ref, local.at[6]),
        pltpu.make_async_copy(counts_hbm, counts_ref, local.at[7]),
    ]
    for copy in small:
        copy.start()
    loads = []
    for q in range(8):
        half = own if q < 4 else other
        loads.append(pltpu.make_async_copy(masks.at[:, me.dy(Y_ORDER[q % 4]), half], words.at[q], load.at[q]))
        loads[q].start()
    feat_load = pltpu.make_async_copy(feat_hbm, feat, local.at[8])
    feat_load.start()

    sibling = me.at(c=1 - me.c)
    x_peer = me.at(x=1 - me.x)
    z_peers = [me.at(z=me.dz(n)) for n in (1, 2, 3)]
    y_peers = [me.at(y=me.dy(n)) for n in (1, 2, 3)]
    rep_peers = [sibling, me.at(xl=1 - me.xl), me.at(xl=1 - me.xl, c=1 - me.c)]
    everyone = z_peers + y_peers + rep_peers + [x_peer]
    barrier = pltpu.get_barrier_semaphore()
    for peer in everyone:
        pl.semaphore_signal(barrier, inc=1, device_id=peer, device_id_type=MESH)

    def narrow(q):
        loads[q].wait()

        def tiles(xz, _):
            for slot in range(16):
                tile = words[q, xz, slot].astype(jnp.int16)
                if q < 3:
                    m16[q, xz, slot] = tile
                else:
                    rm[me.y, xz, slot] = tile
            return 0

        lax.fori_loop(0, 8, tiles, 0)

    narrow(0)
    pl.semaphore_wait(barrier, len(everyone))
    copies = Copies(send, recv)

    def cot_rows(rep):
        return cot.at[pl.ds(pl.multiple_of(rep * 256, 256), 256), :]

    mask_copies = []
    for q in range(3):
        if q:
            narrow(q)
        mask_copies.append(copies.start(m16.at[q], rm.at[me.y], y_peers[Y_ORDER[q] - 1]))
    early = []
    for peer in rep_peers:
        early.append(copies.start(cot_rows(peer[1]), cotr.at[me.rep], peer))
        early.append(copies.start(w, wc.at[me.rep], peer))
    narrow(3)
    for copy in small:
        copy.wait()
    tile_row = lax.broadcasted_iota(jnp.int32, (8, 128), 0)

    def scan(q, degrees):
        n = Y_ORDER[q % 4]
        half = own if q < 4 else other
        if q >= 4:
            loads[q].wait()

        def tiles(xz, degrees):
            first = ((xz * 4 + me.dy(n)) * 2 + half) * 4
            for tc in range(4):
                count = counts_ref[0, first + tc]
                for s in range(4):
                    slot = tc * 4 + s
                    t = jnp.where(s < count, rows_ref[s, first + tc], 8)
                    tile = words[q, xz, slot]
                    if q < 4:
                        slots_s[q, 0, xz * 16 + slot] = t
                    joined = jnp.bitwise_or(tile[:8], jnp.left_shift(tile[8:], 8))
                    counted = jnp.sum(lax.population_count(joined), axis=0, keepdims=True)
                    degrees = degrees + jnp.where(tile_row == t, counted, 0)
            return degrees

        return lax.fori_loop(0, 8, tiles, degrees)

    degrees = jnp.zeros((8, 128), jnp.int32)
    for q in range(8):
        degrees = scan(q, degrees)

    inv = lax.rsqrt(1.0 + degrees.astype(F32))
    place = lax.broadcasted_iota(jnp.int32, (128, 128), 1)
    source = 8 * jnp.bitwise_and(place, 15) + jnp.right_shift(place, 4)
    perm = jnp.where(lax.broadcasted_iota(jnp.int32, (128, 128), 0) == source, 1.0, 0.0).astype(BF16)
    feat_load.wait()
    for t in range(8):
        lanes = inv[t:t + 1, :]
        row[:, t * 128:(t + 1) * 128] = jnp.broadcast_to(lanes, (8, 128))
        spread = jnp.broadcast_to(lanes, (128, 128))
        col[t * 128:(t + 1) * 128, :] = spread.T
        scaled = (feat[t * 128:(t + 1) * 128, :].astype(F32).T * spread).astype(BF16)
        moved = jnp.dot(scaled, perm, preferred_element_type=F32).astype(BF16)
        xt[t // 4, :, (t % 4) * 128:(t % 4 + 1) * 128] = moved

    def at(core, xz):
        return g.at[xz, core]

    to_sibling = copies.start(xt.at[other], at(own, me.xz), sibling)
    first = [copies.start(xt.at[own], at(own, me.xz), p) for p in z_peers]
    across = copies.start(xt.at[own], at(own, me.xz), x_peer)
    stays = [
        pltpu.make_async_copy(xt.at[own], at(own, me.xz), local.at[0]),
        pltpu.make_async_copy(w, wc.at[me.rep], local.at[1]),
        pltpu.make_async_copy(cot_rows(me.rep), cotr.at[me.rep], local.at[5]),
        pltpu.make_async_copy(bias_hbm, bias, local.at[9]),
    ]
    for copy in stays:
        copy.start()
    to_vmem = pltpu.make_async_copy(slots_s, slots_v, local.at[2])
    to_vmem.start()
    to_vmem.wait()
    slot_copies = [copies.start(slots_v.at[q], landed_v.at[me.y], y_peers[Y_ORDER[q] - 1]) for q in range(3)]
    kept = pltpu.make_async_copy(slots_v.at[3], landed_v.at[me.y], local.at[3])
    kept.start()

    to_sibling.wait_recv()
    other_x = copies.start(at(other, me.xz), at(other, me.xz), x_peer)
    second = [copies.start(at(other, me.xz), at(other, me.xz), p) for p in z_peers]

    def put_tiles(n, slot_rows, at):
        i = me.dy(n)

        def column(j, _):
            for tc in range(4):
                rows = [slot_rows[at, 0, j * 16 + tc * 4 + s] for s in range(4)]
                tiles = [rm[i, j, tc * 4 + s] for s in range(4)]
                for t in range(8):
                    found = jnp.zeros((16, 128), jnp.int16)
                    for s in range(4):
                        found = jnp.where(rows[s] == t, tiles[s], found)
                    dense[i * 8 + j, tc, t] = found
            return 0

        lax.fori_loop(0, 8, column, 0)

    last = []
    for n in (1, 2, 3):
        first[n - 1].wait_recv()
        source = me.x * 4 + me.dz(4 - n)
        last.append(copies.start(at(own, source), at(own, source), x_peer))
    other_x.wait_recv()
    far = (1 - me.x) * 4 + me.z
    last += [copies.start(at(other, far), at(other, far), p) for p in z_peers]
    put_tiles(0, slots_s, 3)
    kept.wait()
    for copy in slot_copies:
        copy.wait_recv()
    to_smem = pltpu.make_async_copy(landed_v, landed_s, local.at[4])
    to_smem.start()
    to_smem.wait()
    for q in range(3):
        mask_copies[q].wait_recv()
        put_tiles(4 - Y_ORDER[q], landed_s, me.dy(4 - Y_ORDER[q]))
    for copy in [across] + second + last:
        copy.wait_recv()
    stays[0].wait()

    def parameters():
        for copy in early:
            copy.wait_recv()
        for copy in stays[1:]:
            copy.wait()

    return parameters, copies.wait_sends


def table(values, step):
    found = values[-1]
    for n in range(len(values) - 1):
        found = jnp.where(step == n, values[n], found)
    return found


def unpack(dense, i, j, out_ref):
    one, zero = jnp.asarray(1, BF16), jnp.asarray(0, BF16)
    for tc in range(4):
        for t in range(8):
            words = dense[i * 8 + j, tc, t]
            for k in range(8):
                bits = jnp.where(jnp.bitwise_and(words, jnp.int16(1 << k)) != 0, one, zero)
                first = tc * 128 + k * 16
                out_ref[first:first + 16, t * 128:(t + 1) * 128] = bits


def layer(me, parameters, dense, g, row, col, wc, bias, cotr, act, ball, gwx, a0, a1,
          acc, part, rc, snd, ry, agg_s, agg, agg_t, slope, act_s, back_s,
          core_s, core_r, sum_s, sum_r, send, recv, local):
    sibling = me.at(c=1 - me.c)
    xl_peer = me.at(xl=1 - me.xl)
    xl_other = me.at(xl=1 - me.xl, c=1 - me.c)
    y_peers = [me.at(y=me.dy(n)) for n in (1, 2, 3)]
    copies = Copies(send, recv)
    own, other = me.c, 1 - me.c

    def to_sibling(s):
        return pltpu.make_async_remote_copy(
            src_ref=part.at[s, other], dst_ref=rc.at[s], send_sem=core_s.at[s], recv_sem=core_r.at[s],
            device_id=sibling, device_id_type=MESH,
        )

    def rows_of(m):
        return pl.ds(pl.multiple_of(m * 256, 256), 256)

    def to_owner(k, m):
        return pltpu.make_async_remote_copy(
            src_ref=snd.at[k, m], dst_ref=ry.at[k, m], send_sem=sum_s.at[k * 4 + m], recv_sem=sum_r.at[k * 4 + m],
            device_id=me.at(y=me.dy(table((2, 1, 3), k))), device_id_type=MESH,
        )

    def pass_on(k):
        to_sibling(k).wait_recv()
        for m in range(4):
            rows = slice(m * 256, (m + 1) * 256)
            snd[k, m] = (part[k, own, :, rows].astype(F32) + rc[k, :, rows].astype(F32)).astype(BF16)
            to_owner(k, m).start()

    def chunk(c):
        return me.dy(table((2, 1, 3, 0), c // 8)), lax.rem(c, 8)

    bufs = (a0, a1)
    unpack(dense, *chunk(0), a0)

    def two_chunks(n, _):
        k, pair = n // 4, lax.rem(n, 4)
        for h in range(2):
            unpack(dense, *chunk(jnp.minimum(n * 2 + h + 1, 31)), bufs[1 - h])
            prod = jnp.dot(g[pair * 2 + h].reshape(256, 512), bufs[h][...], preferred_element_type=F32)
            if h == 0:
                acc[...] = jnp.where(pair == 0, 0.0, acc[...]) + prod
            else:
                acc[...] += prod

        @pl.when(pair == 3)
        def _():
            part[k, 0] = acc[0:128].astype(BF16)
            part[k, 1] = acc[128:256].astype(BF16)
            to_sibling(k).start()

        @pl.when(jnp.logical_and(pair == 0, k >= 1))
        def _():
            pass_on(k - 1)

        return 0

    lax.fori_loop(0, 16, two_chunks, 0)
    to_sibling(3).wait_recv()

    def finish_sum(m, out):
        for k in range(3):
            to_owner(k, m).wait_recv()
        rows = rows_of(m)
        total = part[3, own, :, rows].astype(F32) + rc[3, :, rows].astype(F32)
        for k in range(3):
            total = total + ry[k, m].astype(F32)
        total = total * row[0:1, rows]
        agg_t[:, rows] = total.astype(BF16)
        out[...] = total.T.astype(BF16)

    swaps = []
    peers = (xl_peer, xl_other, sibling)
    for n in range(3):
        finish_sum(peers[n][1], agg_s.at[n])
        swaps.append(copies.start(agg_s.at[n], agg.at[me.rep], peers[n]))
    finish_sum(me.rep, agg.at[me.rep])
    parameters()
    for copy in reversed(swaps):
        copy.wait_recv()

    for half in range(2):
        rows = slice(half * 128, (half + 1) * 128)
        hidden = jnp.dot(agg[0, rows, :], wc[0], preferred_element_type=F32)
        for q in range(1, 4):
            hidden = hidden + jnp.dot(agg[q, rows, :], wc[q], preferred_element_type=F32)
        hidden = hidden + bias[...]
        logistic = jax.nn.sigmoid(hidden)
        value = hidden * logistic
        factor = logistic * (1.0 + hidden * (1.0 - logistic))
        for q in range(4):
            lanes = slice(q * 128, (q + 1) * 128)
            act_s[q, rows, :] = value[:, lanes]
            slope[me.rep, rows, lanes] = (cotr[q, rows, :].astype(F32) * factor[:, lanes]).astype(BF16)

    def block(y, rep):
        return ball.at[pl.ds(pl.multiple_of(y * 1024 + rep * 256, 256), 256), :]

    def back_into(xl, out):
        for core in range(2):
            value = lax.dot_general(
                slope[me.rep], wc[xl * 2 + core], (((1,), (1,)), ((), ())), preferred_element_type=F32
            )
            out[:, core * 128:(core + 1) * 128] = (value * col[rows_of(me.rep), :]).astype(BF16)

    theirs = (1 - me.xl) * 2 + me.c
    back_into(1 - me.xl, back_s)
    from_xl = copies.start(back_s, block(me.y, me.rep), xl_peer)
    back_into(me.xl, block(me.y, me.rep))

    def send_block(rep):
        here = block(me.y, rep)
        return [copies.start(here, here, y_peers[n - 1]) for n in (2, 1, 3)] + [copies.start(here, here, sibling)]

    mine = send_block(me.rep)
    slope_far = copies.start(slope.at[me.rep], slope.at[me.rep], xl_peer)
    slope_near = copies.start(slope.at[me.rep], slope.at[me.rep], sibling)
    from_xl.wait_recv()
    passed = send_block(theirs)
    acts = [
        copies.start(act_s.at[peer[1]], act.at[rows_of(me.rep), :], peer)
        for peer in (xl_peer, xl_other, sibling)
    ]
    act_kept = pltpu.make_async_copy(act_s.at[me.rep], act.at[rows_of(me.rep), :], local)
    act_kept.start()
    slope_far.wait_recv()
    slope_relay = copies.start(slope.at[theirs], slope.at[theirs], sibling)

    relays = []
    for sent, rep in ((mine, me.rep), (passed, theirs)):
        if rep is theirs:
            slope_near.wait_recv()
            slope_relay.wait_recv()
            ones = jnp.ones((8, 256), BF16)
            grad = jnp.zeros((128, 512), F32)
            gb = jnp.zeros((8, 512), F32)
            for q in range(4):
                grad = grad + jnp.dot(agg_t[:, q * 256:(q + 1) * 256], slope[q], preferred_element_type=F32)
                gb = gb + jnp.dot(ones, slope[q], preferred_element_type=F32)
            for n in range(4):
                gwx[n, 0:32, :] = grad[n * 32:(n + 1) * 32]
                gwx[n, 32:40, :] = gb
        for n, copy in zip((2, 1, 3), sent):
            copy.wait_recv()
            here = block(me.dy(4 - n), rep)
            relays.append(copies.start(here, here, sibling))
    for copy in [mine[3], passed[3]] + relays:
        copy.wait_recv()

    def finish():
        for copy in acts:
            copy.wait_recv()
        act_kept.wait()
        copies.wait_sends()
        for k in range(3):
            for m in range(4):
                to_owner(k, m).wait_send()
        for k in range(4):
            to_sibling(k).wait_send()

    return finish


BLOCKS = ((1, 2), (1, 1), (1, 3), (1, 0), (0, 2), (0, 1), (0, 3), (0, 0))
ORDER = {key: n for n, key in enumerate(BLOCKS)}


def settle(me, dense, col, ball, gwx, out, gw, a0, a1,
           acc, part, az, a_sum, ax, bx, b_sum, bz, hold, final, wy, wz, wx_send, wx, gw_own, send, recv, local):
    sibling = me.at(c=1 - me.c)
    x_peer = me.at(x=1 - me.x)
    z_peers = [me.at(z=me.dz(n)) for n in (1, 2, 3)]
    y_peers = [me.at(y=me.dy(n)) for n in (1, 2, 3)]

    def remote(n, src, dst, peer):
        return pltpu.make_async_remote_copy(
            src_ref=src, dst_ref=dst, send_sem=send.at[n], recv_sem=recv.at[n],
            device_id=peer, device_id_type=MESH,
        )

    x_first = {n: remote(n, part.at[ORDER[1, n], 1], bx.at[n], x_peer) for n in range(4)}
    z_first = {
        (side, n): remote(4 + side * 3 + n - 1, part.at[ORDER[side, n], 0], az.at[side, n - 1], z_peers[n - 1])
        for side in range(2) for n in (1, 2, 3)
    }
    z_second = {n: remote(9 + n, b_sum.at[n - 1], bz.at[n - 1], z_peers[n - 1]) for n in (1, 2, 3)}
    x_second = remote(13, a_sum, ax, x_peer)
    w_y = [remote(13 + n, gwx.at[me.dy(n)], wy.at[me.y], y_peers[n - 1]) for n in (1, 2, 3)]
    w_z = [remote(16 + n, wz.at[me.z], wz.at[me.z], z_peers[n - 1]) for n in (1, 2, 3)]
    w_x = remote(20, wx_send, wx, x_peer)
    w_back = [remote(20 + n, gw_own, gw.at[me.y], y_peers[n - 1]) for n in (1, 2, 3)]
    w_kept = pltpu.make_async_copy(gw_own, gw.at[me.y], local.at[0])

    def pass_b(n):
        x_first[n].wait_recv()
        b_sum[n - 1] = (part[ORDER[0, n], 1].astype(F32) + bx[n].astype(F32)).astype(BF16)
        z_second[n].start()

    def pass_a():
        total = part[ORDER[1, 0], 0].astype(F32)
        for n in (1, 2, 3):
            z_first[1, n].wait_recv()
            total = total + az[1, n - 1].astype(F32)
        a_sum[...] = total.astype(BF16)
        x_second.start()

    def weights_z():
        for copy in w_y:
            copy.wait_recv()
        wz[me.z] = (wy[0] + wy[1]) + (wy[2] + wy[3])
        for copy in w_z:
            copy.start()

    def weights_x():
        for copy in w_z:
            copy.wait_recv()
        wx_send[...] = (wz[0] + wz[1]) + (wz[2] + wz[3])
        w_x.start()

    def weights_back():
        w_x.wait_recv()
        gw_own[...] = wx_send[...] + wx[...]
        w_kept.start()
        for copy in w_back:
            copy.start()

    actions = {n: [] for n in range(8)}
    for n in range(4):
        actions[ORDER[1, n]].append(x_first[n].start)
    for n in (2, 1, 3):
        actions[ORDER[0, n]].append(functools.partial(pass_b, n))
    for key, copy in z_first.items():
        actions[ORDER[key]].append(copy.start)
    actions[3].append(weights_z)
    actions[4].append(pass_a)
    actions[5].append(weights_x)
    actions[6].append(weights_back)

    for copy in w_y:
        copy.start()
    wy[me.y] = gwx[me.y]

    def chunk(c):
        at = c // 4
        x = lax.rem(me.x + table([block[0] for block in BLOCKS], at), 2)
        z = lax.rem(me.z + table([block[1] for block in BLOCKS], at), 4)
        return lax.rem(c, 4), x * 4 + z

    bufs = (a0, a1)
    unpack(dense, *chunk(0), a0)

    def two_chunks(step, _):
        block, pair = step // 2, lax.rem(step, 2)
        for h in range(2):
            unpack(dense, *chunk(jnp.minimum(step * 2 + h + 1, 31)), bufs[1 - h])
            prod = jnp.dot(bufs[h][...], ball[pl.ds(pl.multiple_of((pair * 2 + h) * 1024, 1024), 1024), :], preferred_element_type=F32)
            if h == 0:
                acc[...] = jnp.where(pair == 0, 0.0, acc[...]) + prod
            else:
                acc[...] += prod

        @pl.when(pair == 1)
        def _():
            part[block, 0] = acc[0:256].astype(BF16)
            part[block, 1] = acc[256:512].astype(BF16)

        for at, calls in actions.items():
            if calls:
                @pl.when(step == at * 2 + 1)
                def _():
                    for call in calls:
                        call()

        return 0

    lax.fori_loop(0, 16, two_chunks, 0)

    def place(tile, total):
        here = slice(tile * 128, tile * 128 + 256)
        for q in range(2):
            hold[q * 512 + tile * 128:q * 512 + tile * 128 + 256, :] = total[:, q * 128:(q + 1) * 128]
        for t in range(tile, tile + 2):
            for w in range(16):
                first = t * 128 + w * 8
                scale = col[pl.ds(pl.multiple_of(me.c * 512 + first, 8), 8), :]
                for q in range(2):
                    final[q, first:first + 8, :] = hold[pl.ds(q * 512 + t * 128 + w, 8, stride=16), :] * scale
        at = tile // 2
        swap = remote(24 + at, final.at[1 - me.c, here], out.at[me.c, here], sibling)
        keep = pltpu.make_async_copy(final.at[me.c, here], out.at[me.c, here], local.at[1 + at])
        swap.start()
        keep.start()
        return swap, keep

    total = part[ORDER[0, 0], 1].astype(F32)
    x_first[0].wait_recv()
    total = total + bx[0].astype(F32)
    for n in (1, 2, 3):
        z_second[n].wait_recv()
        total = total + bz[n - 1].astype(F32)
    swaps = [place(2, total)]
    total = part[ORDER[0, 0], 0].astype(F32)
    for n in (1, 2, 3):
        z_first[0, n].wait_recv()
        total = total + az[0, n - 1].astype(F32)
    x_second.wait_recv()
    total = total + ax[...].astype(F32)
    swaps.append(place(0, total))
    for copy in w_back:
        copy.wait_recv()
    for swap, keep in swaps:
        swap.wait_recv()
        keep.wait()
    w_kept.wait()
    for copy in list(x_first.values()) + list(z_first.values()) + list(z_second.values()):
        copy.wait_send()
    for copy in [x_second, w_x] + [swap for swap, _ in swaps] + w_y + w_z + w_back:
        copy.wait_send()


HALF = (256, 256)
HELD = (
    pltpu.VMEM((32, 4, 8, 16, 128), jnp.int16),
    pltpu.VMEM((8, 1024), F32),
    pltpu.VMEM((1024, 128), F32),
    pltpu.VMEM((8, 2, 128, 512), BF16),
    pltpu.VMEM((4, 128, 512), BF16),
    pltpu.VMEM((4, 256, 128), BF16),
    pltpu.VMEM((1, 512), F32),
    pltpu.VMEM((4096, 256), BF16),
    pltpu.VMEM((4, 40, 512), F32),
    pltpu.VMEM((512, 1024), BF16),
    pltpu.VMEM((512, 1024), BF16),
)
SPREAD = (
    pltpu.SMEM((4, 256), jnp.int32),
    pltpu.SMEM((1, 256), jnp.int32),
    pltpu.VMEM((1024, 128), BF16),
    pltpu.VMEM((8, 8, 16, 16, 128), jnp.int32),
    pltpu.VMEM((3, 8, 16, 16, 128), jnp.int16),
    pltpu.VMEM((4, 8, 16, 16, 128), jnp.int16),
    pltpu.SMEM((4, 1, 128), jnp.int32),
    pltpu.VMEM((4, 1, 128), jnp.int32),
    pltpu.VMEM((4, 1, 128), jnp.int32),
    pltpu.SMEM((4, 1, 128), jnp.int32),
    pltpu.VMEM((2, 128, 512), BF16),
    DMA((27,)),
    DMA((27,)),
    DMA((8,)),
    DMA((10,)),
)
LAYER = (
    pltpu.VMEM((256, 1024), F32),
    pltpu.VMEM((4, 2, 128, 1024), BF16),
    pltpu.VMEM((4, 128, 1024), BF16),
    pltpu.VMEM((3, 4, 128, 256), BF16),
    pltpu.VMEM((3, 4, 128, 256), BF16),
    pltpu.VMEM((3, 256, 128), BF16),
    pltpu.VMEM((4, 256, 128), BF16),
    pltpu.VMEM((128, 1024), BF16),
    pltpu.VMEM((4, 256, 512), BF16),
    pltpu.VMEM((4, 256, 128), F32),
    pltpu.VMEM((256, 256), BF16),
    DMA((4,)),
    DMA((4,)),
    DMA((12,)),
    DMA((12,)),
    DMA((24,)),
    DMA((24,)),
    DMA,
)
SETTLE = (
    pltpu.VMEM((512, 256), F32),
    pltpu.VMEM((8, 2) + HALF, BF16),
    pltpu.VMEM((2, 3) + HALF, BF16),
    pltpu.VMEM(HALF, BF16),
    pltpu.VMEM(HALF, BF16),
    pltpu.VMEM((4,) + HALF, BF16),
    pltpu.VMEM((3,) + HALF, BF16),
    pltpu.VMEM((3,) + HALF, BF16),
    pltpu.VMEM((1024, 128), F32),
    pltpu.VMEM((2, 512, 128), F32),
    pltpu.VMEM((4, 40, 512), F32),
    pltpu.VMEM((4, 40, 512), F32),
    pltpu.VMEM((40, 512), F32),
    pltpu.VMEM((40, 512), F32),
    pltpu.VMEM((40, 512), F32),
    DMA((26,)),
    DMA((26,)),
    DMA((3,)),
)


def all_kernel(*refs):
    groups, first = [], 0
    for size in (7, 3, len(HELD), len(SPREAD), len(LAYER), len(SETTLE)):
        groups.append(refs[first:first + size])
        first += size
    ins, (act, out, gw), held, spread_refs, layer_refs, settle_refs = groups
    dense, row, col, g, wc, cotr, bias, ball, gwx, a0, a1 = held
    me = Place()
    parameters, finish_spread = spread(me, *ins, dense, row, col, g, wc, cotr, bias, *spread_refs)
    finish_layer = layer(
        me, parameters, dense, g, row, col, wc, bias, cotr, act, ball, gwx, a0, a1, *layer_refs
    )
    settle(me, dense, col, ball, gwx, out, gw, a0, a1, *settle_refs)
    finish_layer()
    finish_spread()


def results_kernel(act, out, gw, act_out, feat_out, gw_out, gb_out, act_v, feat_v, gw_v, load, store):
    loads = [pltpu.make_async_copy(gw, gw_v, load.at[0])]
    for n in range(2):
        here = slice(n * 512, n * 512 + 512)
        loads.append(pltpu.make_async_copy(act.at[here], act_v.at[here], load.at[1 + n]))
        loads.append(pltpu.make_async_copy(out.at[here], feat_v.at[here], load.at[3 + n]))
    for copy in loads:
        copy.start()
    loads[0].wait()
    stores = [
        pltpu.make_async_copy(gw_v.at[:, 0:32], gw_out, store.at[0]),
        pltpu.make_async_copy(gw_v.at[0, 32:33], gb_out, store.at[1]),
    ]
    for copy in stores:
        copy.start()
    for n in range(2):
        here = slice(n * 512, n * 512 + 512)
        loads[1 + 2 * n].wait()
        stores.append(pltpu.make_async_copy(act_v.at[here], act_out.at[here], store.at[2 + n]))
        stores[-1].start()
        loads[2 + 2 * n].wait()
        stores.append(pltpu.make_async_copy(feat_v.at[here], feat_out.at[here], store.at[4 + n]))
        stores[-1].start()
    for copy in stores:
        copy.wait()


def body(features, weight, bias_vector, cotangent, tile_masks, tile_rows, tile_counts):
    masks = tile_masks.reshape(8, 4, 2, 16, 16, 128)
    act, out, gw = pl.pallas_call(
        all_kernel,
        out_shape=(
            jax.ShapeDtypeStruct((1024, 128), F32),
            jax.ShapeDtypeStruct((2, 512, 128), F32),
            jax.ShapeDtypeStruct((4, 40, 512), F32),
        ),
        in_specs=[HBM] * 7,
        out_specs=(HBM,) * 3,
        scratch_shapes=HELD + SPREAD + LAYER + SETTLE,
        compiler_params=pltpu.CompilerParams(
            collective_id=0, has_side_effects=True, vmem_limit_bytes=VMEM_MIB * MIB
        ),
        name="layer",
    )(tile_rows[0].T, tile_counts, masks, features, weight, bias_vector.reshape(1, 512), cotangent)
    act, out, gw, gb = pl.pallas_call(
        results_kernel,
        out_shape=(
            jax.ShapeDtypeStruct((1024, 128), F32),
            jax.ShapeDtypeStruct((1024, 128), F32),
            jax.ShapeDtypeStruct((4, 32, 512), F32),
            jax.ShapeDtypeStruct((1, 512), F32),
        ),
        in_specs=[HBM] * 3,
        out_specs=(HBM,) * 4,
        scratch_shapes=[
            pltpu.VMEM((1024, 128), F32),
            pltpu.VMEM((1024, 128), F32),
            pltpu.VMEM((4, 40, 512), F32),
            DMA((5,)),
            DMA((6,)),
        ],
        compiler_params=pltpu.CompilerParams(vmem_limit_bytes=VMEM_MIB * MIB),
        name="results",
    )(act, out.reshape(1024, 128), gw)
    return act, out, gw.reshape(128, 512), gb.reshape(512)


def solution(mesh):
    return jax.shard_map(
        body,
        mesh=mesh,
        in_specs=(
            P("blk", "rep"),
            P("rep", None),
            P(),
            P("blk", "rep"),
            P("blk", None, None, None, None),
            P("blk", None, None),
            P("blk", None),
        ),
        out_specs=(P("blk", "rep"), P("blk", "rep"), P("rep", None), P()),
        check_vma=False,
    )
```

```python
import functools

import jax
import jax.numpy as jnp
from jax import lax
from jax.experimental import pallas as pl
from jax.experimental.pallas import tpu as pltpu
from jax.sharding import PartitionSpec as P

MESH = pl.DeviceIdType.MESH
BF16 = jnp.bfloat16
F32 = jnp.float32
HBM = pl.BlockSpec(memory_space=pltpu.HBM)
DMA = pltpu.SemaphoreType.DMA
MIB = 2**20
VMEM_MIB = 60


class Place:
    def __init__(self):
        blk = lax.axis_index("blk")
        rep = lax.axis_index("rep")
        self.x, self.z, self.y = blk // 16, lax.rem(blk // 4, 4), lax.rem(blk, 4)
        self.xl, self.c = rep // 2, lax.rem(rep, 2)
        self.rep = rep
        self.xz = self.x * 4 + self.z

    def at(self, x=None, z=None, y=None, xl=None, c=None):
        x = self.x if x is None else x
        z = self.z if z is None else z
        y = self.y if y is None else y
        xl = self.xl if xl is None else xl
        c = self.c if c is None else c
        return (x * 16 + z * 4 + y, xl * 2 + c)

    def dy(self, n):
        return lax.rem(self.y + n, 4)

    def dz(self, n):
        return lax.rem(self.z + n, 4)

    def column(self, n):
        return lax.rem(self.x + n // 4, 2) * 4 + self.dz(4 - lax.rem(n, 4))


class Copies:
    def __init__(self, send, recv):
        self.send, self.recv, self.used = send, recv, []

    def start(self, src, dst, peer):
        n = len(self.used)
        copy = pltpu.make_async_remote_copy(
            src_ref=src, dst_ref=dst, send_sem=self.send.at[n], recv_sem=self.recv.at[n],
            device_id=peer, device_id_type=MESH,
        )
        copy.start()
        self.used.append(copy)
        return copy

    def wait_sends(self):
        for copy in self.used:
            copy.wait_send()


Y_ORDER = (2, 1, 3, 0)
ROWS = (0, 2, 1, 3)


def spread(me, rows_hbm, counts_hbm, masks, feat_hbm, w, bias_hbm, cot, dense, row, col, g, wc, cotr, bias,
           rows_ref, counts_ref, feat, words, m16, rm, slots_s, slots_v, landed_v, landed_s, xt, send, recv, load, local):
    own, other = me.c, 1 - me.c
    small = [
        pltpu.make_async_copy(rows_hbm, rows_ref, local.at[6]),
        pltpu.make_async_copy(counts_hbm, counts_ref, local.at[7]),
    ]
    for copy in small:
        copy.start()
    loads = []
    for q in range(8):
        half = own if q < 4 else other
        loads.append(pltpu.make_async_copy(masks.at[:, me.dy(Y_ORDER[q % 4]), half], words.at[q], load.at[q]))
        loads[q].start()
    feat_load = pltpu.make_async_copy(feat_hbm, feat, local.at[8])
    feat_load.start()

    sibling = me.at(c=1 - me.c)
    x_peer = me.at(x=1 - me.x)
    z_peers = [me.at(z=me.dz(n)) for n in (1, 2, 3)]
    y_peers = [me.at(y=me.dy(n)) for n in (1, 2, 3)]
    rep_peers = [sibling, me.at(xl=1 - me.xl), me.at(xl=1 - me.xl, c=1 - me.c)]
    everyone = z_peers + y_peers + rep_peers + [x_peer]
    barrier = pltpu.get_barrier_semaphore()
    for peer in everyone:
        pl.semaphore_signal(barrier, inc=1, device_id=peer, device_id_type=MESH)

    def narrow(q):
        loads[q].wait()

        def tiles(xz, _):
            for slot in range(16):
                tile = words[q, xz, slot].astype(jnp.int16)
                if q < 3:
                    m16[q, xz, slot] = tile
                else:
                    rm[me.y, xz, slot] = tile
            return 0

        lax.fori_loop(0, 8, tiles, 0)

    narrow(0)
    pl.semaphore_wait(barrier, len(everyone))
    copies = Copies(send, recv)

    def cot_rows(rep):
        return cot.at[pl.ds(pl.multiple_of(rep * 256, 256), 256), :]

    mask_copies = []
    for q in range(3):
        if q:
            narrow(q)
        mask_copies.append(copies.start(m16.at[q], rm.at[me.y], y_peers[Y_ORDER[q] - 1]))
    early = []
    for peer in rep_peers:
        early.append(copies.start(cot_rows(peer[1]), cotr.at[me.rep], peer))
        early.append(copies.start(w, wc.at[me.rep], peer))
    narrow(3)
    for copy in small:
        copy.wait()
    tile_row = lax.broadcasted_iota(jnp.int32, (8, 128), 0)

    def scan(q, degrees):
        n = Y_ORDER[q % 4]
        half = own if q < 4 else other
        if q >= 4:
            loads[q].wait()

        def tiles(xz, degrees):
            first = ((xz * 4 + me.dy(n)) * 2 + half) * 4
            for tc in range(4):
                count = counts_ref[0, first + tc]
                for s in range(4):
                    slot = tc * 4 + s
                    t = jnp.where(s < count, rows_ref[s, first + tc], 8)
                    tile = words[q, xz, slot]
                    if q < 4:
                        slots_s[q, 0, xz * 16 + slot] = t
                    joined = jnp.bitwise_or(tile[:8], jnp.left_shift(tile[8:], 8))
                    counted = jnp.sum(lax.population_count(joined), axis=0, keepdims=True)
                    degrees = degrees + jnp.where(tile_row == t, counted, 0)
            return degrees

        return lax.fori_loop(0, 8, tiles, degrees)

    degrees = jnp.zeros((8, 128), jnp.int32)
    for q in range(8):
        degrees = scan(q, degrees)

    inv = lax.rsqrt(1.0 + degrees.astype(F32))
    place = lax.broadcasted_iota(jnp.int32, (128, 128), 1)
    source = 8 * jnp.bitwise_and(place, 15) + jnp.right_shift(place, 4)
    perm = jnp.where(lax.broadcasted_iota(jnp.int32, (128, 128), 0) == source, 1.0, 0.0).astype(BF16)
    feat_load.wait()
    for t in range(8):
        lanes = inv[t:t + 1, :]
        row[:, t * 128:(t + 1) * 128] = jnp.broadcast_to(lanes, (8, 128))
        spread = jnp.broadcast_to(lanes, (128, 128))
        col[t * 128:(t + 1) * 128, :] = spread.T
        scaled = (feat[t * 128:(t + 1) * 128, :].astype(F32).T * spread).astype(BF16)
        moved = jnp.dot(scaled, perm, preferred_element_type=F32).astype(BF16)
        xt[t // 4, :, (t % 4) * 128:(t % 4 + 1) * 128] = moved

    def at(core, xz):
        return g.at[xz, core]

    to_sibling = copies.start(xt.at[other], at(own, me.xz), sibling)
    first = [copies.start(xt.at[own], at(own, me.xz), p) for p in z_peers]
    across = copies.start(xt.at[own], at(own, me.xz), x_peer)
    stays = [
        pltpu.make_async_copy(xt.at[own], at(own, me.xz), local.at[0]),
        pltpu.make_async_copy(w, wc.at[me.rep], local.at[1]),
        pltpu.make_async_copy(cot_rows(me.rep), cotr.at[me.rep], local.at[5]),
        pltpu.make_async_copy(bias_hbm, bias, local.at[9]),
    ]
    for copy in stays:
        copy.start()
    to_vmem = pltpu.make_async_copy(slots_s, slots_v, local.at[2])
    to_vmem.start()
    to_vmem.wait()
    slot_copies = [copies.start(slots_v.at[q], landed_v.at[me.y], y_peers[Y_ORDER[q] - 1]) for q in range(3)]
    kept = pltpu.make_async_copy(slots_v.at[3], landed_v.at[me.y], local.at[3])
    kept.start()

    to_sibling.wait_recv()
    other_x = copies.start(at(other, me.xz), at(other, me.xz), x_peer)
    second = [copies.start(at(other, me.xz), at(other, me.xz), p) for p in z_peers]

    def put_tiles(n, slot_rows, at):
        i = me.dy(n)

        def column(j, _):
            for tc in range(4):
                rows = [slot_rows[at, 0, j * 16 + tc * 4 + s] for s in range(4)]
                tiles = [rm[i, j, tc * 4 + s] for s in range(4)]
                for t in range(8):
                    found = jnp.zeros((16, 128), jnp.int16)
                    for s in range(4):
                        found = jnp.where(rows[s] == t, tiles[s], found)
                    dense[i * 8 + j, tc, t] = found
            return 0

        lax.fori_loop(0, 8, column, 0)

    put_tiles(0, slots_s, 3)
    last = []
    for n in (1, 2, 3):
        first[n - 1].wait_recv()
        source = me.x * 4 + me.dz(4 - n)
        last.append(copies.start(at(own, source), at(own, source), x_peer))
    other_x.wait_recv()
    far = (1 - me.x) * 4 + me.z
    last += [copies.start(at(other, far), at(other, far), p) for p in z_peers]

    def arrive(column):
        n = column % 4
        if column == 0:
            stays[0].wait()
        elif column < 4:
            second[n - 1].wait_recv()
        elif column == 4:
            across.wait_recv()
        else:
            last[n - 1].wait_recv()
            last[n + 2].wait_recv()

    def slots():
        kept.wait()
        for copy in slot_copies:
            copy.wait_recv()
        to_smem = pltpu.make_async_copy(landed_v, landed_s, local.at[4])
        to_smem.start()
        to_smem.wait()

    def place_tiles(n):
        q = Y_ORDER.index(4 - n)
        mask_copies[q].wait_recv()
        put_tiles(n, landed_s, me.dy(n))

    def parameters():
        for copy in early:
            copy.wait_recv()
        for copy in stays[1:]:
            copy.wait()

    return arrive, slots, place_tiles, parameters, copies.wait_sends


def table(values, step):
    found = values[-1]
    for n in range(len(values) - 1):
        found = jnp.where(step == n, values[n], found)
    return found


def unpack(dense, i, j, out_ref):
    one, zero = jnp.asarray(1, BF16), jnp.asarray(0, BF16)
    for tc in range(4):
        for t in range(8):
            words = dense[i * 8 + j, tc, t]
            for k in range(8):
                bits = jnp.where(jnp.bitwise_and(words, jnp.int16(1 << k)) != 0, one, zero)
                first = tc * 128 + k * 16
                out_ref[first:first + 16, t * 128:(t + 1) * 128] = bits


def layer(me, arrive, slots, place_tiles, parameters, dense, g, row, col, wc, bias, cotr, act, ball, gwx, a0, a1,
          acc, part, rc, snd, ry, agg_s, agg, agg_t, slope, act_s, back_s,
          core_s, core_r, sum_s, sum_r, send, recv, local):
    sibling = me.at(c=1 - me.c)
    xl_peer = me.at(xl=1 - me.xl)
    xl_other = me.at(xl=1 - me.xl, c=1 - me.c)
    y_peers = [me.at(y=me.dy(n)) for n in (1, 2, 3)]
    copies = Copies(send, recv)
    own, other = me.c, 1 - me.c

    def to_sibling(s):
        return pltpu.make_async_remote_copy(
            src_ref=part.at[s, other], dst_ref=rc.at[s], send_sem=core_s.at[s], recv_sem=core_r.at[s],
            device_id=sibling, device_id_type=MESH,
        )

    def rows_of(m):
        return pl.ds(pl.multiple_of(m * 256, 256), 256)

    def to_owner(k, m):
        return pltpu.make_async_remote_copy(
            src_ref=snd.at[k - 1, m], dst_ref=ry.at[k - 1, m],
            send_sem=sum_s.at[k * 4 + m - 4], recv_sem=sum_r.at[k * 4 + m - 4],
            device_id=me.at(y=me.dy(table(ROWS, k))), device_id_type=MESH,
        )

    def pass_on(k):
        to_sibling(k).wait_recv()
        for m in range(4):
            rows = slice(m * 256, (m + 1) * 256)
            snd[k - 1, m] = (part[k, own, :, rows].astype(F32) + rc[k, :, rows].astype(F32)).astype(BF16)
            to_owner(k, m).start()

    def chunk(c):
        return me.dy(table(ROWS, c // 8)), me.column(lax.rem(c, 8))

    bufs = (a0, a1)
    unpack(dense, *chunk(0), a0)

    def two_chunks(n, _):
        k, pair = n // 4, lax.rem(n, 4)
        for step in range(4):
            @pl.when(n == step)
            def _():
                arrive(step * 2)
                arrive(step * 2 + 1)

        for step in range(1, 4):
            @pl.when(n == step * 4 - 1)
            def _():
                if step == 1:
                    slots()
                place_tiles(ROWS[step])

        for h in range(2):
            unpack(dense, *chunk(jnp.minimum(n * 2 + h + 1, 31)), bufs[1 - h])
            prod = jnp.dot(g[me.column(pair * 2 + h)].reshape(256, 512), bufs[h][...], preferred_element_type=F32)
            if h == 0:
                acc[...] = jnp.where(pair == 0, 0.0, acc[...]) + prod
            else:
                acc[...] += prod

        @pl.when(pair == 3)
        def _():
            part[k, 0] = acc[0:128].astype(BF16)
            part[k, 1] = acc[128:256].astype(BF16)
            to_sibling(k).start()

        @pl.when(jnp.logical_and(pair == 0, k >= 2))
        def _():
            pass_on(k - 1)

        return 0

    lax.fori_loop(0, 16, two_chunks, 0)
    pass_on(3)
    to_sibling(0).wait_recv()

    def finish_sum(m, out):
        for k in (1, 2, 3):
            to_owner(k, m).wait_recv()
        rows = rows_of(m)
        total = part[0, own, :, rows].astype(F32) + rc[0, :, rows].astype(F32)
        for k in range(3):
            total = total + ry[k, m].astype(F32)
        total = total * row[0:1, rows]
        agg_t[:, rows] = total.astype(BF16)
        out[...] = total.T.astype(BF16)

    swaps = []
    peers = (xl_peer, xl_other, sibling)
    for n in range(3):
        finish_sum(peers[n][1], agg_s.at[n])
        swaps.append(copies.start(agg_s.at[n], agg.at[me.rep], peers[n]))
    finish_sum(me.rep, agg.at[me.rep])
    parameters()
    for copy in reversed(swaps):
        copy.wait_recv()

    for half in range(2):
        rows = slice(half * 128, (half + 1) * 128)
        hidden = jnp.dot(agg[0, rows, :], wc[0], preferred_element_type=F32)
        for q in range(1, 4):
            hidden = hidden + jnp.dot(agg[q, rows, :], wc[q], preferred_element_type=F32)
        hidden = hidden + bias[...]
        logistic = jax.nn.sigmoid(hidden)
        value = hidden * logistic
        factor = logistic * (1.0 + hidden * (1.0 - logistic))
        for q in range(4):
            lanes = slice(q * 128, (q + 1) * 128)
            act_s[q, rows, :] = value[:, lanes]
            slope[me.rep, rows, lanes] = (cotr[q, rows, :].astype(F32) * factor[:, lanes]).astype(BF16)

    def block(y, rep):
        return ball.at[pl.ds(pl.multiple_of(y * 1024 + rep * 256, 256), 256), :]

    def back_into(xl, out):
        for core in range(2):
            value = lax.dot_general(
                slope[me.rep], wc[xl * 2 + core], (((1,), (1,)), ((), ())), preferred_element_type=F32
            )
            out[:, core * 128:(core + 1) * 128] = (value * col[rows_of(me.rep), :]).astype(BF16)

    theirs = (1 - me.xl) * 2 + me.c
    back_into(1 - me.xl, back_s)
    from_xl = copies.start(back_s, block(me.y, me.rep), xl_peer)
    back_into(me.xl, block(me.y, me.rep))

    def send_block(rep):
        here = block(me.y, rep)
        return [copies.start(here, here, y_peers[n - 1]) for n in (2, 1, 3)] + [copies.start(here, here, sibling)]

    mine = send_block(me.rep)
    slope_far = copies.start(slope.at[me.rep], slope.at[me.rep], xl_peer)
    slope_near = copies.start(slope.at[me.rep], slope.at[me.rep], sibling)
    from_xl.wait_recv()
    passed = send_block(theirs)
    acts = [
        copies.start(act_s.at[peer[1]], act.at[rows_of(me.rep), :], peer)
        for peer in (xl_peer, xl_other, sibling)
    ]
    act_kept = pltpu.make_async_copy(act_s.at[me.rep], act.at[rows_of(me.rep), :], local)
    act_kept.start()
    slope_far.wait_recv()
    slope_relay = copies.start(slope.at[theirs], slope.at[theirs], sibling)

    relays = []
    for sent, rep in ((mine, me.rep), (passed, theirs)):
        if rep is theirs:
            slope_near.wait_recv()
            slope_relay.wait_recv()
            ones = jnp.ones((8, 256), BF16)
            grad = jnp.zeros((128, 512), F32)
            gb = jnp.zeros((8, 512), F32)
            for q in range(4):
                grad = grad + jnp.dot(agg_t[:, q * 256:(q + 1) * 256], slope[q], preferred_element_type=F32)
                gb = gb + jnp.dot(ones, slope[q], preferred_element_type=F32)
            for n in range(4):
                gwx[n, 0:32, :] = grad[n * 32:(n + 1) * 32]
                gwx[n, 32:40, :] = gb
        for n, copy in zip((2, 1, 3), sent):
            copy.wait_recv()
            here = block(me.dy(4 - n), rep)
            relays.append(copies.start(here, here, sibling))
    for copy in [mine[3], passed[3]] + relays:
        copy.wait_recv()

    def finish():
        for copy in acts:
            copy.wait_recv()
        act_kept.wait()
        copies.wait_sends()
        for k in (1, 2, 3):
            for m in range(4):
                to_owner(k, m).wait_send()
        for k in range(4):
            to_sibling(k).wait_send()

    return finish


BLOCKS = ((1, 2), (0, 2), (1, 1), (1, 3), (0, 1), (0, 3), (1, 0), (0, 0))
ORDER = {key: n for n, key in enumerate(BLOCKS)}


def settle(me, dense, col, ball, gwx, out, gw, a0, a1,
           acc, part, az, a_sum, ax, bx, b_sum, bz, hold, final, wy, wz, wx_send, wx, gw_own, send, recv, local):
    sibling = me.at(c=1 - me.c)
    x_peer = me.at(x=1 - me.x)
    z_peers = [me.at(z=me.dz(n)) for n in (1, 2, 3)]
    y_peers = [me.at(y=me.dy(n)) for n in (1, 2, 3)]

    def remote(n, src, dst, peer):
        return pltpu.make_async_remote_copy(
            src_ref=src, dst_ref=dst, send_sem=send.at[n], recv_sem=recv.at[n],
            device_id=peer, device_id_type=MESH,
        )

    x_first = {n: remote(n, part.at[ORDER[1, n], 1], bx.at[n], x_peer) for n in range(4)}
    z_first = {
        (side, n): remote(4 + side * 3 + n - 1, part.at[ORDER[side, n], 0], az.at[side, n - 1], z_peers[n - 1])
        for side in range(2) for n in (1, 2, 3)
    }
    z_second = {n: remote(9 + n, b_sum.at[n - 1], bz.at[n - 1], z_peers[n - 1]) for n in (1, 2, 3)}
    x_second = remote(13, a_sum, ax, x_peer)
    w_y = [remote(13 + n, gwx.at[me.dy(n)], wy.at[me.y], y_peers[n - 1]) for n in (1, 2, 3)]
    w_z = [remote(16 + n, wz.at[me.z], wz.at[me.z], z_peers[n - 1]) for n in (1, 2, 3)]
    w_x = remote(20, wx_send, wx, x_peer)
    w_back = [remote(20 + n, gw_own, gw.at[me.y], y_peers[n - 1]) for n in (1, 2, 3)]
    w_kept = pltpu.make_async_copy(gw_own, gw.at[me.y], local.at[0])

    def pass_b(n):
        x_first[n].wait_recv()
        b_sum[n - 1] = (part[ORDER[0, n], 1].astype(F32) + bx[n].astype(F32)).astype(BF16)
        z_second[n].start()

    def pass_a():
        total = part[ORDER[1, 0], 0].astype(F32)
        for n in (1, 2, 3):
            z_first[1, n].wait_recv()
            total = total + az[1, n - 1].astype(F32)
        a_sum[...] = total.astype(BF16)
        x_second.start()

    def weights_z():
        for copy in w_y:
            copy.wait_recv()
        wz[me.z] = (wy[0] + wy[1]) + (wy[2] + wy[3])
        for copy in w_z:
            copy.start()

    def weights_x():
        for copy in w_z:
            copy.wait_recv()
        wx_send[...] = (wz[0] + wz[1]) + (wz[2] + wz[3])
        w_x.start()

    def weights_back():
        w_x.wait_recv()
        gw_own[...] = wx_send[...] + wx[...]
        w_kept.start()
        for copy in w_back:
            copy.start()

    actions = {n: [] for n in range(8)}
    for n in range(4):
        actions[ORDER[1, n]].append(x_first[n].start)
    for key, copy in z_first.items():
        actions[ORDER[key]].append(copy.start)
    for n, step in ((2, 2), (1, 4), (3, 5)):
        actions[step].append(functools.partial(pass_b, n))
    actions[1].append(weights_z)
    actions[3].append(weights_x)
    actions[6].append(pass_a)
    actions[6].append(weights_back)

    for copy in w_y:
        copy.start()
    wy[me.y] = gwx[me.y]

    def chunk(c):
        at = c // 4
        x = lax.rem(me.x + table([block[0] for block in BLOCKS], at), 2)
        z = lax.rem(me.z + table([block[1] for block in BLOCKS], at), 4)
        return lax.rem(c, 4), x * 4 + z

    bufs = (a0, a1)
    unpack(dense, *chunk(0), a0)

    def two_chunks(step, _):
        block, pair = step // 2, lax.rem(step, 2)
        for h in range(2):
            unpack(dense, *chunk(jnp.minimum(step * 2 + h + 1, 31)), bufs[1 - h])
            prod = jnp.dot(bufs[h][...], ball[pl.ds(pl.multiple_of((pair * 2 + h) * 1024, 1024), 1024), :], preferred_element_type=F32)
            if h == 0:
                acc[...] = jnp.where(pair == 0, 0.0, acc[...]) + prod
            else:
                acc[...] += prod

        @pl.when(pair == 1)
        def _():
            part[block, 0] = acc[0:256].astype(BF16)
            part[block, 1] = acc[256:512].astype(BF16)

        for at, calls in actions.items():
            if calls:
                @pl.when(step == at * 2 + 1)
                def _():
                    for call in calls:
                        call()

        return 0

    lax.fori_loop(0, 16, two_chunks, 0)

    def place(tile, total):
        here = slice(tile * 128, tile * 128 + 256)
        for q in range(2):
            hold[q * 512 + tile * 128:q * 512 + tile * 128 + 256, :] = total[:, q * 128:(q + 1) * 128]
        for t in range(tile, tile + 2):
            for w in range(16):
                first = t * 128 + w * 8
                scale = col[pl.ds(pl.multiple_of(me.c * 512 + first, 8), 8), :]
                for q in range(2):
                    final[q, first:first + 8, :] = hold[pl.ds(q * 512 + t * 128 + w, 8, stride=16), :] * scale
        at = tile // 2
        swap = remote(24 + at, final.at[1 - me.c, here], out.at[me.c, here], sibling)
        keep = pltpu.make_async_copy(final.at[me.c, here], out.at[me.c, here], local.at[1 + at])
        swap.start()
        keep.start()
        return swap, keep

    total = part[ORDER[0, 0], 1].astype(F32)
    x_first[0].wait_recv()
    total = total + bx[0].astype(F32)
    for n in (1, 2, 3):
        z_second[n].wait_recv()
        total = total + bz[n - 1].astype(F32)
    swaps = [place(2, total)]
    total = part[ORDER[0, 0], 0].astype(F32)
    for n in (1, 2, 3):
        z_first[0, n].wait_recv()
        total = total + az[0, n - 1].astype(F32)
    x_second.wait_recv()
    total = total + ax[...].astype(F32)
    swaps.append(place(0, total))
    for copy in w_back:
        copy.wait_recv()
    for swap, keep in swaps:
        swap.wait_recv()
        keep.wait()
    w_kept.wait()
    for copy in list(x_first.values()) + list(z_first.values()) + list(z_second.values()):
        copy.wait_send()
    for copy in [x_second, w_x] + [swap for swap, _ in swaps] + w_y + w_z + w_back:
        copy.wait_send()


HALF = (256, 256)
HELD = (
    pltpu.VMEM((32, 4, 8, 16, 128), jnp.int16),
    pltpu.VMEM((8, 1024), F32),
    pltpu.VMEM((1024, 128), F32),
    pltpu.VMEM((8, 2, 128, 512), BF16),
    pltpu.VMEM((4, 128, 512), BF16),
    pltpu.VMEM((4, 256, 128), BF16),
    pltpu.VMEM((1, 512), F32),
    pltpu.VMEM((4096, 256), BF16),
    pltpu.VMEM((4, 40, 512), F32),
    pltpu.VMEM((512, 1024), BF16),
    pltpu.VMEM((512, 1024), BF16),
)
SPREAD = (
    pltpu.SMEM((4, 256), jnp.int32),
    pltpu.SMEM((1, 256), jnp.int32),
    pltpu.VMEM((1024, 128), BF16),
    pltpu.VMEM((8, 8, 16, 16, 128), jnp.int32),
    pltpu.VMEM((3, 8, 16, 16, 128), jnp.int16),
    pltpu.VMEM((4, 8, 16, 16, 128), jnp.int16),
    pltpu.SMEM((4, 1, 128), jnp.int32),
    pltpu.VMEM((4, 1, 128), jnp.int32),
    pltpu.VMEM((4, 1, 128), jnp.int32),
    pltpu.SMEM((4, 1, 128), jnp.int32),
    pltpu.VMEM((2, 128, 512), BF16),
    DMA((27,)),
    DMA((27,)),
    DMA((8,)),
    DMA((10,)),
)
LAYER = (
    pltpu.VMEM((256, 1024), F32),
    pltpu.VMEM((4, 2, 128, 1024), BF16),
    pltpu.VMEM((4, 128, 1024), BF16),
    pltpu.VMEM((3, 4, 128, 256), BF16),
    pltpu.VMEM((3, 4, 128, 256), BF16),
    pltpu.VMEM((3, 256, 128), BF16),
    pltpu.VMEM((4, 256, 128), BF16),
    pltpu.VMEM((128, 1024), BF16),
    pltpu.VMEM((4, 256, 512), BF16),
    pltpu.VMEM((4, 256, 128), F32),
    pltpu.VMEM((256, 256), BF16),
    DMA((4,)),
    DMA((4,)),
    DMA((12,)),
    DMA((12,)),
    DMA((24,)),
    DMA((24,)),
    DMA,
)
SETTLE = (
    pltpu.VMEM((512, 256), F32),
    pltpu.VMEM((8, 2) + HALF, BF16),
    pltpu.VMEM((2, 3) + HALF, BF16),
    pltpu.VMEM(HALF, BF16),
    pltpu.VMEM(HALF, BF16),
    pltpu.VMEM((4,) + HALF, BF16),
    pltpu.VMEM((3,) + HALF, BF16),
    pltpu.VMEM((3,) + HALF, BF16),
    pltpu.VMEM((1024, 128), F32),
    pltpu.VMEM((2, 512, 128), F32),
    pltpu.VMEM((4, 40, 512), F32),
    pltpu.VMEM((4, 40, 512), F32),
    pltpu.VMEM((40, 512), F32),
    pltpu.VMEM((40, 512), F32),
    pltpu.VMEM((40, 512), F32),
    DMA((26,)),
    DMA((26,)),
    DMA((3,)),
)


def all_kernel(*refs):
    groups, first = [], 0
    for size in (7, 3, len(HELD), len(SPREAD), len(LAYER), len(SETTLE)):
        groups.append(refs[first:first + size])
        first += size
    ins, (act, out, gw), held, spread_refs, layer_refs, settle_refs = groups
    dense, row, col, g, wc, cotr, bias, ball, gwx, a0, a1 = held
    me = Place()
    *arrivals, finish_spread = spread(me, *ins, dense, row, col, g, wc, cotr, bias, *spread_refs)
    finish_layer = layer(
        me, *arrivals, dense, g, row, col, wc, bias, cotr, act, ball, gwx, a0, a1, *layer_refs
    )
    settle(me, dense, col, ball, gwx, out, gw, a0, a1, *settle_refs)
    finish_layer()
    finish_spread()


def results_kernel(act, out, gw, act_out, feat_out, gw_out, gb_out, act_v, feat_v, gw_v, load, store):
    loads = [pltpu.make_async_copy(gw, gw_v, load.at[0])]
    for n in range(2):
        here = slice(n * 512, n * 512 + 512)
        loads.append(pltpu.make_async_copy(act.at[here], act_v.at[here], load.at[1 + n]))
        loads.append(pltpu.make_async_copy(out.at[here], feat_v.at[here], load.at[3 + n]))
    for copy in loads:
        copy.start()
    loads[0].wait()
    stores = [
        pltpu.make_async_copy(gw_v.at[:, 0:32], gw_out, store.at[0]),
        pltpu.make_async_copy(gw_v.at[0, 32:33], gb_out, store.at[1]),
    ]
    for copy in stores:
        copy.start()
    for n in range(2):
        here = slice(n * 512, n * 512 + 512)
        loads[1 + 2 * n].wait()
        stores.append(pltpu.make_async_copy(act_v.at[here], act_out.at[here], store.at[2 + n]))
        stores[-1].start()
        loads[2 + 2 * n].wait()
        stores.append(pltpu.make_async_copy(feat_v.at[here], feat_out.at[here], store.at[4 + n]))
        stores[-1].start()
    for copy in stores:
        copy.wait()


def body(features, weight, bias_vector, cotangent, tile_masks, tile_rows, tile_counts):
    masks = tile_masks.reshape(8, 4, 2, 16, 16, 128)
    act, out, gw = pl.pallas_call(
        all_kernel,
        out_shape=(
            jax.ShapeDtypeStruct((1024, 128), F32),
            jax.ShapeDtypeStruct((2, 512, 128), F32),
            jax.ShapeDtypeStruct((4, 40, 512), F32),
        ),
        in_specs=[HBM] * 7,
        out_specs=(HBM,) * 3,
        scratch_shapes=HELD + SPREAD + LAYER + SETTLE,
        compiler_params=pltpu.CompilerParams(
            collective_id=0, has_side_effects=True, vmem_limit_bytes=VMEM_MIB * MIB
        ),
        name="layer",
    )(tile_rows[0].T, tile_counts, masks, features, weight, bias_vector.reshape(1, 512), cotangent)
    act, out, gw, gb = pl.pallas_call(
        results_kernel,
        out_shape=(
            jax.ShapeDtypeStruct((1024, 128), F32),
            jax.ShapeDtypeStruct((1024, 128), F32),
            jax.ShapeDtypeStruct((4, 32, 512), F32),
            jax.ShapeDtypeStruct((1, 512), F32),
        ),
        in_specs=[HBM] * 3,
        out_specs=(HBM,) * 4,
        scratch_shapes=[
            pltpu.VMEM((1024, 128), F32),
            pltpu.VMEM((1024, 128), F32),
            pltpu.VMEM((4, 40, 512), F32),
            DMA((5,)),
            DMA((6,)),
        ],
        compiler_params=pltpu.CompilerParams(vmem_limit_bytes=VMEM_MIB * MIB),
        name="results",
    )(act, out.reshape(1024, 128), gw)
    return act, out, gw.reshape(128, 512), gb.reshape(512)


def solution(mesh):
    return jax.shard_map(
        body,
        mesh=mesh,
        in_specs=(
            P("blk", "rep"),
            P("rep", None),
            P(),
            P("blk", "rep"),
            P("blk", None, None, None, None),
            P("blk", None, None),
            P("blk", None),
        ),
        out_specs=(P("blk", "rep"), P("blk", "rep"), P("rep", None), P()),
        check_vma=False,
    )
```

```python
import functools

import jax
import jax.numpy as jnp
from jax import lax
from jax.experimental import pallas as pl
from jax.experimental.pallas import tpu as pltpu
from jax.sharding import PartitionSpec as P

MESH = pl.DeviceIdType.MESH
BF16 = jnp.bfloat16
F32 = jnp.float32
HBM = pl.BlockSpec(memory_space=pltpu.HBM)
DMA = pltpu.SemaphoreType.DMA
MIB = 2**20
VMEM_MIB = 60


class Place:
    def __init__(self):
        blk = lax.axis_index("blk")
        rep = lax.axis_index("rep")
        self.x, self.z, self.y = blk // 16, lax.rem(blk // 4, 4), lax.rem(blk, 4)
        self.xl, self.c = rep // 2, lax.rem(rep, 2)
        self.rep = rep
        self.xz = self.x * 4 + self.z

    def at(self, x=None, z=None, y=None, xl=None, c=None):
        x = self.x if x is None else x
        z = self.z if z is None else z
        y = self.y if y is None else y
        xl = self.xl if xl is None else xl
        c = self.c if c is None else c
        return (x * 16 + z * 4 + y, xl * 2 + c)

    def dy(self, n):
        return lax.rem(self.y + n, 4)

    def dz(self, n):
        return lax.rem(self.z + n, 4)

    def column(self, n):
        return lax.rem(self.x + n // 4, 2) * 4 + self.dz(4 - lax.rem(n, 4))


class Copies:
    def __init__(self, send, recv):
        self.send, self.recv, self.used = send, recv, []

    def start(self, src, dst, peer):
        n = len(self.used)
        copy = pltpu.make_async_remote_copy(
            src_ref=src, dst_ref=dst, send_sem=self.send.at[n], recv_sem=self.recv.at[n],
            device_id=peer, device_id_type=MESH,
        )
        copy.start()
        self.used.append(copy)
        return copy

    def wait_sends(self):
        for copy in self.used:
            copy.wait_send()


Y_ORDER = (2, 1, 3, 0)
ROWS = (2, 1, 3, 0)


def spread(me, rows_hbm, counts_hbm, masks, feat_hbm, w, bias_hbm, cot, dense, row, col, gs, wc, cotr, bias,
           rows_ref, counts_ref, feat, g, inv_s, scale, words, m16, rm, slots_s, slots_v, landed_v, landed_s, xt, send, recv, load, local):
    own, other = me.c, 1 - me.c
    small = [
        pltpu.make_async_copy(rows_hbm, rows_ref, local.at[6]),
        pltpu.make_async_copy(counts_hbm, counts_ref, local.at[7]),
    ]
    for copy in small:
        copy.start()
    loads = []
    for q in range(8):
        half = own if q < 4 else other
        loads.append(pltpu.make_async_copy(masks.at[:, me.dy(Y_ORDER[q % 4]), half], words.at[q], load.at[q]))
        loads[q].start()
    feat_load = pltpu.make_async_copy(feat_hbm, feat, local.at[8])
    feat_load.start()

    sibling = me.at(c=1 - me.c)
    x_peer = me.at(x=1 - me.x)
    z_peers = [me.at(z=me.dz(n)) for n in (1, 2, 3)]
    y_peers = [me.at(y=me.dy(n)) for n in (1, 2, 3)]
    rep_peers = [sibling, me.at(xl=1 - me.xl), me.at(xl=1 - me.xl, c=1 - me.c)]
    xz_peers = z_peers + [x_peer] + [me.at(x=1 - me.x, z=me.dz(n)) for n in (1, 2, 3)]
    everyone = xz_peers + y_peers + rep_peers
    barrier = pltpu.get_barrier_semaphore()
    for peer in everyone:
        pl.semaphore_signal(barrier, inc=1, device_id=peer, device_id_type=MESH)

    def narrow(q):
        loads[q].wait()

        def tiles(xz, _):
            for slot in range(16):
                tile = words[q, xz, slot].astype(jnp.int16)
                if q < 3:
                    m16[q, xz, slot] = tile
                else:
                    rm[me.y, xz, slot] = tile
            return 0

        lax.fori_loop(0, 8, tiles, 0)

    for copy in small:
        copy.wait()

    def fill(xz, _):
        for q in range(4):
            first = ((xz * 4 + me.dy(Y_ORDER[q])) * 2 + own) * 4
            for tc in range(4):
                count = counts_ref[0, first + tc]
                for s in range(4):
                    slots_s[q, 0, xz * 16 + tc * 4 + s] = jnp.where(s < count, rows_ref[s, first + tc], 8)
        return 0

    lax.fori_loop(0, 8, fill, 0)
    to_vmem = pltpu.make_async_copy(slots_s, slots_v, local.at[2])
    to_vmem.start()

    place = lax.broadcasted_iota(jnp.int32, (128, 128), 1)
    source = 8 * jnp.bitwise_and(place, 15) + jnp.right_shift(place, 4)
    perm = jnp.where(lax.broadcasted_iota(jnp.int32, (128, 128), 0) == source, 1.0, 0.0).astype(BF16)
    feat_load.wait()
    for t in range(8):
        turned = feat[t * 128:(t + 1) * 128, :].astype(F32).T.astype(BF16)
        moved = jnp.dot(turned, perm, preferred_element_type=F32).astype(BF16)
        xt[t // 4, :, (t % 4) * 128:(t % 4 + 1) * 128] = moved
    narrow(0)
    to_vmem.wait()
    pl.semaphore_wait(barrier, len(everyone))
    copies = Copies(send, recv)

    def cot_rows(rep):
        return cot.at[pl.ds(pl.multiple_of(rep * 256, 256), 256), :]

    def at(core, xz):
        return g.at[xz, core]

    slot_copies = [copies.start(slots_v.at[q], landed_v.at[me.y], y_peers[Y_ORDER[q] - 1]) for q in range(3)]
    to_sibling = copies.start(xt.at[other], at(own, me.xz), sibling)
    first = [copies.start(xt.at[own], at(own, me.xz), p) for p in z_peers]
    across = copies.start(xt.at[own], at(own, me.xz), x_peer)
    mask_copies = [copies.start(m16.at[0], rm.at[me.y], y_peers[Y_ORDER[0] - 1])]
    stays = [
        pltpu.make_async_copy(xt.at[own], at(own, me.xz), local.at[0]),
        pltpu.make_async_copy(w, wc.at[me.rep], local.at[1]),
        pltpu.make_async_copy(cot_rows(me.rep), cotr.at[me.rep], local.at[5]),
        pltpu.make_async_copy(bias_hbm, bias, local.at[9]),
    ]
    for copy in stays:
        copy.start()
    kept = pltpu.make_async_copy(slots_v.at[3], landed_v.at[me.y], local.at[3])
    kept.start()
    tile_row = lax.broadcasted_iota(jnp.int32, (8, 128), 0)

    def scan(q, degrees):
        n = Y_ORDER[q % 4]
        half = own if q < 4 else other
        if q >= 4:
            loads[q].wait()

        def tiles(xz, degrees):
            first = ((xz * 4 + me.dy(n)) * 2 + half) * 4
            for tc in range(4):
                count = counts_ref[0, first + tc]
                for s in range(4):
                    t = jnp.where(s < count, rows_ref[s, first + tc], 8)
                    tile = words[q, xz, tc * 4 + s]
                    joined = jnp.bitwise_or(tile[:8], jnp.left_shift(tile[8:], 8))
                    counted = jnp.sum(lax.population_count(joined), axis=0, keepdims=True)
                    degrees = degrees + jnp.where(tile_row == t, counted, 0)
            return degrees

        return lax.fori_loop(0, 8, tiles, degrees)

    degrees = scan(0, jnp.zeros((8, 128), jnp.int32))
    narrow(1)
    to_sibling.wait_recv()
    other_x = copies.start(at(other, me.xz), at(other, me.xz), x_peer)
    second = [copies.start(at(other, me.xz), at(other, me.xz), p) for p in z_peers]
    degrees = scan(1, degrees)
    narrow(2)
    for q in (1, 2):
        mask_copies.append(copies.start(m16.at[q], rm.at[me.y], y_peers[Y_ORDER[q] - 1]))
    early = []
    for peer in rep_peers:
        early.append(copies.start(cot_rows(peer[1]), cotr.at[me.rep], peer))
        early.append(copies.start(w, wc.at[me.rep], peer))
    narrow(3)
    for q in (2, 3, 4):
        degrees = scan(q, degrees)
    last = []
    for n in (1, 2, 3):
        first[n - 1].wait_recv()
        source = me.x * 4 + me.dz(4 - n)
        last.append(copies.start(at(own, source), at(own, source), x_peer))
    for q in (5, 6, 7):
        degrees = scan(q, degrees)

    degrees = 1.0 + degrees.astype(F32)
    high = jnp.floor(degrees * (1.0 / 256.0))
    low = degrees - high * 256.0
    placed = 256.0 * jnp.dot(high.astype(BF16), perm, preferred_element_type=F32)
    placed = placed + jnp.dot(low.astype(BF16), perm, preferred_element_type=F32)
    inv_s[...] = lax.rsqrt(placed)
    inv_copies = [copies.start(inv_s, scale.at[me.xz], peer) for peer in xz_peers]
    inv = lax.rsqrt(degrees)
    other_x.wait_recv()
    far = (1 - me.x) * 4 + me.z
    last += [copies.start(at(other, far), at(other, far), p) for p in z_peers]
    scale[me.xz] = inv_s[...]
    for t in range(8):
        lanes = inv[t:t + 1, :]
        row[:, t * 128:(t + 1) * 128] = jnp.broadcast_to(lanes, (8, 128))
        col[t * 128:(t + 1) * 128, :] = jnp.broadcast_to(lanes, (128, 128)).T

    def put_tiles(n, slot_rows, at):
        i = me.dy(n)

        def column(j, _):
            for tc in range(4):
                rows = [slot_rows[at, 0, j * 16 + tc * 4 + s] for s in range(4)]
                tiles = [rm[i, j, tc * 4 + s] for s in range(4)]
                for t in range(8):
                    found = jnp.zeros((16, 128), jnp.int16)
                    for s in range(4):
                        found = jnp.where(rows[s] == t, tiles[s], found)
                    dense[i * 8 + j, tc, t] = found
            return 0

        lax.fori_loop(0, 8, column, 0)

    put_tiles(0, slots_s, 3)

    def arrive(column):
        n = column % 4
        if column == 0:
            stays[0].wait()
        elif column < 4:
            second[n - 1].wait_recv()
        elif column == 4:
            across.wait_recv()
        else:
            last[n - 1].wait_recv()
            last[n + 2].wait_recv()
        if column:
            inv_copies[column - 1].wait_recv()
        xz = me.column(column)
        for t in range(4):
            lanes = slice(t * 128, (t + 1) * 128)
            factor = scale[xz, pl.ds(own * 4 + t, 1), :]
            for core in range(2):
                gs[xz, core, :, lanes] = (g[xz, core, :, lanes].astype(F32) * factor).astype(BF16)

    def slots():
        kept.wait()
        for copy in slot_copies:
            copy.wait_recv()
        to_smem = pltpu.make_async_copy(landed_v, landed_s, local.at[4])
        to_smem.start()
        to_smem.wait()

    def place_tiles(n):
        q = Y_ORDER.index(4 - n)
        mask_copies[q].wait_recv()
        put_tiles(n, landed_s, me.dy(n))

    def parameters():
        for copy in early:
            copy.wait_recv()
        for copy in stays[1:]:
            copy.wait()

    return arrive, slots, place_tiles, parameters, copies.wait_sends


def table(values, step):
    found = values[-1]
    for n in range(len(values) - 1):
        found = jnp.where(step == n, values[n], found)
    return found


def unpack(dense, i, j, out_ref):
    one, zero = jnp.asarray(1, BF16), jnp.asarray(0, BF16)
    for tc in range(4):
        for t in range(8):
            words = dense[i * 8 + j, tc, t]
            for k in range(8):
                bits = jnp.where(jnp.bitwise_and(words, jnp.int16(1 << k)) != 0, one, zero)
                first = tc * 128 + k * 16
                out_ref[first:first + 16, t * 128:(t + 1) * 128] = bits


def layer(me, arrive, slots, place_tiles, parameters, dense, g, row, col, wc, bias, cotr, act, ball, gwx, a0, a1,
          acc, part, rc, snd, ry, agg_s, agg, agg_t, slope, act_s, back_s,
          core_s, core_r, sum_s, sum_r, send, recv, local):
    sibling = me.at(c=1 - me.c)
    xl_peer = me.at(xl=1 - me.xl)
    xl_other = me.at(xl=1 - me.xl, c=1 - me.c)
    y_peers = [me.at(y=me.dy(n)) for n in (1, 2, 3)]
    copies = Copies(send, recv)
    own, other = me.c, 1 - me.c

    def to_sibling(s):
        return pltpu.make_async_remote_copy(
            src_ref=part.at[s, other], dst_ref=rc.at[s], send_sem=core_s.at[s], recv_sem=core_r.at[s],
            device_id=sibling, device_id_type=MESH,
        )

    def rows_of(m):
        return pl.ds(pl.multiple_of(m * 256, 256), 256)

    def to_owner(k, m):
        return pltpu.make_async_remote_copy(
            src_ref=snd.at[k, m], dst_ref=ry.at[k, m], send_sem=sum_s.at[k * 4 + m], recv_sem=sum_r.at[k * 4 + m],
            device_id=me.at(y=me.dy(table((2, 1, 3), k))), device_id_type=MESH,
        )

    def pass_on(k):
        to_sibling(k).wait_recv()
        for m in range(4):
            rows = slice(m * 256, (m + 1) * 256)
            snd[k, m] = (part[k, own, :, rows].astype(F32) + rc[k, :, rows].astype(F32)).astype(BF16)
            to_owner(k, m).start()

    def chunk(c):
        return me.dy(table(ROWS, c // 8)), me.column(lax.rem(c, 8))

    slots()
    place_tiles(ROWS[0])
    bufs = (a0, a1)
    unpack(dense, *chunk(0), a0)

    def two_chunks(n, _):
        k, pair = n // 4, lax.rem(n, 4)
        for step in range(4):
            @pl.when(n == step)
            def _():
                arrive(step * 2)
                arrive(step * 2 + 1)

        for step in (1, 2):
            @pl.when(n == step * 4 - 1)
            def _():
                place_tiles(ROWS[step])

        for h in range(2):
            unpack(dense, *chunk(jnp.minimum(n * 2 + h + 1, 31)), bufs[1 - h])
            prod = jnp.dot(g[me.column(pair * 2 + h)].reshape(256, 512), bufs[h][...], preferred_element_type=F32)
            if h == 0:
                acc[...] = jnp.where(pair == 0, 0.0, acc[...]) + prod
            else:
                acc[...] += prod

        @pl.when(pair == 3)
        def _():
            part[k, 0] = acc[0:128].astype(BF16)
            part[k, 1] = acc[128:256].astype(BF16)
            to_sibling(k).start()

        @pl.when(jnp.logical_and(pair == 0, k >= 1))
        def _():
            pass_on(k - 1)

        return 0

    lax.fori_loop(0, 16, two_chunks, 0)
    to_sibling(3).wait_recv()

    def finish_sum(m, out):
        for k in range(3):
            to_owner(k, m).wait_recv()
        rows = rows_of(m)
        total = part[3, own, :, rows].astype(F32) + rc[3, :, rows].astype(F32)
        for k in range(3):
            total = total + ry[k, m].astype(F32)
        total = total * row[0:1, rows]
        agg_t[:, rows] = total.astype(BF16)
        out[...] = total.T.astype(BF16)

    swaps = []
    peers = (xl_peer, xl_other, sibling)
    for n in range(3):
        finish_sum(peers[n][1], agg_s.at[n])
        swaps.append(copies.start(agg_s.at[n], agg.at[me.rep], peers[n]))
    finish_sum(me.rep, agg.at[me.rep])
    parameters()
    for copy in reversed(swaps):
        copy.wait_recv()

    for half in range(2):
        rows = slice(half * 128, (half + 1) * 128)
        hidden = jnp.dot(agg[0, rows, :], wc[0], preferred_element_type=F32)
        for q in range(1, 4):
            hidden = hidden + jnp.dot(agg[q, rows, :], wc[q], preferred_element_type=F32)
        hidden = hidden + bias[...]
        logistic = jax.nn.sigmoid(hidden)
        value = hidden * logistic
        factor = logistic * (1.0 + hidden * (1.0 - logistic))
        for q in range(4):
            lanes = slice(q * 128, (q + 1) * 128)
            act_s[q, rows, :] = value[:, lanes]
            slope[me.rep, rows, lanes] = (cotr[q, rows, :].astype(F32) * factor[:, lanes]).astype(BF16)

    def block(y, rep):
        return ball.at[pl.ds(pl.multiple_of(y * 1024 + rep * 256, 256), 256), :]

    def back_into(xl, out):
        for core in range(2):
            value = lax.dot_general(
                slope[me.rep], wc[xl * 2 + core], (((1,), (1,)), ((), ())), preferred_element_type=F32
            )
            out[:, core * 128:(core + 1) * 128] = (value * col[rows_of(me.rep), :]).astype(BF16)

    theirs = (1 - me.xl) * 2 + me.c
    back_into(1 - me.xl, back_s)
    from_xl = copies.start(back_s, block(me.y, me.rep), xl_peer)
    back_into(me.xl, block(me.y, me.rep))

    def send_block(rep):
        here = block(me.y, rep)
        return [copies.start(here, here, y_peers[n - 1]) for n in (2, 1, 3)] + [copies.start(here, here, sibling)]

    mine = send_block(me.rep)
    slope_far = copies.start(slope.at[me.rep], slope.at[me.rep], xl_peer)
    slope_near = copies.start(slope.at[me.rep], slope.at[me.rep], sibling)
    from_xl.wait_recv()
    passed = send_block(theirs)
    acts = [
        copies.start(act_s.at[peer[1]], act.at[rows_of(me.rep), :], peer)
        for peer in (xl_peer, xl_other, sibling)
    ]
    act_kept = pltpu.make_async_copy(act_s.at[me.rep], act.at[rows_of(me.rep), :], local)
    act_kept.start()
    slope_far.wait_recv()
    slope_relay = copies.start(slope.at[theirs], slope.at[theirs], sibling)

    relays = []
    for sent, rep in ((mine, me.rep), (passed, theirs)):
        if rep is theirs:
            slope_near.wait_recv()
            slope_relay.wait_recv()
            ones = jnp.ones((8, 256), BF16)
            grad = jnp.zeros((128, 512), F32)
            gb = jnp.zeros((8, 512), F32)
            for q in range(4):
                grad = grad + jnp.dot(agg_t[:, q * 256:(q + 1) * 256], slope[q], preferred_element_type=F32)
                gb = gb + jnp.dot(ones, slope[q], preferred_element_type=F32)
            for n in range(4):
                gwx[n, 0:32, :] = grad[n * 32:(n + 1) * 32]
                gwx[n, 32:40, :] = gb
        for n, copy in zip((2, 1, 3), sent):
            copy.wait_recv()
            here = block(me.dy(4 - n), rep)
            relays.append(copies.start(here, here, sibling))
    for copy in [mine[3], passed[3]] + relays:
        copy.wait_recv()

    def finish():
        for copy in acts:
            copy.wait_recv()
        act_kept.wait()
        copies.wait_sends()
        for k in range(3):
            for m in range(4):
                to_owner(k, m).wait_send()
        for k in range(4):
            to_sibling(k).wait_send()

    return finish


BLOCKS = ((1, 2), (1, 1), (1, 3), (1, 0), (0, 2), (0, 1), (0, 3), (0, 0))
ORDER = {key: n for n, key in enumerate(BLOCKS)}


def settle(me, dense, col, ball, gwx, out, gw, a0, a1,
           acc, part, az, a_sum, ax, bx, b_sum, bz, hold, final, wy, wz, wx_send, wx, gw_own, send, recv, local):
    sibling = me.at(c=1 - me.c)
    x_peer = me.at(x=1 - me.x)
    z_peers = [me.at(z=me.dz(n)) for n in (1, 2, 3)]
    y_peers = [me.at(y=me.dy(n)) for n in (1, 2, 3)]

    def remote(n, src, dst, peer):
        return pltpu.make_async_remote_copy(
            src_ref=src, dst_ref=dst, send_sem=send.at[n], recv_sem=recv.at[n],
            device_id=peer, device_id_type=MESH,
        )

    x_first = {n: remote(n, part.at[ORDER[1, n], 1], bx.at[n], x_peer) for n in range(4)}
    z_first = {
        (side, n): remote(4 + side * 3 + n - 1, part.at[ORDER[side, n], 0], az.at[side, n - 1], z_peers[n - 1])
        for side in range(2) for n in (1, 2, 3)
    }
    z_second = {n: remote(9 + n, b_sum.at[n - 1], bz.at[n - 1], z_peers[n - 1]) for n in (1, 2, 3)}
    x_second = remote(13, a_sum, ax, x_peer)
    w_y = [remote(13 + n, gwx.at[me.dy(n)], wy.at[me.y], y_peers[n - 1]) for n in (1, 2, 3)]
    w_z = [remote(16 + n, wz.at[me.z], wz.at[me.z], z_peers[n - 1]) for n in (1, 2, 3)]
    w_x = remote(20, wx_send, wx, x_peer)
    w_back = [remote(20 + n, gw_own, gw.at[me.y], y_peers[n - 1]) for n in (1, 2, 3)]
    w_kept = pltpu.make_async_copy(gw_own, gw.at[me.y], local.at[0])

    def pass_b(n):
        x_first[n].wait_recv()
        b_sum[n - 1] = (part[ORDER[0, n], 1].astype(F32) + bx[n].astype(F32)).astype(BF16)
        z_second[n].start()

    def pass_a():
        total = part[ORDER[1, 0], 0].astype(F32)
        for n in (1, 2, 3):
            z_first[1, n].wait_recv()
            total = total + az[1, n - 1].astype(F32)
        a_sum[...] = total.astype(BF16)
        x_second.start()

    def weights_z():
        for copy in w_y:
            copy.wait_recv()
        wz[me.z] = (wy[0] + wy[1]) + (wy[2] + wy[3])
        for copy in w_z:
            copy.start()

    def weights_x():
        for copy in w_z:
            copy.wait_recv()
        wx_send[...] = (wz[0] + wz[1]) + (wz[2] + wz[3])
        w_x.start()

    def weights_back():
        w_x.wait_recv()
        gw_own[...] = wx_send[...] + wx[...]
        w_kept.start()
        for copy in w_back:
            copy.start()

    actions = {n: [] for n in range(8)}
    for n in range(4):
        actions[ORDER[1, n]].append(x_first[n].start)
    for n in (2, 1, 3):
        actions[ORDER[0, n]].append(functools.partial(pass_b, n))
    for key, copy in z_first.items():
        actions[ORDER[key]].append(copy.start)
    actions[3].append(weights_z)
    actions[4].append(pass_a)
    actions[5].append(weights_x)
    actions[6].append(weights_back)

    for copy in w_y:
        copy.start()
    wy[me.y] = gwx[me.y]

    def chunk(c):
        at = c // 4
        x = lax.rem(me.x + table([block[0] for block in BLOCKS], at), 2)
        z = lax.rem(me.z + table([block[1] for block in BLOCKS], at), 4)
        return lax.rem(c, 4), x * 4 + z

    bufs = (a0, a1)
    unpack(dense, *chunk(0), a0)

    def two_chunks(step, _):
        block, pair = step // 2, lax.rem(step, 2)
        for h in range(2):
            unpack(dense, *chunk(jnp.minimum(step * 2 + h + 1, 31)), bufs[1 - h])
            prod = jnp.dot(bufs[h][...], ball[pl.ds(pl.multiple_of((pair * 2 + h) * 1024, 1024), 1024), :], preferred_element_type=F32)
            if h == 0:
                acc[...] = jnp.where(pair == 0, 0.0, acc[...]) + prod
            else:
                acc[...] += prod

        @pl.when(pair == 1)
        def _():
            part[block, 0] = acc[0:256].astype(BF16)
            part[block, 1] = acc[256:512].astype(BF16)

        for at, calls in actions.items():
            if calls:
                @pl.when(step == at * 2 + 1)
                def _():
                    for call in calls:
                        call()

        return 0

    lax.fori_loop(0, 16, two_chunks, 0)

    def place(tile, total):
        here = slice(tile * 128, tile * 128 + 256)
        for q in range(2):
            hold[q * 512 + tile * 128:q * 512 + tile * 128 + 256, :] = total[:, q * 128:(q + 1) * 128]
        for t in range(tile, tile + 2):
            for w in range(16):
                first = t * 128 + w * 8
                scale = col[pl.ds(pl.multiple_of(me.c * 512 + first, 8), 8), :]
                for q in range(2):
                    final[q, first:first + 8, :] = hold[pl.ds(q * 512 + t * 128 + w, 8, stride=16), :] * scale
        at = tile // 2
        swap = remote(24 + at, final.at[1 - me.c, here], out.at[me.c, here], sibling)
        keep = pltpu.make_async_copy(final.at[me.c, here], out.at[me.c, here], local.at[1 + at])
        swap.start()
        keep.start()
        return swap, keep

    total = part[ORDER[0, 0], 1].astype(F32)
    x_first[0].wait_recv()
    total = total + bx[0].astype(F32)
    for n in (1, 2, 3):
        z_second[n].wait_recv()
        total = total + bz[n - 1].astype(F32)
    swaps = [place(2, total)]
    total = part[ORDER[0, 0], 0].astype(F32)
    for n in (1, 2, 3):
        z_first[0, n].wait_recv()
        total = total + az[0, n - 1].astype(F32)
    x_second.wait_recv()
    total = total + ax[...].astype(F32)
    swaps.append(place(0, total))
    for copy in w_back:
        copy.wait_recv()
    for swap, keep in swaps:
        swap.wait_recv()
        keep.wait()
    w_kept.wait()
    for copy in list(x_first.values()) + list(z_first.values()) + list(z_second.values()):
        copy.wait_send()
    for copy in [x_second, w_x] + [swap for swap, _ in swaps] + w_y + w_z + w_back:
        copy.wait_send()


HALF = (256, 256)
HELD = (
    pltpu.VMEM((32, 4, 8, 16, 128), jnp.int16),
    pltpu.VMEM((8, 1024), F32),
    pltpu.VMEM((1024, 128), F32),
    pltpu.VMEM((8, 2, 128, 512), BF16),
    pltpu.VMEM((4, 128, 512), BF16),
    pltpu.VMEM((4, 256, 128), BF16),
    pltpu.VMEM((1, 512), F32),
    pltpu.VMEM((4096, 256), BF16),
    pltpu.VMEM((4, 40, 512), F32),
    pltpu.VMEM((512, 1024), BF16),
    pltpu.VMEM((512, 1024), BF16),
)
SPREAD = (
    pltpu.SMEM((4, 256), jnp.int32),
    pltpu.SMEM((1, 256), jnp.int32),
    pltpu.VMEM((1024, 128), BF16),
    pltpu.VMEM((8, 2, 128, 512), BF16),
    pltpu.VMEM((8, 128), F32),
    pltpu.VMEM((8, 8, 128), F32),
    pltpu.VMEM((8, 8, 16, 16, 128), jnp.int32),
    pltpu.VMEM((3, 8, 16, 16, 128), jnp.int16),
    pltpu.VMEM((4, 8, 16, 16, 128), jnp.int16),
    pltpu.SMEM((4, 1, 128), jnp.int32),
    pltpu.VMEM((4, 1, 128), jnp.int32),
    pltpu.VMEM((4, 1, 128), jnp.int32),
    pltpu.SMEM((4, 1, 128), jnp.int32),
    pltpu.VMEM((2, 128, 512), BF16),
    DMA((34,)),
    DMA((34,)),
    DMA((8,)),
    DMA((10,)),
)
LAYER = (
    pltpu.VMEM((256, 1024), F32),
    pltpu.VMEM((4, 2, 128, 1024), BF16),
    pltpu.VMEM((4, 128, 1024), BF16),
    pltpu.VMEM((3, 4, 128, 256), BF16),
    pltpu.VMEM((3, 4, 128, 256), BF16),
    pltpu.VMEM((3, 256, 128), BF16),
    pltpu.VMEM((4, 256, 128), BF16),
    pltpu.VMEM((128, 1024), BF16),
    pltpu.VMEM((4, 256, 512), BF16),
    pltpu.VMEM((4, 256, 128), F32),
    pltpu.VMEM((256, 256), BF16),
    DMA((4,)),
    DMA((4,)),
    DMA((12,)),
    DMA((12,)),
    DMA((24,)),
    DMA((24,)),
    DMA,
)
SETTLE = (
    pltpu.VMEM((512, 256), F32),
    pltpu.VMEM((8, 2) + HALF, BF16),
    pltpu.VMEM((2, 3) + HALF, BF16),
    pltpu.VMEM(HALF, BF16),
    pltpu.VMEM(HALF, BF16),
    pltpu.VMEM((4,) + HALF, BF16),
    pltpu.VMEM((3,) + HALF, BF16),
    pltpu.VMEM((3,) + HALF, BF16),
    pltpu.VMEM((1024, 128), F32),
    pltpu.VMEM((2, 512, 128), F32),
    pltpu.VMEM((4, 40, 512), F32),
    pltpu.VMEM((4, 40, 512), F32),
    pltpu.VMEM((40, 512), F32),
    pltpu.VMEM((40, 512), F32),
    pltpu.VMEM((40, 512), F32),
    DMA((26,)),
    DMA((26,)),
    DMA((3,)),
)


def all_kernel(*refs):
    groups, first = [], 0
    for size in (7, 3, len(HELD), len(SPREAD), len(LAYER), len(SETTLE)):
        groups.append(refs[first:first + size])
        first += size
    ins, (act, out, gw), held, spread_refs, layer_refs, settle_refs = groups
    dense, row, col, g, wc, cotr, bias, ball, gwx, a0, a1 = held
    me = Place()
    *arrivals, finish_spread = spread(me, *ins, dense, row, col, g, wc, cotr, bias, *spread_refs)
    finish_layer = layer(
        me, *arrivals, dense, g, row, col, wc, bias, cotr, act, ball, gwx, a0, a1, *layer_refs
    )
    settle(me, dense, col, ball, gwx, out, gw, a0, a1, *settle_refs)
    finish_layer()
    finish_spread()


def results_kernel(act, out, gw, act_out, feat_out, gw_out, gb_out, act_v, feat_v, gw_v, load, store):
    loads = [pltpu.make_async_copy(gw, gw_v, load.at[0])]
    for n in range(2):
        here = slice(n * 512, n * 512 + 512)
        loads.append(pltpu.make_async_copy(act.at[here], act_v.at[here], load.at[1 + n]))
        loads.append(pltpu.make_async_copy(out.at[here], feat_v.at[here], load.at[3 + n]))
    for copy in loads:
        copy.start()
    loads[0].wait()
    stores = [
        pltpu.make_async_copy(gw_v.at[:, 0:32], gw_out, store.at[0]),
        pltpu.make_async_copy(gw_v.at[0, 32:33], gb_out, store.at[1]),
    ]
    for copy in stores:
        copy.start()
    for n in range(2):
        here = slice(n * 512, n * 512 + 512)
        loads[1 + 2 * n].wait()
        stores.append(pltpu.make_async_copy(act_v.at[here], act_out.at[here], store.at[2 + n]))
        stores[-1].start()
        loads[2 + 2 * n].wait()
        stores.append(pltpu.make_async_copy(feat_v.at[here], feat_out.at[here], store.at[4 + n]))
        stores[-1].start()
    for copy in stores:
        copy.wait()


def body(features, weight, bias_vector, cotangent, tile_masks, tile_rows, tile_counts):
    masks = tile_masks.reshape(8, 4, 2, 16, 16, 128)
    act, out, gw = pl.pallas_call(
        all_kernel,
        out_shape=(
            jax.ShapeDtypeStruct((1024, 128), F32),
            jax.ShapeDtypeStruct((2, 512, 128), F32),
            jax.ShapeDtypeStruct((4, 40, 512), F32),
        ),
        in_specs=[HBM] * 7,
        out_specs=(HBM,) * 3,
        scratch_shapes=HELD + SPREAD + LAYER + SETTLE,
        compiler_params=pltpu.CompilerParams(
            collective_id=0, has_side_effects=True, vmem_limit_bytes=VMEM_MIB * MIB
        ),
        name="layer",
    )(tile_rows[0].T, tile_counts, masks, features, weight, bias_vector.reshape(1, 512), cotangent)
    act, out, gw, gb = pl.pallas_call(
        results_kernel,
        out_shape=(
            jax.ShapeDtypeStruct((1024, 128), F32),
            jax.ShapeDtypeStruct((1024, 128), F32),
            jax.ShapeDtypeStruct((4, 32, 512), F32),
            jax.ShapeDtypeStruct((1, 512), F32),
        ),
        in_specs=[HBM] * 3,
        out_specs=(HBM,) * 4,
        scratch_shapes=[
            pltpu.VMEM((1024, 128), F32),
            pltpu.VMEM((1024, 128), F32),
            pltpu.VMEM((4, 40, 512), F32),
            DMA((5,)),
            DMA((6,)),
        ],
        compiler_params=pltpu.CompilerParams(vmem_limit_bytes=VMEM_MIB * MIB),
        name="results",
    )(act, out.reshape(1024, 128), gw)
    return act, out, gw.reshape(128, 512), gb.reshape(512)


def solution(mesh):
    return jax.shard_map(
        body,
        mesh=mesh,
        in_specs=(
            P("blk", "rep"),
            P("rep", None),
            P(),
            P("blk", "rep"),
            P("blk", None, None, None, None),
            P("blk", None, None),
            P("blk", None),
        ),
        out_specs=(P("blk", "rep"), P("blk", "rep"), P("rep", None), P()),
        check_vma=False,
    )
```

```python
import functools

import jax
import jax.numpy as jnp
from jax import lax
from jax.experimental import pallas as pl
from jax.experimental.pallas import tpu as pltpu
from jax.sharding import PartitionSpec as P

MESH = pl.DeviceIdType.MESH
BF16 = jnp.bfloat16
F32 = jnp.float32
HBM = pl.BlockSpec(memory_space=pltpu.HBM)
DMA = pltpu.SemaphoreType.DMA
MIB = 2**20
VMEM_MIB = 60


class Place:
    def __init__(self):
        blk = lax.axis_index("blk")
        rep = lax.axis_index("rep")
        self.x, self.z, self.y = blk // 16, lax.rem(blk // 4, 4), lax.rem(blk, 4)
        self.xl, self.c = rep // 2, lax.rem(rep, 2)
        self.rep = rep
        self.xz = self.x * 4 + self.z

    def at(self, x=None, z=None, y=None, xl=None, c=None):
        x = self.x if x is None else x
        z = self.z if z is None else z
        y = self.y if y is None else y
        xl = self.xl if xl is None else xl
        c = self.c if c is None else c
        return (x * 16 + z * 4 + y, xl * 2 + c)

    def dy(self, n):
        return lax.rem(self.y + n, 4)

    def dz(self, n):
        return lax.rem(self.z + n, 4)

    def column(self, n):
        return lax.rem(self.x + n // 4, 2) * 4 + self.dz(4 - lax.rem(n, 4))


class Copies:
    def __init__(self, send, recv):
        self.send, self.recv, self.used = send, recv, []

    def start(self, src, dst, peer):
        copy = self.make(src, dst, peer)
        copy.start()
        return copy

    def make(self, src, dst, peer):
        n = len(self.used)
        copy = pltpu.make_async_remote_copy(
            src_ref=src, dst_ref=dst, send_sem=self.send.at[n], recv_sem=self.recv.at[n],
            device_id=peer, device_id_type=MESH,
        )
        self.used.append(copy)
        return copy

    def wait_sends(self):
        for copy in self.used:
            copy.wait_send()


Y_ORDER = (2, 1, 3, 0)
ROWS = (2, 1, 3, 0)


def spread(me, rows_hbm, counts_hbm, masks, feat_hbm, w, bias_hbm, cot, dense, row, col, gs, wc, cotr, bias,
           rows_ref, counts_ref, feat, g, inv_s, scale, words, m16, rm, slots_s, slots_v, landed_v, landed_s, xt, send, recv, load, local):
    own, other = me.c, 1 - me.c
    small = [
        pltpu.make_async_copy(rows_hbm, rows_ref, local.at[6]),
        pltpu.make_async_copy(counts_hbm, counts_ref, local.at[7]),
    ]
    for copy in small:
        copy.start()
    loads = []
    for q in range(8):
        half = own if q < 4 else other
        loads.append(pltpu.make_async_copy(masks.at[:, me.dy(Y_ORDER[q % 4]), half], words.at[q], load.at[q]))
        loads[q].start()
    feat_load = pltpu.make_async_copy(feat_hbm, feat, local.at[8])
    feat_load.start()

    sibling = me.at(c=1 - me.c)
    x_peer = me.at(x=1 - me.x)
    z_peers = [me.at(z=me.dz(n)) for n in (1, 2, 3)]
    y_peers = [me.at(y=me.dy(n)) for n in (1, 2, 3)]
    rep_peers = [sibling, me.at(xl=1 - me.xl), me.at(xl=1 - me.xl, c=1 - me.c)]
    xz_peers = z_peers + [x_peer] + [me.at(x=1 - me.x, z=me.dz(n)) for n in (1, 2, 3)]
    everyone = xz_peers + y_peers + rep_peers
    barrier = pltpu.get_barrier_semaphore()
    for peer in everyone:
        pl.semaphore_signal(barrier, inc=1, device_id=peer, device_id_type=MESH)

    def narrow(q):
        loads[q].wait()

        def tiles(xz, _):
            for slot in range(16):
                tile = words[q, xz, slot].astype(jnp.int16)
                if q < 3:
                    m16[q, xz, slot] = tile
                else:
                    rm[me.y, xz, slot] = tile
            return 0

        lax.fori_loop(0, 8, tiles, 0)

    for copy in small:
        copy.wait()

    def fill(xz, _):
        for q in range(4):
            first = ((xz * 4 + me.dy(Y_ORDER[q])) * 2 + own) * 4
            for tc in range(4):
                count = counts_ref[0, first + tc]
                for s in range(4):
                    slots_s[q, 0, xz * 16 + tc * 4 + s] = jnp.where(s < count, rows_ref[s, first + tc], 8)
        return 0

    lax.fori_loop(0, 8, fill, 0)
    to_vmem = pltpu.make_async_copy(slots_s, slots_v, local.at[2])
    to_vmem.start()

    place = lax.broadcasted_iota(jnp.int32, (128, 128), 1)
    source = 8 * jnp.bitwise_and(place, 15) + jnp.right_shift(place, 4)
    perm = jnp.where(lax.broadcasted_iota(jnp.int32, (128, 128), 0) == source, 1.0, 0.0).astype(BF16)
    feat_load.wait()
    for t in range(8):
        turned = feat[t * 128:(t + 1) * 128, :].astype(F32).T.astype(BF16)
        moved = jnp.dot(turned, perm, preferred_element_type=F32).astype(BF16)
        xt[t // 4, :, (t % 4) * 128:(t % 4 + 1) * 128] = moved
    narrow(0)
    to_vmem.wait()
    pl.semaphore_wait(barrier, len(everyone))
    copies = Copies(send, recv)

    def cot_rows(rep):
        return cot.at[pl.ds(pl.multiple_of(rep * 256, 256), 256), :]

    def at(core, xz):
        return g.at[xz, core]

    slot_copies = [copies.start(slots_v.at[q], landed_v.at[me.y], y_peers[Y_ORDER[q] - 1]) for q in range(3)]
    to_sibling = copies.start(xt.at[other], at(own, me.xz), sibling)
    first = [copies.start(xt.at[own], at(own, me.xz), p) for p in z_peers]
    across = copies.start(xt.at[own], at(own, me.xz), x_peer)
    mask_copies = [copies.start(m16.at[0], rm.at[me.y], y_peers[Y_ORDER[0] - 1])]
    stays = [
        pltpu.make_async_copy(xt.at[own], at(own, me.xz), local.at[0]),
        pltpu.make_async_copy(w, wc.at[me.rep], local.at[1]),
        pltpu.make_async_copy(cot_rows(me.rep), cotr.at[me.rep], local.at[5]),
        pltpu.make_async_copy(bias_hbm, bias, local.at[9]),
    ]
    for copy in stays:
        copy.start()
    kept = pltpu.make_async_copy(slots_v.at[3], landed_v.at[me.y], local.at[3])
    kept.start()
    tile_row = lax.broadcasted_iota(jnp.int32, (8, 128), 0)

    def scan(q, degrees):
        n = Y_ORDER[q % 4]
        half = own if q < 4 else other
        if q >= 4:
            loads[q].wait()

        def tiles(xz, degrees):
            first = ((xz * 4 + me.dy(n)) * 2 + half) * 4
            for tc in range(4):
                count = counts_ref[0, first + tc]
                for s in range(4):
                    t = jnp.where(s < count, rows_ref[s, first + tc], 8)
                    tile = words[q, xz, tc * 4 + s]
                    joined = jnp.bitwise_or(tile[:8], jnp.left_shift(tile[8:], 8))
                    counted = jnp.sum(lax.population_count(joined), axis=0, keepdims=True)
                    degrees = degrees + jnp.where(tile_row == t, counted, 0)
            return degrees

        return lax.fori_loop(0, 8, tiles, degrees)

    degrees = scan(0, jnp.zeros((8, 128), jnp.int32))
    narrow(1)
    to_sibling.wait_recv()
    other_x = copies.start(at(other, me.xz), at(other, me.xz), x_peer)
    second = [copies.start(at(other, me.xz), at(other, me.xz), p) for p in z_peers]
    degrees = scan(1, degrees)
    narrow(2)
    for q in (1, 2):
        mask_copies.append(copies.start(m16.at[q], rm.at[me.y], y_peers[Y_ORDER[q] - 1]))
    early = []
    for peer in rep_peers:
        early.append(copies.make(cot_rows(peer[1]), cotr.at[me.rep], peer))
        early.append(copies.make(w, wc.at[me.rep], peer))
    narrow(3)
    for q in (2, 3, 4):
        degrees = scan(q, degrees)
    last = []
    for n in (1, 2, 3):
        first[n - 1].wait_recv()
        source = me.x * 4 + me.dz(4 - n)
        last.append(copies.start(at(own, source), at(own, source), x_peer))
    for q in (5, 6, 7):
        degrees = scan(q, degrees)

    degrees = 1.0 + degrees.astype(F32)
    high = jnp.floor(degrees * (1.0 / 256.0))
    low = degrees - high * 256.0
    placed = 256.0 * jnp.dot(high.astype(BF16), perm, preferred_element_type=F32)
    placed = placed + jnp.dot(low.astype(BF16), perm, preferred_element_type=F32)
    inv_s[...] = lax.rsqrt(placed)
    inv_copies = [copies.start(inv_s, scale.at[me.xz], peer) for peer in xz_peers]
    inv = lax.rsqrt(degrees)
    other_x.wait_recv()
    far = (1 - me.x) * 4 + me.z
    last += [copies.start(at(other, far), at(other, far), p) for p in z_peers]
    scale[me.xz] = inv_s[...]
    for t in range(8):
        lanes = inv[t:t + 1, :]
        row[:, t * 128:(t + 1) * 128] = jnp.broadcast_to(lanes, (8, 128))
        col[t * 128:(t + 1) * 128, :] = jnp.broadcast_to(lanes, (128, 128)).T

    def put_tiles(n, slot_rows, at):
        i = me.dy(n)

        def column(j, _):
            for tc in range(4):
                rows = [slot_rows[at, 0, j * 16 + tc * 4 + s] for s in range(4)]
                tiles = [rm[i, j, tc * 4 + s] for s in range(4)]
                for t in range(8):
                    found = jnp.zeros((16, 128), jnp.int16)
                    for s in range(4):
                        found = jnp.where(rows[s] == t, tiles[s], found)
                    dense[i * 8 + j, tc, t] = found
            return 0

        lax.fori_loop(0, 8, column, 0)

    put_tiles(0, slots_s, 3)

    def arrive(column):
        n = column % 4
        if column == 0:
            stays[0].wait()
        elif column < 4:
            second[n - 1].wait_recv()
        elif column == 4:
            across.wait_recv()
        else:
            last[n - 1].wait_recv()
            last[n + 2].wait_recv()
        if column:
            inv_copies[column - 1].wait_recv()
        xz = me.column(column)
        for t in range(4):
            lanes = slice(t * 128, (t + 1) * 128)
            factor = scale[xz, pl.ds(own * 4 + t, 1), :]
            for core in range(2):
                gs[xz, core, :, lanes] = (g[xz, core, :, lanes].astype(F32) * factor).astype(BF16)

    def slots():
        kept.wait()
        for copy in slot_copies:
            copy.wait_recv()
        to_smem = pltpu.make_async_copy(landed_v, landed_s, local.at[4])
        to_smem.start()
        to_smem.wait()

    def place_tiles(n):
        q = Y_ORDER.index(4 - n)
        mask_copies[q].wait_recv()
        put_tiles(n, landed_s, me.dy(n))

    def send_parameters():
        for copy in early:
            copy.start()

    def parameters():
        for copy in early:
            copy.wait_recv()
        for copy in stays[1:]:
            copy.wait()

    return arrive, slots, place_tiles, send_parameters, parameters, copies.wait_sends


def table(values, step):
    found = values[-1]
    for n in range(len(values) - 1):
        found = jnp.where(step == n, values[n], found)
    return found


def unpack(dense, i, j, out_ref):
    one, zero = jnp.asarray(1, BF16), jnp.asarray(0, BF16)
    for tc in range(4):
        for t in range(8):
            words = dense[i * 8 + j, tc, t]
            for k in range(8):
                bits = jnp.where(jnp.bitwise_and(words, jnp.int16(1 << k)) != 0, one, zero)
                first = tc * 128 + k * 16
                out_ref[first:first + 16, t * 128:(t + 1) * 128] = bits


def layer(me, arrive, slots, place_tiles, send_parameters, parameters, dense, g, row, col, wc, bias, cotr, act, ball, gwx, a0, a1,
          acc, part, rc, snd, ry, agg_s, agg, agg_t, slope, act_s, back_s,
          core_s, core_r, sum_s, sum_r, send, recv, local):
    sibling = me.at(c=1 - me.c)
    xl_peer = me.at(xl=1 - me.xl)
    xl_other = me.at(xl=1 - me.xl, c=1 - me.c)
    y_peers = [me.at(y=me.dy(n)) for n in (1, 2, 3)]
    copies = Copies(send, recv)
    own, other = me.c, 1 - me.c

    def to_sibling(s):
        return pltpu.make_async_remote_copy(
            src_ref=part.at[s, other], dst_ref=rc.at[s], send_sem=core_s.at[s], recv_sem=core_r.at[s],
            device_id=sibling, device_id_type=MESH,
        )

    def rows_of(m):
        return pl.ds(pl.multiple_of(m * 256, 256), 256)

    def to_owner(k, m):
        return pltpu.make_async_remote_copy(
            src_ref=snd.at[k, m], dst_ref=ry.at[k, m], send_sem=sum_s.at[k * 4 + m], recv_sem=sum_r.at[k * 4 + m],
            device_id=me.at(y=me.dy(table((2, 1, 3), k))), device_id_type=MESH,
        )

    def pass_on(k):
        to_sibling(k).wait_recv()
        for m in range(4):
            rows = slice(m * 256, (m + 1) * 256)
            snd[k, m] = (part[k, own, :, rows].astype(F32) + rc[k, :, rows].astype(F32)).astype(BF16)
            to_owner(k, m).start()

    def chunk(c):
        return me.dy(table(ROWS, c // 8)), me.column(lax.rem(c, 8))

    slots()
    place_tiles(ROWS[0])
    bufs = (a0, a1)
    unpack(dense, *chunk(0), a0)

    def two_chunks(n, _):
        k, pair = n // 4, lax.rem(n, 4)
        for step in range(4):
            @pl.when(n == step)
            def _():
                arrive(step * 2)
                arrive(step * 2 + 1)

        for step in (1, 2):
            @pl.when(n == step * 4 - 1)
            def _():
                if step == 1:
                    send_parameters()
                place_tiles(ROWS[step])

        for h in range(2):
            unpack(dense, *chunk(jnp.minimum(n * 2 + h + 1, 31)), bufs[1 - h])
            prod = jnp.dot(g[me.column(pair * 2 + h)].reshape(256, 512), bufs[h][...], preferred_element_type=F32)
            if h == 0:
                acc[...] = jnp.where(pair == 0, 0.0, acc[...]) + prod
            else:
                acc[...] += prod

        @pl.when(pair == 3)
        def _():
            part[k, 0] = acc[0:128].astype(BF16)
            part[k, 1] = acc[128:256].astype(BF16)
            to_sibling(k).start()

        @pl.when(jnp.logical_and(pair == 0, k >= 1))
        def _():
            pass_on(k - 1)

        return 0

    lax.fori_loop(0, 16, two_chunks, 0)
    to_sibling(3).wait_recv()

    def finish_sum(m, out):
        for k in range(3):
            to_owner(k, m).wait_recv()
        rows = rows_of(m)
        total = part[3, own, :, rows].astype(F32) + rc[3, :, rows].astype(F32)
        for k in range(3):
            total = total + ry[k, m].astype(F32)
        total = total * row[0:1, rows]
        agg_t[:, rows] = total.astype(BF16)
        out[...] = total.T.astype(BF16)

    swaps = []
    peers = (xl_peer, xl_other, sibling)
    for n in range(3):
        finish_sum(peers[n][1], agg_s.at[n])
        swaps.append(copies.start(agg_s.at[n], agg.at[me.rep], peers[n]))
    finish_sum(me.rep, agg.at[me.rep])
    parameters()
    for copy in reversed(swaps):
        copy.wait_recv()

    for half in range(2):
        rows = slice(half * 128, (half + 1) * 128)
        hidden = jnp.dot(agg[0, rows, :], wc[0], preferred_element_type=F32)
        for q in range(1, 4):
            hidden = hidden + jnp.dot(agg[q, rows, :], wc[q], preferred_element_type=F32)
        hidden = hidden + bias[...]
        logistic = jax.nn.sigmoid(hidden)
        value = hidden * logistic
        factor = logistic * (1.0 + hidden * (1.0 - logistic))
        for q in range(4):
            lanes = slice(q * 128, (q + 1) * 128)
            act_s[q, rows, :] = value[:, lanes]
            slope[me.rep, rows, lanes] = (cotr[q, rows, :].astype(F32) * factor[:, lanes]).astype(BF16)

    def block(y, rep):
        return ball.at[pl.ds(pl.multiple_of(y * 1024 + rep * 256, 256), 256), :]

    def back_into(xl, out):
        for core in range(2):
            value = lax.dot_general(
                slope[me.rep], wc[xl * 2 + core], (((1,), (1,)), ((), ())), preferred_element_type=F32
            )
            out[:, core * 128:(core + 1) * 128] = (value * col[rows_of(me.rep), :]).astype(BF16)

    theirs = (1 - me.xl) * 2 + me.c
    back_into(1 - me.xl, back_s)
    from_xl = copies.start(back_s, block(me.y, me.rep), xl_peer)
    back_into(me.xl, block(me.y, me.rep))

    def send_block(rep):
        here = block(me.y, rep)
        return [copies.start(here, here, y_peers[n - 1]) for n in (2, 1, 3)] + [copies.start(here, here, sibling)]

    mine = send_block(me.rep)
    slope_far = copies.start(slope.at[me.rep], slope.at[me.rep], xl_peer)
    slope_near = copies.start(slope.at[me.rep], slope.at[me.rep], sibling)
    from_xl.wait_recv()
    passed = send_block(theirs)
    acts = [
        copies.start(act_s.at[peer[1]], act.at[rows_of(me.rep), :], peer)
        for peer in (xl_peer, xl_other, sibling)
    ]
    act_kept = pltpu.make_async_copy(act_s.at[me.rep], act.at[rows_of(me.rep), :], local)
    act_kept.start()
    slope_far.wait_recv()
    slope_relay = copies.start(slope.at[theirs], slope.at[theirs], sibling)

    relays = []
    for sent, rep in ((mine, me.rep), (passed, theirs)):
        if rep is theirs:
            slope_near.wait_recv()
            slope_relay.wait_recv()
            ones = jnp.ones((8, 256), BF16)
            grad = jnp.zeros((128, 512), F32)
            gb = jnp.zeros((8, 512), F32)
            for q in range(4):
                grad = grad + jnp.dot(agg_t[:, q * 256:(q + 1) * 256], slope[q], preferred_element_type=F32)
                gb = gb + jnp.dot(ones, slope[q], preferred_element_type=F32)
            for n in range(4):
                gwx[n, 0:32, :] = grad[n * 32:(n + 1) * 32]
                gwx[n, 32:40, :] = gb
        for n, copy in zip((2, 1, 3), sent):
            copy.wait_recv()
            here = block(me.dy(4 - n), rep)
            relays.append(copies.start(here, here, sibling))
    for copy in [mine[3], passed[3]] + relays:
        copy.wait_recv()

    def finish():
        for copy in acts:
            copy.wait_recv()
        act_kept.wait()
        copies.wait_sends()
        for k in range(3):
            for m in range(4):
                to_owner(k, m).wait_send()
        for k in range(4):
            to_sibling(k).wait_send()

    return finish


SPLIT = 192
BLOCKS = ((1, 2), (1, 1), (1, 3), (1, 0), (0, 2), (0, 1), (0, 3), (0, 0))
ORDER = {key: n for n, key in enumerate(BLOCKS)}


def settle(me, dense, col, ball, gwx, out, gw, a0, a1,
           acc, part_a, part_b, az, a_sum, ax, bx, b_sum, bz, hold, final, wy, wz, wx_send, wx, gw_own, send, recv, local):
    sibling = me.at(c=1 - me.c)
    x_peer = me.at(x=1 - me.x)
    z_peers = [me.at(z=me.dz(n)) for n in (1, 2, 3)]
    y_peers = [me.at(y=me.dy(n)) for n in (1, 2, 3)]

    def remote(n, src, dst, peer):
        return pltpu.make_async_remote_copy(
            src_ref=src, dst_ref=dst, send_sem=send.at[n], recv_sem=recv.at[n],
            device_id=peer, device_id_type=MESH,
        )

    x_first = {n: remote(n, part_b.at[ORDER[1, n]], bx.at[n], x_peer) for n in range(4)}
    z_first = {
        (side, n): remote(4 + side * 3 + n - 1, part_a.at[ORDER[side, n]], az.at[side, n - 1], z_peers[n - 1])
        for side in range(2) for n in (1, 2, 3)
    }
    z_second = {n: remote(9 + n, b_sum.at[n - 1], bz.at[n - 1], z_peers[n - 1]) for n in (1, 2, 3)}
    x_second = remote(13, a_sum, ax, x_peer)
    w_y = [remote(13 + n, gwx.at[me.dy(n)], wy.at[me.y], y_peers[n - 1]) for n in (1, 2, 3)]
    w_z = [remote(16 + n, wz.at[me.z], wz.at[me.z], z_peers[n - 1]) for n in (1, 2, 3)]
    w_x = remote(20, wx_send, wx, x_peer)
    w_back = [remote(20 + n, gw_own, gw.at[me.y], y_peers[n - 1]) for n in (1, 2, 3)]
    w_kept = pltpu.make_async_copy(gw_own, gw.at[me.y], local.at[0])

    def pass_b(n):
        x_first[n].wait_recv()
        b_sum[n - 1] = (part_b[ORDER[0, n]].astype(F32) + bx[n].astype(F32)).astype(BF16)
        z_second[n].start()

    def pass_a():
        total = part_a[ORDER[1, 0]].astype(F32)
        for n in (1, 2, 3):
            z_first[1, n].wait_recv()
            total = total + az[1, n - 1].astype(F32)
        a_sum[...] = total.astype(BF16)
        x_second.start()

    def weights_z():
        for copy in w_y:
            copy.wait_recv()
        wz[me.z] = (wy[0] + wy[1]) + (wy[2] + wy[3])
        for copy in w_z:
            copy.start()

    def weights_x():
        for copy in w_z:
            copy.wait_recv()
        wx_send[...] = (wz[0] + wz[1]) + (wz[2] + wz[3])
        w_x.start()

    def weights_back():
        w_x.wait_recv()
        gw_own[...] = wx_send[...] + wx[...]
        w_kept.start()
        for copy in w_back:
            copy.start()

    actions = {n: [] for n in range(8)}
    for n in range(4):
        actions[ORDER[1, n]].append(x_first[n].start)
    for n in (2, 1, 3):
        actions[ORDER[0, n]].append(functools.partial(pass_b, n))
    for key, copy in z_first.items():
        actions[ORDER[key]].append(copy.start)
    actions[3].append(weights_z)
    actions[4].append(pass_a)
    actions[5].append(weights_x)
    actions[6].append(weights_back)

    for copy in w_y:
        copy.start()
    wy[me.y] = gwx[me.y]

    def chunk(c):
        at = c // 4
        x = lax.rem(me.x + table([block[0] for block in BLOCKS], at), 2)
        z = lax.rem(me.z + table([block[1] for block in BLOCKS], at), 4)
        return lax.rem(c, 4), x * 4 + z

    bufs = (a0, a1)
    unpack(dense, *chunk(0), a0)

    def two_chunks(step, _):
        block, pair = step // 2, lax.rem(step, 2)
        for h in range(2):
            unpack(dense, *chunk(jnp.minimum(step * 2 + h + 1, 31)), bufs[1 - h])
            prod = jnp.dot(bufs[h][...], ball[pl.ds(pl.multiple_of((pair * 2 + h) * 1024, 1024), 1024), :], preferred_element_type=F32)
            if h == 0:
                acc[...] = jnp.where(pair == 0, 0.0, acc[...]) + prod
            else:
                acc[...] += prod

        @pl.when(pair == 1)
        def _():
            part_a[block] = acc[0:SPLIT].astype(BF16)
            part_b[block] = acc[SPLIT:512].astype(BF16)

        for at, calls in actions.items():
            if calls:
                @pl.when(step == at * 2 + 1)
                def _():
                    for call in calls:
                        call()

        return 0

    lax.fori_loop(0, 16, two_chunks, 0)

    def keep_rows(first, total):
        for q in range(2):
            hold[q * 512 + first:q * 512 + first + total.shape[0], :] = total[:, q * 128:(q + 1) * 128]

    def place(tile):
        here = slice(tile * 128, tile * 128 + 256)
        for t in range(tile, tile + 2):
            for w in range(16):
                first = t * 128 + w * 8
                scale = col[pl.ds(pl.multiple_of(me.c * 512 + first, 8), 8), :]
                for q in range(2):
                    final[q, first:first + 8, :] = hold[pl.ds(q * 512 + t * 128 + w, 8, stride=16), :] * scale
        at = tile // 2
        swap = remote(24 + at, final.at[1 - me.c, here], out.at[me.c, here], sibling)
        keep = pltpu.make_async_copy(final.at[me.c, here], out.at[me.c, here], local.at[1 + at])
        swap.start()
        keep.start()
        return swap, keep

    total = part_b[ORDER[0, 0]].astype(F32)
    x_first[0].wait_recv()
    total = total + bx[0].astype(F32)
    for n in (1, 2, 3):
        z_second[n].wait_recv()
        total = total + bz[n - 1].astype(F32)
    keep_rows(SPLIT, total)
    swaps = [place(2)]
    total = part_a[ORDER[0, 0]].astype(F32)
    for n in (1, 2, 3):
        z_first[0, n].wait_recv()
        total = total + az[0, n - 1].astype(F32)
    x_second.wait_recv()
    total = total + ax[...].astype(F32)
    keep_rows(0, total)
    swaps.append(place(0))
    for copy in w_back:
        copy.wait_recv()
    for swap, keep in swaps:
        swap.wait_recv()
        keep.wait()
    w_kept.wait()
    for copy in list(x_first.values()) + list(z_first.values()) + list(z_second.values()):
        copy.wait_send()
    for copy in [x_second, w_x] + [swap for swap, _ in swaps] + w_y + w_z + w_back:
        copy.wait_send()


PART_A, PART_B = (SPLIT, 256), (512 - SPLIT, 256)
HELD = (
    pltpu.VMEM((32, 4, 8, 16, 128), jnp.int16),
    pltpu.VMEM((8, 1024), F32),
    pltpu.VMEM((1024, 128), F32),
    pltpu.VMEM((8, 2, 128, 512), BF16),
    pltpu.VMEM((4, 128, 512), BF16),
    pltpu.VMEM((4, 256, 128), BF16),
    pltpu.VMEM((1, 512), F32),
    pltpu.VMEM((4096, 256), BF16),
    pltpu.VMEM((4, 40, 512), F32),
    pltpu.VMEM((512, 1024), BF16),
    pltpu.VMEM((512, 1024), BF16),
)
SPREAD = (
    pltpu.SMEM((4, 256), jnp.int32),
    pltpu.SMEM((1, 256), jnp.int32),
    pltpu.VMEM((1024, 128), BF16),
    pltpu.VMEM((8, 2, 128, 512), BF16),
    pltpu.VMEM((8, 128), F32),
    pltpu.VMEM((8, 8, 128), F32),
    pltpu.VMEM((8, 8, 16, 16, 128), jnp.int32),
    pltpu.VMEM((3, 8, 16, 16, 128), jnp.int16),
    pltpu.VMEM((4, 8, 16, 16, 128), jnp.int16),
    pltpu.SMEM((4, 1, 128), jnp.int32),
    pltpu.VMEM((4, 1, 128), jnp.int32),
    pltpu.VMEM((4, 1, 128), jnp.int32),
    pltpu.SMEM((4, 1, 128), jnp.int32),
    pltpu.VMEM((2, 128, 512), BF16),
    DMA((34,)),
    DMA((34,)),
    DMA((8,)),
    DMA((10,)),
)
LAYER = (
    pltpu.VMEM((256, 1024), F32),
    pltpu.VMEM((4, 2, 128, 1024), BF16),
    pltpu.VMEM((4, 128, 1024), BF16),
    pltpu.VMEM((3, 4, 128, 256), BF16),
    pltpu.VMEM((3, 4, 128, 256), BF16),
    pltpu.VMEM((3, 256, 128), BF16),
    pltpu.VMEM((4, 256, 128), BF16),
    pltpu.VMEM((128, 1024), BF16),
    pltpu.VMEM((4, 256, 512), BF16),
    pltpu.VMEM((4, 256, 128), F32),
    pltpu.VMEM((256, 256), BF16),
    DMA((4,)),
    DMA((4,)),
    DMA((12,)),
    DMA((12,)),
    DMA((24,)),
    DMA((24,)),
    DMA,
)
SETTLE = (
    pltpu.VMEM((512, 256), F32),
    pltpu.VMEM((8,) + PART_A, BF16),
    pltpu.VMEM((8,) + PART_B, BF16),
    pltpu.VMEM((2, 3) + PART_A, BF16),
    pltpu.VMEM(PART_A, BF16),
    pltpu.VMEM(PART_A, BF16),
    pltpu.VMEM((4,) + PART_B, BF16),
    pltpu.VMEM((3,) + PART_B, BF16),
    pltpu.VMEM((3,) + PART_B, BF16),
    pltpu.VMEM((1024, 128), F32),
    pltpu.VMEM((2, 512, 128), F32),
    pltpu.VMEM((4, 40, 512), F32),
    pltpu.VMEM((4, 40, 512), F32),
    pltpu.VMEM((40, 512), F32),
    pltpu.VMEM((40, 512), F32),
    pltpu.VMEM((40, 512), F32),
    DMA((26,)),
    DMA((26,)),
    DMA((3,)),
)


def all_kernel(*refs):
    groups, first = [], 0
    for size in (7, 3, len(HELD), len(SPREAD), len(LAYER), len(SETTLE)):
        groups.append(refs[first:first + size])
        first += size
    ins, (act, out, gw), held, spread_refs, layer_refs, settle_refs = groups
    dense, row, col, g, wc, cotr, bias, ball, gwx, a0, a1 = held
    me = Place()
    *arrivals, finish_spread = spread(me, *ins, dense, row, col, g, wc, cotr, bias, *spread_refs)
    finish_layer = layer(
        me, *arrivals, dense, g, row, col, wc, bias, cotr, act, ball, gwx, a0, a1, *layer_refs
    )
    settle(me, dense, col, ball, gwx, out, gw, a0, a1, *settle_refs)
    finish_layer()
    finish_spread()


def results_kernel(act, out, gw, act_out, feat_out, gw_out, gb_out, act_v, feat_v, gw_v, load, store):
    loads = [pltpu.make_async_copy(gw, gw_v, load.at[0])]
    for n in range(2):
        here = slice(n * 512, n * 512 + 512)
        loads.append(pltpu.make_async_copy(act.at[here], act_v.at[here], load.at[1 + n]))
        loads.append(pltpu.make_async_copy(out.at[here], feat_v.at[here], load.at[3 + n]))
    for copy in loads:
        copy.start()
    loads[0].wait()
    stores = [
        pltpu.make_async_copy(gw_v.at[:, 0:32], gw_out, store.at[0]),
        pltpu.make_async_copy(gw_v.at[0, 32:33], gb_out, store.at[1]),
    ]
    for copy in stores:
        copy.start()
    for n in range(2):
        here = slice(n * 512, n * 512 + 512)
        loads[1 + 2 * n].wait()
        stores.append(pltpu.make_async_copy(act_v.at[here], act_out.at[here], store.at[2 + n]))
        stores[-1].start()
        loads[2 + 2 * n].wait()
        stores.append(pltpu.make_async_copy(feat_v.at[here], feat_out.at[here], store.at[4 + n]))
        stores[-1].start()
    for copy in stores:
        copy.wait()


def body(features, weight, bias_vector, cotangent, tile_masks, tile_rows, tile_counts):
    masks = tile_masks.reshape(8, 4, 2, 16, 16, 128)
    act, out, gw = pl.pallas_call(
        all_kernel,
        out_shape=(
            jax.ShapeDtypeStruct((1024, 128), F32),
            jax.ShapeDtypeStruct((2, 512, 128), F32),
            jax.ShapeDtypeStruct((4, 40, 512), F32),
        ),
        in_specs=[HBM] * 7,
        out_specs=(HBM,) * 3,
        scratch_shapes=HELD + SPREAD + LAYER + SETTLE,
        compiler_params=pltpu.CompilerParams(
            collective_id=0, has_side_effects=True, vmem_limit_bytes=VMEM_MIB * MIB
        ),
        name="layer",
    )(tile_rows[0].T, tile_counts, masks, features, weight, bias_vector.reshape(1, 512), cotangent)
    act, out, gw, gb = pl.pallas_call(
        results_kernel,
        out_shape=(
            jax.ShapeDtypeStruct((1024, 128), F32),
            jax.ShapeDtypeStruct((1024, 128), F32),
            jax.ShapeDtypeStruct((4, 32, 512), F32),
            jax.ShapeDtypeStruct((1, 512), F32),
        ),
        in_specs=[HBM] * 3,
        out_specs=(HBM,) * 4,
        scratch_shapes=[
            pltpu.VMEM((1024, 128), F32),
            pltpu.VMEM((1024, 128), F32),
            pltpu.VMEM((4, 40, 512), F32),
            DMA((5,)),
            DMA((6,)),
        ],
        compiler_params=pltpu.CompilerParams(vmem_limit_bytes=VMEM_MIB * MIB),
        name="results",
    )(act, out.reshape(1024, 128), gw)
    return act, out, gw.reshape(128, 512), gb.reshape(512)


def solution(mesh):
    return jax.shard_map(
        body,
        mesh=mesh,
        in_specs=(
            P("blk", "rep"),
            P("rep", None),
            P(),
            P("blk", "rep"),
            P("blk", None, None, None, None),
            P("blk", None, None),
            P("blk", None),
        ),
        out_specs=(P("blk", "rep"), P("blk", "rep"), P("rep", None), P()),
        check_vma=False,
    )
```

```python
import functools

import jax
import jax.numpy as jnp
from jax import lax
from jax.experimental import pallas as pl
from jax.experimental.pallas import tpu as pltpu
from jax.sharding import PartitionSpec as P

MESH = pl.DeviceIdType.MESH
BF16 = jnp.bfloat16
F32 = jnp.float32
HBM = pl.BlockSpec(memory_space=pltpu.HBM)
DMA = pltpu.SemaphoreType.DMA
MIB = 2**20
VMEM_MIB = 60


class Place:
    def __init__(self):
        blk = lax.axis_index("blk")
        rep = lax.axis_index("rep")
        self.x, self.z, self.y = blk // 16, lax.rem(blk // 4, 4), lax.rem(blk, 4)
        self.xl, self.c = rep // 2, lax.rem(rep, 2)
        self.rep = rep
        self.xz = self.x * 4 + self.z

    def at(self, x=None, z=None, y=None, xl=None, c=None):
        x = self.x if x is None else x
        z = self.z if z is None else z
        y = self.y if y is None else y
        xl = self.xl if xl is None else xl
        c = self.c if c is None else c
        return (x * 16 + z * 4 + y, xl * 2 + c)

    def dy(self, n):
        return lax.rem(self.y + n, 4)

    def dz(self, n):
        return lax.rem(self.z + n, 4)

    def column(self, n):
        return lax.rem(self.x + n // 4, 2) * 4 + self.dz(4 - lax.rem(n, 4))


class Copies:
    def __init__(self, send, recv):
        self.send, self.recv, self.used = send, recv, []

    def start(self, src, dst, peer):
        copy = self.make(src, dst, peer)
        copy.start()
        return copy

    def make(self, src, dst, peer):
        n = len(self.used)
        copy = pltpu.make_async_remote_copy(
            src_ref=src, dst_ref=dst, send_sem=self.send.at[n], recv_sem=self.recv.at[n],
            device_id=peer, device_id_type=MESH,
        )
        self.used.append(copy)
        return copy

    def wait_sends(self):
        for copy in self.used:
            copy.wait_send()


Y_ORDER = (2, 1, 3, 0)
ROWS = (2, 1, 3, 0)


def spread(me, rows_hbm, counts_hbm, masks, feat_hbm, w, bias_hbm, cot, dense, row, col, gs, wc, cotr, bias,
           rows_ref, counts_ref, feat, g, inv_s, scale, words, m16, rm, slots_s, slots_v, landed_v, landed_s, xt, send, recv, load, local):
    own, other = me.c, 1 - me.c
    feat_load = pltpu.make_async_copy(feat_hbm, feat, local.at[8])
    feat_load.start()
    small = [
        pltpu.make_async_copy(rows_hbm, rows_ref, local.at[6]),
        pltpu.make_async_copy(counts_hbm, counts_ref, local.at[7]),
    ]
    for copy in small:
        copy.start()
    loads = []
    for q in range(8):
        half = own if q < 4 else other
        loads.append(pltpu.make_async_copy(masks.at[:, me.dy(Y_ORDER[q % 4]), half], words.at[q], load.at[q]))
        loads[q].start()

    sibling = me.at(c=1 - me.c)
    x_peer = me.at(x=1 - me.x)
    z_peers = [me.at(z=me.dz(n)) for n in (1, 2, 3)]
    y_peers = [me.at(y=me.dy(n)) for n in (1, 2, 3)]
    rep_peers = [sibling, me.at(xl=1 - me.xl), me.at(xl=1 - me.xl, c=1 - me.c)]
    xz_peers = z_peers + [x_peer] + [me.at(x=1 - me.x, z=me.dz(n)) for n in (1, 2, 3)]
    everyone = xz_peers + y_peers + rep_peers
    barrier = pltpu.get_barrier_semaphore()
    for peer in everyone:
        pl.semaphore_signal(barrier, inc=1, device_id=peer, device_id_type=MESH)

    def narrow(q):
        loads[q].wait()

        def tiles(xz, _):
            for slot in range(16):
                tile = words[q, xz, slot].astype(jnp.int16)
                if q < 3:
                    m16[q, xz, slot] = tile
                else:
                    rm[me.y, xz, slot] = tile
            return 0

        lax.fori_loop(0, 8, tiles, 0)

    place = lax.broadcasted_iota(jnp.int32, (128, 128), 1)
    source = 8 * jnp.bitwise_and(place, 15) + jnp.right_shift(place, 4)
    perm = jnp.where(lax.broadcasted_iota(jnp.int32, (128, 128), 0) == source, 1.0, 0.0).astype(BF16)
    feat_load.wait()
    for t in range(8):
        turned = feat[t * 128:(t + 1) * 128, :].astype(F32).T.astype(BF16)
        moved = jnp.dot(turned, perm, preferred_element_type=F32).astype(BF16)
        xt[t // 4, :, (t % 4) * 128:(t % 4 + 1) * 128] = moved
    pl.semaphore_wait(barrier, len(everyone))
    copies = Copies(send, recv)

    def cot_rows(rep):
        return cot.at[pl.ds(pl.multiple_of(rep * 256, 256), 256), :]

    def at(core, xz):
        return g.at[xz, core]

    to_sibling = copies.start(xt.at[other], at(own, me.xz), sibling)
    first = [copies.start(xt.at[own], at(own, me.xz), p) for p in z_peers]
    across = copies.start(xt.at[own], at(own, me.xz), x_peer)
    for copy in small:
        copy.wait()

    def fill(xz, _):
        for q in range(4):
            first = ((xz * 4 + me.dy(Y_ORDER[q])) * 2 + own) * 4
            for tc in range(4):
                count = counts_ref[0, first + tc]
                for s in range(4):
                    slots_s[q, 0, xz * 16 + tc * 4 + s] = jnp.where(s < count, rows_ref[s, first + tc], 8)
        return 0

    lax.fori_loop(0, 8, fill, 0)
    to_vmem = pltpu.make_async_copy(slots_s, slots_v, local.at[2])
    to_vmem.start()
    narrow(0)
    to_vmem.wait()
    slot_copies = [copies.start(slots_v.at[q], landed_v.at[me.y], y_peers[Y_ORDER[q] - 1]) for q in range(3)]
    mask_copies = [copies.start(m16.at[0], rm.at[me.y], y_peers[Y_ORDER[0] - 1])]
    to_sibling.wait_recv()
    other_x = copies.start(at(other, me.xz), at(other, me.xz), x_peer)
    second = [copies.start(at(other, me.xz), at(other, me.xz), p) for p in z_peers]
    stays = [
        pltpu.make_async_copy(xt.at[own], at(own, me.xz), local.at[0]),
        pltpu.make_async_copy(w, wc.at[me.rep], local.at[1]),
        pltpu.make_async_copy(cot_rows(me.rep), cotr.at[me.rep], local.at[5]),
        pltpu.make_async_copy(bias_hbm, bias, local.at[9]),
    ]
    for copy in stays:
        copy.start()
    kept = pltpu.make_async_copy(slots_v.at[3], landed_v.at[me.y], local.at[3])
    kept.start()
    tile_row = lax.broadcasted_iota(jnp.int32, (8, 128), 0)

    def scan(q, degrees):
        n = Y_ORDER[q % 4]
        half = own if q < 4 else other
        if q >= 4:
            loads[q].wait()

        def tiles(xz, degrees):
            first = ((xz * 4 + me.dy(n)) * 2 + half) * 4
            for tc in range(4):
                count = counts_ref[0, first + tc]
                for s in range(4):
                    t = jnp.where(s < count, rows_ref[s, first + tc], 8)
                    tile = words[q, xz, tc * 4 + s]
                    joined = jnp.bitwise_or(tile[:8], jnp.left_shift(tile[8:], 8))
                    counted = jnp.sum(lax.population_count(joined), axis=0, keepdims=True)
                    degrees = degrees + jnp.where(tile_row == t, counted, 0)
            return degrees

        return lax.fori_loop(0, 8, tiles, degrees)

    degrees = scan(0, jnp.zeros((8, 128), jnp.int32))
    narrow(1)
    degrees = scan(1, degrees)
    narrow(2)
    for q in (1, 2):
        mask_copies.append(copies.start(m16.at[q], rm.at[me.y], y_peers[Y_ORDER[q] - 1]))
    early = []
    for peer in rep_peers:
        early.append(copies.make(cot_rows(peer[1]), cotr.at[me.rep], peer))
        early.append(copies.make(w, wc.at[me.rep], peer))
    narrow(3)
    for q in (2, 3, 4):
        degrees = scan(q, degrees)
    last = []
    for n in (1, 2, 3):
        first[n - 1].wait_recv()
        source = me.x * 4 + me.dz(4 - n)
        last.append(copies.start(at(own, source), at(own, source), x_peer))
    for q in (5, 6, 7):
        degrees = scan(q, degrees)

    degrees = 1.0 + degrees.astype(F32)
    high = jnp.floor(degrees * (1.0 / 256.0))
    low = degrees - high * 256.0
    placed = 256.0 * jnp.dot(high.astype(BF16), perm, preferred_element_type=F32)
    placed = placed + jnp.dot(low.astype(BF16), perm, preferred_element_type=F32)
    inv_s[...] = lax.rsqrt(placed)
    inv_copies = [copies.start(inv_s, scale.at[me.xz], peer) for peer in xz_peers]
    inv = lax.rsqrt(degrees)
    other_x.wait_recv()
    far = (1 - me.x) * 4 + me.z
    last += [copies.start(at(other, far), at(other, far), p) for p in z_peers]
    scale[me.xz] = inv_s[...]
    for t in range(8):
        lanes = inv[t:t + 1, :]
        row[:, t * 128:(t + 1) * 128] = jnp.broadcast_to(lanes, (8, 128))
        col[t * 128:(t + 1) * 128, :] = jnp.broadcast_to(lanes, (128, 128)).T

    def put_tiles(n, slot_rows, at):
        i = me.dy(n)

        def column(j, _):
            for tc in range(4):
                rows = [slot_rows[at, 0, j * 16 + tc * 4 + s] for s in range(4)]
                tiles = [rm[i, j, tc * 4 + s] for s in range(4)]
                for t in range(8):
                    found = jnp.zeros((16, 128), jnp.int16)
                    for s in range(4):
                        found = jnp.where(rows[s] == t, tiles[s], found)
                    dense[i * 8 + j, tc, t] = found
            return 0

        lax.fori_loop(0, 8, column, 0)

    put_tiles(0, slots_s, 3)

    def arrive(column):
        n = column % 4
        if column == 0:
            stays[0].wait()
        elif column < 4:
            second[n - 1].wait_recv()
        elif column == 4:
            across.wait_recv()
        else:
            last[n - 1].wait_recv()
            last[n + 2].wait_recv()
        if column:
            inv_copies[column - 1].wait_recv()
        xz = me.column(column)
        for t in range(4):
            lanes = slice(t * 128, (t + 1) * 128)
            factor = scale[xz, pl.ds(own * 4 + t, 1), :]
            for core in range(2):
                gs[xz, core, :, lanes] = (g[xz, core, :, lanes].astype(F32) * factor).astype(BF16)

    def slots():
        kept.wait()
        for copy in slot_copies:
            copy.wait_recv()
        to_smem = pltpu.make_async_copy(landed_v, landed_s, local.at[4])
        to_smem.start()
        to_smem.wait()

    def place_tiles(n):
        q = Y_ORDER.index(4 - n)
        mask_copies[q].wait_recv()
        put_tiles(n, landed_s, me.dy(n))

    def send_parameters():
        for copy in early:
            copy.start()

    def parameters():
        for copy in early:
            copy.wait_recv()
        for copy in stays[1:]:
            copy.wait()

    return arrive, slots, place_tiles, send_parameters, parameters, copies.wait_sends


def table(values, step):
    found = values[-1]
    for n in range(len(values) - 1):
        found = jnp.where(step == n, values[n], found)
    return found


def unpack(dense, i, j, out_ref):
    one, zero = jnp.asarray(1, BF16), jnp.asarray(0, BF16)
    for tc in range(4):
        for t in range(8):
            words = dense[i * 8 + j, tc, t]
            for k in range(8):
                bits = jnp.where(jnp.bitwise_and(words, jnp.int16(1 << k)) != 0, one, zero)
                first = tc * 128 + k * 16
                out_ref[first:first + 16, t * 128:(t + 1) * 128] = bits


def layer(me, arrive, slots, place_tiles, send_parameters, parameters, dense, g, row, col, wc, bias, cotr, act, ball, gwx, a0, a1,
          acc, part, rc, snd, ry, agg_s, agg, agg_t, slope, act_s, back_s,
          core_s, core_r, sum_s, sum_r, send, recv, local):
    sibling = me.at(c=1 - me.c)
    xl_peer = me.at(xl=1 - me.xl)
    xl_other = me.at(xl=1 - me.xl, c=1 - me.c)
    y_peers = [me.at(y=me.dy(n)) for n in (1, 2, 3)]
    copies = Copies(send, recv)
    own, other = me.c, 1 - me.c

    def to_sibling(s):
        return pltpu.make_async_remote_copy(
            src_ref=part.at[s, other], dst_ref=rc.at[s], send_sem=core_s.at[s], recv_sem=core_r.at[s],
            device_id=sibling, device_id_type=MESH,
        )

    def rows_of(m):
        return pl.ds(pl.multiple_of(m * 256, 256), 256)

    def to_owner(k, m):
        return pltpu.make_async_remote_copy(
            src_ref=snd.at[k, m], dst_ref=ry.at[k, m], send_sem=sum_s.at[k * 4 + m], recv_sem=sum_r.at[k * 4 + m],
            device_id=me.at(y=me.dy(table((2, 1, 3), k))), device_id_type=MESH,
        )

    def pass_on(k):
        to_sibling(k).wait_recv()
        for m in range(4):
            rows = slice(m * 256, (m + 1) * 256)
            snd[k, m] = (part[k, own, :, rows].astype(F32) + rc[k, :, rows].astype(F32)).astype(BF16)
            to_owner(k, m).start()

    def chunk(c):
        return me.dy(table(ROWS, c // 8)), me.column(lax.rem(c, 8))

    slots()
    place_tiles(ROWS[0])
    bufs = (a0, a1)
    unpack(dense, *chunk(0), a0)

    def two_chunks(n, _):
        k, pair = n // 4, lax.rem(n, 4)
        for step in range(4):
            @pl.when(n == step)
            def _():
                arrive(step * 2)
                arrive(step * 2 + 1)

        for step in (1, 2):
            @pl.when(n == step * 4 - 1)
            def _():
                if step == 1:
                    send_parameters()
                place_tiles(ROWS[step])

        for h in range(2):
            unpack(dense, *chunk(jnp.minimum(n * 2 + h + 1, 31)), bufs[1 - h])
            prod = jnp.dot(g[me.column(pair * 2 + h)].reshape(256, 512), bufs[h][...], preferred_element_type=F32)
            if h == 0:
                acc[...] = jnp.where(pair == 0, 0.0, acc[...]) + prod
            else:
                acc[...] += prod

        @pl.when(pair == 3)
        def _():
            part[k, 0] = acc[0:128].astype(BF16)
            part[k, 1] = acc[128:256].astype(BF16)
            to_sibling(k).start()

        @pl.when(jnp.logical_and(pair == 0, k >= 1))
        def _():
            pass_on(k - 1)

        return 0

    lax.fori_loop(0, 16, two_chunks, 0)
    to_sibling(3).wait_recv()

    def finish_sum(m, out):
        for k in range(3):
            to_owner(k, m).wait_recv()
        rows = rows_of(m)
        total = part[3, own, :, rows].astype(F32) + rc[3, :, rows].astype(F32)
        for k in range(3):
            total = total + ry[k, m].astype(F32)
        total = total * row[0:1, rows]
        agg_t[:, rows] = total.astype(BF16)
        out[...] = total.T.astype(BF16)

    swaps = []
    peers = (xl_peer, xl_other, sibling)
    for n in range(3):
        finish_sum(peers[n][1], agg_s.at[n])
        swaps.append(copies.start(agg_s.at[n], agg.at[me.rep], peers[n]))
    finish_sum(me.rep, agg.at[me.rep])
    parameters()
    for copy in reversed(swaps):
        copy.wait_recv()

    for half in range(2):
        rows = slice(half * 128, (half + 1) * 128)
        hidden = jnp.dot(agg[0, rows, :], wc[0], preferred_element_type=F32)
        for q in range(1, 4):
            hidden = hidden + jnp.dot(agg[q, rows, :], wc[q], preferred_element_type=F32)
        hidden = hidden + bias[...]
        logistic = jax.nn.sigmoid(hidden)
        value = hidden * logistic
        factor = logistic * (1.0 + hidden * (1.0 - logistic))
        for q in range(4):
            lanes = slice(q * 128, (q + 1) * 128)
            act_s[q, rows, :] = value[:, lanes]
            slope[me.rep, rows, lanes] = (cotr[q, rows, :].astype(F32) * factor[:, lanes]).astype(BF16)

    def block(y, rep):
        return ball.at[pl.ds(pl.multiple_of(y * 1024 + rep * 256, 256), 256), :]

    def back_into(xl, out):
        for core in range(2):
            value = lax.dot_general(
                slope[me.rep], wc[xl * 2 + core], (((1,), (1,)), ((), ())), preferred_element_type=F32
            )
            out[:, core * 128:(core + 1) * 128] = (value * col[rows_of(me.rep), :]).astype(BF16)

    theirs = (1 - me.xl) * 2 + me.c
    back_into(1 - me.xl, back_s)
    from_xl = copies.start(back_s, block(me.y, me.rep), xl_peer)
    back_into(me.xl, block(me.y, me.rep))

    def send_block(rep):
        here = block(me.y, rep)
        return [copies.start(here, here, y_peers[n - 1]) for n in (2, 1, 3)] + [copies.start(here, here, sibling)]

    mine = send_block(me.rep)
    slope_far = copies.start(slope.at[me.rep], slope.at[me.rep], xl_peer)
    slope_near = copies.start(slope.at[me.rep], slope.at[me.rep], sibling)
    from_xl.wait_recv()
    passed = send_block(theirs)
    acts = [
        copies.start(act_s.at[peer[1]], act.at[rows_of(me.rep), :], peer)
        for peer in (xl_peer, xl_other, sibling)
    ]
    act_kept = pltpu.make_async_copy(act_s.at[me.rep], act.at[rows_of(me.rep), :], local)
    act_kept.start()
    slope_far.wait_recv()
    slope_relay = copies.start(slope.at[theirs], slope.at[theirs], sibling)

    relays = []
    for sent, rep in ((mine, me.rep), (passed, theirs)):
        if rep is theirs:
            slope_near.wait_recv()
            slope_relay.wait_recv()
            ones = jnp.ones((8, 256), BF16)
            grad = jnp.zeros((128, 512), F32)
            gb = jnp.zeros((8, 512), F32)
            for q in range(4):
                grad = grad + jnp.dot(agg_t[:, q * 256:(q + 1) * 256], slope[q], preferred_element_type=F32)
                gb = gb + jnp.dot(ones, slope[q], preferred_element_type=F32)
            for n in range(4):
                gwx[n, 0:32, :] = grad[n * 32:(n + 1) * 32]
                gwx[n, 32:40, :] = gb
        for n, copy in zip((2, 1, 3), sent):
            copy.wait_recv()
            here = block(me.dy(4 - n), rep)
            relays.append(copies.start(here, here, sibling))
    for copy in [mine[3], passed[3]] + relays:
        copy.wait_recv()

    def finish():
        for copy in acts:
            copy.wait_recv()
        act_kept.wait()
        copies.wait_sends()
        for k in range(3):
            for m in range(4):
                to_owner(k, m).wait_send()
        for k in range(4):
            to_sibling(k).wait_send()

    return finish


SPLIT = 192
BLOCKS = ((1, 2), (1, 1), (1, 3), (1, 0), (0, 2), (0, 1), (0, 3), (0, 0))
ORDER = {key: n for n, key in enumerate(BLOCKS)}


def settle(me, dense, col, ball, gwx, out, gw, a0, a1,
           acc, part_a, part_b, az, a_sum, ax, bx, b_sum, bz, hold, final, wy, wz, wx_send, wx, gw_own, send, recv, local):
    sibling = me.at(c=1 - me.c)
    x_peer = me.at(x=1 - me.x)
    z_peers = [me.at(z=me.dz(n)) for n in (1, 2, 3)]
    y_peers = [me.at(y=me.dy(n)) for n in (1, 2, 3)]

    def remote(n, src, dst, peer):
        return pltpu.make_async_remote_copy(
            src_ref=src, dst_ref=dst, send_sem=send.at[n], recv_sem=recv.at[n],
            device_id=peer, device_id_type=MESH,
        )

    x_first = {n: remote(n, part_b.at[ORDER[1, n]], bx.at[n], x_peer) for n in range(4)}
    z_first = {
        (side, n): remote(4 + side * 3 + n - 1, part_a.at[ORDER[side, n]], az.at[side, n - 1], z_peers[n - 1])
        for side in range(2) for n in (1, 2, 3)
    }
    z_second = {n: remote(9 + n, b_sum.at[n - 1], bz.at[n - 1], z_peers[n - 1]) for n in (1, 2, 3)}
    x_second = remote(13, a_sum, ax, x_peer)
    w_y = [remote(13 + n, gwx.at[me.dy(n)], wy.at[me.y], y_peers[n - 1]) for n in (1, 2, 3)]
    w_z = [remote(16 + n, wz.at[me.z], wz.at[me.z], z_peers[n - 1]) for n in (1, 2, 3)]
    w_x = remote(20, wx_send, wx, x_peer)
    w_back = [remote(20 + n, gw_own, gw.at[me.y], y_peers[n - 1]) for n in (1, 2, 3)]
    w_kept = pltpu.make_async_copy(gw_own, gw.at[me.y], local.at[0])

    def pass_b(n):
        x_first[n].wait_recv()
        b_sum[n - 1] = (part_b[ORDER[0, n]].astype(F32) + bx[n].astype(F32)).astype(BF16)
        z_second[n].start()

    def pass_a():
        total = part_a[ORDER[1, 0]].astype(F32)
        for n in (1, 2, 3):
            z_first[1, n].wait_recv()
            total = total + az[1, n - 1].astype(F32)
        a_sum[...] = total.astype(BF16)
        x_second.start()

    def weights_z():
        for copy in w_y:
            copy.wait_recv()
        wz[me.z] = (wy[0] + wy[1]) + (wy[2] + wy[3])
        for copy in w_z:
            copy.start()

    def weights_x():
        for copy in w_z:
            copy.wait_recv()
        wx_send[...] = (wz[0] + wz[1]) + (wz[2] + wz[3])
        w_x.start()

    def weights_back():
        w_x.wait_recv()
        gw_own[...] = wx_send[...] + wx[...]
        w_kept.start()
        for copy in w_back:
            copy.start()

    actions = {n: [] for n in range(8)}
    for n in range(4):
        actions[ORDER[1, n]].append(x_first[n].start)
    for n in (2, 1, 3):
        actions[ORDER[0, n]].append(functools.partial(pass_b, n))
    for key, copy in z_first.items():
        actions[ORDER[key]].append(copy.start)
    actions[2].append(weights_z)
    actions[4].append(pass_a)
    actions[4].append(weights_x)
    actions[6].append(weights_back)

    for copy in w_y:
        copy.start()
    wy[me.y] = gwx[me.y]

    def chunk(c):
        at = c // 4
        x = lax.rem(me.x + table([block[0] for block in BLOCKS], at), 2)
        z = lax.rem(me.z + table([block[1] for block in BLOCKS], at), 4)
        return lax.rem(c, 4), x * 4 + z

    bufs = (a0, a1)
    unpack(dense, *chunk(0), a0)

    def two_chunks(step, _):
        block, pair = step // 2, lax.rem(step, 2)
        for h in range(2):
            unpack(dense, *chunk(jnp.minimum(step * 2 + h + 1, 31)), bufs[1 - h])
            prod = jnp.dot(bufs[h][...], ball[pl.ds(pl.multiple_of((pair * 2 + h) * 1024, 1024), 1024), :], preferred_element_type=F32)
            if h == 0:
                acc[...] = jnp.where(pair == 0, 0.0, acc[...]) + prod
            else:
                acc[...] += prod

        @pl.when(pair == 1)
        def _():
            part_a[block] = acc[0:SPLIT].astype(BF16)
            part_b[block] = acc[SPLIT:512].astype(BF16)

        for at, calls in actions.items():
            if calls:
                @pl.when(step == at * 2 + 1)
                def _():
                    for call in calls:
                        call()

        return 0

    lax.fori_loop(0, 16, two_chunks, 0)

    def keep_rows(first, total):
        for q in range(2):
            hold[q * 512 + first:q * 512 + first + total.shape[0], :] = total[:, q * 128:(q + 1) * 128]

    def place(tile):
        here = slice(tile * 128, tile * 128 + 256)
        for t in range(tile, tile + 2):
            for w in range(16):
                first = t * 128 + w * 8
                scale = col[pl.ds(pl.multiple_of(me.c * 512 + first, 8), 8), :]
                for q in range(2):
                    final[q, first:first + 8, :] = hold[pl.ds(q * 512 + t * 128 + w, 8, stride=16), :] * scale
        at = tile // 2
        swap = remote(24 + at, final.at[1 - me.c, here], out.at[me.c, here], sibling)
        keep = pltpu.make_async_copy(final.at[me.c, here], out.at[me.c, here], local.at[1 + at])
        swap.start()
        keep.start()
        return swap, keep

    total = part_b[ORDER[0, 0]].astype(F32)
    x_first[0].wait_recv()
    total = total + bx[0].astype(F32)
    for n in (1, 2, 3):
        z_second[n].wait_recv()
        total = total + bz[n - 1].astype(F32)
    keep_rows(SPLIT, total)
    swaps = [place(2)]
    total = part_a[ORDER[0, 0]].astype(F32)
    for n in (1, 2, 3):
        z_first[0, n].wait_recv()
        total = total + az[0, n - 1].astype(F32)
    x_second.wait_recv()
    total = total + ax[...].astype(F32)
    keep_rows(0, total)
    swaps.append(place(0))
    for copy in w_back:
        copy.wait_recv()
    for swap, keep in swaps:
        swap.wait_recv()
        keep.wait()
    w_kept.wait()
    for copy in list(x_first.values()) + list(z_first.values()) + list(z_second.values()):
        copy.wait_send()
    for copy in [x_second, w_x] + [swap for swap, _ in swaps] + w_y + w_z + w_back:
        copy.wait_send()


PART_A, PART_B = (SPLIT, 256), (512 - SPLIT, 256)
HELD = (
    pltpu.VMEM((32, 4, 8, 16, 128), jnp.int16),
    pltpu.VMEM((8, 1024), F32),
    pltpu.VMEM((1024, 128), F32),
    pltpu.VMEM((8, 2, 128, 512), BF16),
    pltpu.VMEM((4, 128, 512), BF16),
    pltpu.VMEM((4, 256, 128), BF16),
    pltpu.VMEM((1, 512), F32),
    pltpu.VMEM((4096, 256), BF16),
    pltpu.VMEM((4, 40, 512), F32),
    pltpu.VMEM((512, 1024), BF16),
    pltpu.VMEM((512, 1024), BF16),
)
SPREAD = (
    pltpu.SMEM((4, 256), jnp.int32),
    pltpu.SMEM((1, 256), jnp.int32),
    pltpu.VMEM((1024, 128), BF16),
    pltpu.VMEM((8, 2, 128, 512), BF16),
    pltpu.VMEM((8, 128), F32),
    pltpu.VMEM((8, 8, 128), F32),
    pltpu.VMEM((8, 8, 16, 16, 128), jnp.int32),
    pltpu.VMEM((3, 8, 16, 16, 128), jnp.int16),
    pltpu.VMEM((4, 8, 16, 16, 128), jnp.int16),
    pltpu.SMEM((4, 1, 128), jnp.int32),
    pltpu.VMEM((4, 1, 128), jnp.int32),
    pltpu.VMEM((4, 1, 128), jnp.int32),
    pltpu.SMEM((4, 1, 128), jnp.int32),
    pltpu.VMEM((2, 128, 512), BF16),
    DMA((34,)),
    DMA((34,)),
    DMA((8,)),
    DMA((10,)),
)
LAYER = (
    pltpu.VMEM((256, 1024), F32),
    pltpu.VMEM((4, 2, 128, 1024), BF16),
    pltpu.VMEM((4, 128, 1024), BF16),
    pltpu.VMEM((3, 4, 128, 256), BF16),
    pltpu.VMEM((3, 4, 128, 256), BF16),
    pltpu.VMEM((3, 256, 128), BF16),
    pltpu.VMEM((4, 256, 128), BF16),
    pltpu.VMEM((128, 1024), BF16),
    pltpu.VMEM((4, 256, 512), BF16),
    pltpu.VMEM((4, 256, 128), F32),
    pltpu.VMEM((256, 256), BF16),
    DMA((4,)),
    DMA((4,)),
    DMA((12,)),
    DMA((12,)),
    DMA((24,)),
    DMA((24,)),
    DMA,
)
SETTLE = (
    pltpu.VMEM((512, 256), F32),
    pltpu.VMEM((8,) + PART_A, BF16),
    pltpu.VMEM((8,) + PART_B, BF16),
    pltpu.VMEM((2, 3) + PART_A, BF16),
    pltpu.VMEM(PART_A, BF16),
    pltpu.VMEM(PART_A, BF16),
    pltpu.VMEM((4,) + PART_B, BF16),
    pltpu.VMEM((3,) + PART_B, BF16),
    pltpu.VMEM((3,) + PART_B, BF16),
    pltpu.VMEM((1024, 128), F32),
    pltpu.VMEM((2, 512, 128), F32),
    pltpu.VMEM((4, 40, 512), F32),
    pltpu.VMEM((4, 40, 512), F32),
    pltpu.VMEM((40, 512), F32),
    pltpu.VMEM((40, 512), F32),
    pltpu.VMEM((40, 512), F32),
    DMA((26,)),
    DMA((26,)),
    DMA((3,)),
)


def all_kernel(*refs):
    groups, first = [], 0
    for size in (7, 3, len(HELD), len(SPREAD), len(LAYER), len(SETTLE)):
        groups.append(refs[first:first + size])
        first += size
    ins, (act, out, gw), held, spread_refs, layer_refs, settle_refs = groups
    dense, row, col, g, wc, cotr, bias, ball, gwx, a0, a1 = held
    me = Place()
    *arrivals, finish_spread = spread(me, *ins, dense, row, col, g, wc, cotr, bias, *spread_refs)
    finish_layer = layer(
        me, *arrivals, dense, g, row, col, wc, bias, cotr, act, ball, gwx, a0, a1, *layer_refs
    )
    settle(me, dense, col, ball, gwx, out, gw, a0, a1, *settle_refs)
    finish_layer()
    finish_spread()


def results_kernel(act, out, gw, act_out, feat_out, gw_out, gb_out, act_v, feat_v, gw_v, load, store):
    loads = [pltpu.make_async_copy(gw, gw_v, load.at[0])]
    for n in range(2):
        here = slice(n * 512, n * 512 + 512)
        loads.append(pltpu.make_async_copy(act.at[here], act_v.at[here], load.at[1 + n]))
        loads.append(pltpu.make_async_copy(out.at[here], feat_v.at[here], load.at[3 + n]))
    for copy in loads:
        copy.start()
    loads[0].wait()
    stores = [
        pltpu.make_async_copy(gw_v.at[:, 0:32], gw_out, store.at[0]),
        pltpu.make_async_copy(gw_v.at[0, 32:33], gb_out, store.at[1]),
    ]
    for copy in stores:
        copy.start()
    for n in range(2):
        here = slice(n * 512, n * 512 + 512)
        loads[1 + 2 * n].wait()
        stores.append(pltpu.make_async_copy(act_v.at[here], act_out.at[here], store.at[2 + n]))
        stores[-1].start()
        loads[2 + 2 * n].wait()
        stores.append(pltpu.make_async_copy(feat_v.at[here], feat_out.at[here], store.at[4 + n]))
        stores[-1].start()
    for copy in stores:
        copy.wait()


def body(features, weight, bias_vector, cotangent, tile_masks, tile_rows, tile_counts):
    masks = tile_masks.reshape(8, 4, 2, 16, 16, 128)
    act, out, gw = pl.pallas_call(
        all_kernel,
        out_shape=(
            jax.ShapeDtypeStruct((1024, 128), F32),
            jax.ShapeDtypeStruct((2, 512, 128), F32),
            jax.ShapeDtypeStruct((4, 40, 512), F32),
        ),
        in_specs=[HBM] * 7,
        out_specs=(HBM,) * 3,
        scratch_shapes=HELD + SPREAD + LAYER + SETTLE,
        compiler_params=pltpu.CompilerParams(
            collective_id=0, has_side_effects=True, vmem_limit_bytes=VMEM_MIB * MIB
        ),
        name="layer",
    )(tile_rows[0].T, tile_counts, masks, features, weight, bias_vector.reshape(1, 512), cotangent)
    act, out, gw, gb = pl.pallas_call(
        results_kernel,
        out_shape=(
            jax.ShapeDtypeStruct((1024, 128), F32),
            jax.ShapeDtypeStruct((1024, 128), F32),
            jax.ShapeDtypeStruct((4, 32, 512), F32),
            jax.ShapeDtypeStruct((1, 512), F32),
        ),
        in_specs=[HBM] * 3,
        out_specs=(HBM,) * 4,
        scratch_shapes=[
            pltpu.VMEM((1024, 128), F32),
            pltpu.VMEM((1024, 128), F32),
            pltpu.VMEM((4, 40, 512), F32),
            DMA((5,)),
            DMA((6,)),
        ],
        compiler_params=pltpu.CompilerParams(vmem_limit_bytes=VMEM_MIB * MIB),
        name="results",
    )(act, out.reshape(1024, 128), gw)
    return act, out, gw.reshape(128, 512), gb.reshape(512)


def solution(mesh):
    return jax.shard_map(
        body,
        mesh=mesh,
        in_specs=(
            P("blk", "rep"),
            P("rep", None),
            P(),
            P("blk", "rep"),
            P("blk", None, None, None, None),
            P("blk", None, None),
            P("blk", None),
        ),
        out_specs=(P("blk", "rep"), P("blk", "rep"), P("rep", None), P()),
        check_vma=False,
    )
```

```python
import functools

import jax
import jax.numpy as jnp
from jax import lax
from jax.experimental import pallas as pl
from jax.experimental.pallas import tpu as pltpu
from jax.sharding import PartitionSpec as P

MESH = pl.DeviceIdType.MESH
BF16 = jnp.bfloat16
F32 = jnp.float32
HBM = pl.BlockSpec(memory_space=pltpu.HBM)
DMA = pltpu.SemaphoreType.DMA
MIB = 2**20
VMEM_MIB = 60


class Place:
    def __init__(self):
        blk = lax.axis_index("blk")
        rep = lax.axis_index("rep")
        self.x, self.z, self.y = blk // 16, lax.rem(blk // 4, 4), lax.rem(blk, 4)
        self.xl, self.c = rep // 2, lax.rem(rep, 2)
        self.rep = rep
        self.xz = self.x * 4 + self.z

    def at(self, x=None, z=None, y=None, xl=None, c=None):
        x = self.x if x is None else x
        z = self.z if z is None else z
        y = self.y if y is None else y
        xl = self.xl if xl is None else xl
        c = self.c if c is None else c
        return (x * 16 + z * 4 + y, xl * 2 + c)

    def dy(self, n):
        return lax.rem(self.y + n, 4)

    def dz(self, n):
        return lax.rem(self.z + n, 4)

    def column(self, n):
        return lax.rem(self.x + n // 4, 2) * 4 + self.dz(4 - lax.rem(n, 4))


class Copies:
    def __init__(self, send, recv):
        self.send, self.recv, self.used = send, recv, []

    def start(self, src, dst, peer):
        copy = self.make(src, dst, peer)
        copy.start()
        return copy

    def make(self, src, dst, peer):
        n = len(self.used)
        copy = pltpu.make_async_remote_copy(
            src_ref=src, dst_ref=dst, send_sem=self.send.at[n], recv_sem=self.recv.at[n],
            device_id=peer, device_id_type=MESH,
        )
        self.used.append(copy)
        return copy

    def wait_sends(self):
        for copy in self.used:
            copy.wait_send()


Y_ORDER = (2, 1, 3, 0)
ROWS = (2, 1, 3, 0)


def spread(me, rows_hbm, counts_hbm, masks, feat_hbm, w, bias_hbm, cot, dense, row, col, gs, wc, cotr, bias,
           rows_ref, counts_ref, feat, g, inv_s, scale, words, m16, rm, slots_s, slots_v, landed_v, landed_s, xt, send, recv, load, local):
    own, other = me.c, 1 - me.c
    feat_load = pltpu.make_async_copy(feat_hbm, feat, local.at[8])
    feat_load.start()
    small = [
        pltpu.make_async_copy(rows_hbm, rows_ref, local.at[6]),
        pltpu.make_async_copy(counts_hbm, counts_ref, local.at[7]),
    ]
    for copy in small:
        copy.start()
    loads = []
    for q in range(8):
        half = own if q < 4 else other
        loads.append(pltpu.make_async_copy(masks.at[:, me.dy(Y_ORDER[q % 4]), half], words.at[q], load.at[q]))
        loads[q].start()

    sibling = me.at(c=1 - me.c)
    x_peer = me.at(x=1 - me.x)
    z_peers = [me.at(z=me.dz(n)) for n in (1, 2, 3)]
    y_peers = [me.at(y=me.dy(n)) for n in (1, 2, 3)]
    rep_peers = [sibling, me.at(xl=1 - me.xl), me.at(xl=1 - me.xl, c=1 - me.c)]
    xz_peers = z_peers + [x_peer] + [me.at(x=1 - me.x, z=me.dz(n)) for n in (1, 2, 3)]
    everyone = xz_peers + y_peers + rep_peers
    barrier = pltpu.get_barrier_semaphore()
    for peer in everyone:
        pl.semaphore_signal(barrier, inc=1, device_id=peer, device_id_type=MESH)

    def narrow(q):
        loads[q].wait()

        def tiles(xz, _):
            for slot in range(16):
                tile = words[q, xz, slot].astype(jnp.int16)
                if q < 3:
                    m16[q, xz, slot] = tile
                else:
                    rm[me.y, xz, slot] = tile
            return 0

        lax.fori_loop(0, 8, tiles, 0)

    for copy in small:
        copy.wait()

    def fill(xz, _):
        for q in range(4):
            first = ((xz * 4 + me.dy(Y_ORDER[q])) * 2 + own) * 4
            for tc in range(4):
                count = counts_ref[0, first + tc]
                for s in range(4):
                    slots_s[q, 0, xz * 16 + tc * 4 + s] = jnp.where(s < count, rows_ref[s, first + tc], 8)
        return 0

    lax.fori_loop(0, 8, fill, 0)
    to_vmem = pltpu.make_async_copy(slots_s, slots_v, local.at[2])
    to_vmem.start()

    place = lax.broadcasted_iota(jnp.int32, (128, 128), 1)
    source = 8 * jnp.bitwise_and(place, 15) + jnp.right_shift(place, 4)
    perm = jnp.where(lax.broadcasted_iota(jnp.int32, (128, 128), 0) == source, 1.0, 0.0).astype(BF16)
    feat_load.wait()
    for t in range(8):
        turned = feat[t * 128:(t + 1) * 128, :].astype(F32).T.astype(BF16)
        moved = jnp.dot(turned, perm, preferred_element_type=F32).astype(BF16)
        xt[t // 4, :, (t % 4) * 128:(t % 4 + 1) * 128] = moved
    narrow(0)
    to_vmem.wait()
    pl.semaphore_wait(barrier, len(everyone))
    copies = Copies(send, recv)

    def cot_rows(rep):
        return cot.at[pl.ds(pl.multiple_of(rep * 256, 256), 256), :]

    def at(core, xz):
        return g.at[xz, core]

    slot_copies = [copies.start(slots_v.at[q], landed_v.at[me.y], y_peers[Y_ORDER[q] - 1]) for q in range(3)]
    to_sibling = copies.start(xt.at[other], at(own, me.xz), sibling)
    first = [copies.start(xt.at[own], at(own, me.xz), p) for p in z_peers]
    across = copies.start(xt.at[own], at(own, me.xz), x_peer)
    mask_copies = [copies.start(m16.at[0], rm.at[me.y], y_peers[Y_ORDER[0] - 1])]
    stays = [
        pltpu.make_async_copy(xt.at[own], at(own, me.xz), local.at[0]),
        pltpu.make_async_copy(w, wc.at[me.rep], local.at[1]),
        pltpu.make_async_copy(cot_rows(me.rep), cotr.at[me.rep], local.at[5]),
        pltpu.make_async_copy(bias_hbm, bias, local.at[9]),
    ]
    for copy in stays:
        copy.start()
    kept = pltpu.make_async_copy(slots_v.at[3], landed_v.at[me.y], local.at[3])
    kept.start()
    tile_row = lax.broadcasted_iota(jnp.int32, (8, 128), 0)

    def scan(q, degrees):
        n = Y_ORDER[q % 4]
        half = own if q < 4 else other
        if q >= 4:
            loads[q].wait()

        def tiles(xz, degrees):
            first = ((xz * 4 + me.dy(n)) * 2 + half) * 4
            for tc in range(4):
                count = counts_ref[0, first + tc]
                for s in range(4):
                    t = jnp.where(s < count, rows_ref[s, first + tc], 8)
                    tile = words[q, xz, tc * 4 + s]
                    joined = jnp.bitwise_or(tile[:8], jnp.left_shift(tile[8:], 8))
                    counted = jnp.sum(lax.population_count(joined), axis=0, keepdims=True)
                    degrees = degrees + jnp.where(tile_row == t, counted, 0)
            return degrees

        return lax.fori_loop(0, 8, tiles, degrees)

    degrees = scan(0, jnp.zeros((8, 128), jnp.int32))
    narrow(1)
    to_sibling.wait_recv()
    other_x = copies.start(at(other, me.xz), at(other, me.xz), x_peer)
    second = [copies.start(at(other, me.xz), at(other, me.xz), p) for p in z_peers]
    degrees = scan(1, degrees)
    narrow(2)
    for q in (1, 2):
        mask_copies.append(copies.start(m16.at[q], rm.at[me.y], y_peers[Y_ORDER[q] - 1]))
    early = []
    for peer in rep_peers:
        early.append(copies.make(cot_rows(peer[1]), cotr.at[me.rep], peer))
        early.append(copies.make(w, wc.at[me.rep], peer))
    narrow(3)
    for q in (2, 3, 4):
        degrees = scan(q, degrees)
    last = []
    for n in (1, 2, 3):
        first[n - 1].wait_recv()
        source = me.x * 4 + me.dz(4 - n)
        last.append(copies.start(at(own, source), at(own, source), x_peer))
    for q in (5, 6, 7):
        degrees = scan(q, degrees)

    degrees = 1.0 + degrees.astype(F32)
    high = jnp.floor(degrees * (1.0 / 256.0))
    low = degrees - high * 256.0
    placed = 256.0 * jnp.dot(high.astype(BF16), perm, preferred_element_type=F32)
    placed = placed + jnp.dot(low.astype(BF16), perm, preferred_element_type=F32)
    inv_s[...] = lax.rsqrt(placed)
    inv_copies = [copies.start(inv_s, scale.at[me.xz], peer) for peer in xz_peers]
    inv = lax.rsqrt(degrees)
    other_x.wait_recv()
    far = (1 - me.x) * 4 + me.z
    last += [copies.start(at(other, far), at(other, far), p) for p in z_peers]
    scale[me.xz] = inv_s[...]
    for t in range(8):
        lanes = inv[t:t + 1, :]
        row[:, t * 128:(t + 1) * 128] = jnp.broadcast_to(lanes, (8, 128))
        col[t * 128:(t + 1) * 128, :] = jnp.broadcast_to(lanes, (128, 128)).T

    def put_tiles(n, slot_rows, at):
        i = me.dy(n)

        def column(j, _):
            for tc in range(4):
                rows = [slot_rows[at, 0, j * 16 + tc * 4 + s] for s in range(4)]
                tiles = [rm[i, j, tc * 4 + s] for s in range(4)]
                for t in range(8):
                    found = jnp.zeros((16, 128), jnp.int16)
                    for s in range(4):
                        found = jnp.where(rows[s] == t, tiles[s], found)
                    dense[i * 8 + j, tc, t] = found
            return 0

        lax.fori_loop(0, 8, column, 0)

    put_tiles(0, slots_s, 3)

    def arrive(column):
        n = column % 4
        if column == 0:
            stays[0].wait()
        elif column < 4:
            second[n - 1].wait_recv()
        elif column == 4:
            across.wait_recv()
        else:
            last[n - 1].wait_recv()
            last[n + 2].wait_recv()
        if column:
            inv_copies[column - 1].wait_recv()
        xz = me.column(column)
        for t in range(4):
            lanes = slice(t * 128, (t + 1) * 128)
            factor = scale[xz, pl.ds(own * 4 + t, 1), :]
            for core in range(2):
                gs[xz, core, :, lanes] = (g[xz, core, :, lanes].astype(F32) * factor).astype(BF16)

    def slots():
        kept.wait()
        for copy in slot_copies:
            copy.wait_recv()
        to_smem = pltpu.make_async_copy(landed_v, landed_s, local.at[4])
        to_smem.start()
        to_smem.wait()

    def place_tiles(n):
        q = Y_ORDER.index(4 - n)
        mask_copies[q].wait_recv()
        put_tiles(n, landed_s, me.dy(n))

    def send_parameters():
        for copy in early:
            copy.start()

    def parameters():
        for copy in early:
            copy.wait_recv()
        for copy in stays[1:]:
            copy.wait()

    return arrive, slots, place_tiles, send_parameters, parameters, copies.wait_sends


def table(values, step):
    found = values[-1]
    for n in range(len(values) - 1):
        found = jnp.where(step == n, values[n], found)
    return found


def unpack(dense, i, j, out_ref):
    one, zero = jnp.asarray(1, BF16), jnp.asarray(0, BF16)
    for tc in range(4):
        for t in range(8):
            words = dense[i * 8 + j, tc, t]
            for k in range(8):
                bits = jnp.where(jnp.bitwise_and(words, jnp.int16(1 << k)) != 0, one, zero)
                first = tc * 128 + k * 16
                out_ref[first:first + 16, t * 128:(t + 1) * 128] = bits


def layer(me, arrive, slots, place_tiles, send_parameters, parameters, dense, g, row, col, wc, bias, cotr, act, ball, gwx, a0, a1,
          acc, part, rc, snd, ry, agg_s, agg, agg_t, slope, act_s, back_s,
          core_s, core_r, sum_s, sum_r, send, recv, local):
    sibling = me.at(c=1 - me.c)
    xl_peer = me.at(xl=1 - me.xl)
    xl_other = me.at(xl=1 - me.xl, c=1 - me.c)
    y_peers = [me.at(y=me.dy(n)) for n in (1, 2, 3)]
    copies = Copies(send, recv)
    own, other = me.c, 1 - me.c

    def to_sibling(s):
        return pltpu.make_async_remote_copy(
            src_ref=part.at[s, other], dst_ref=rc.at[s], send_sem=core_s.at[s], recv_sem=core_r.at[s],
            device_id=sibling, device_id_type=MESH,
        )

    def rows_of(m):
        return pl.ds(pl.multiple_of(m * 256, 256), 256)

    def to_owner(k, m):
        return pltpu.make_async_remote_copy(
            src_ref=snd.at[k, m], dst_ref=ry.at[k, m], send_sem=sum_s.at[k * 4 + m], recv_sem=sum_r.at[k * 4 + m],
            device_id=me.at(y=me.dy(table((2, 1, 3), k))), device_id_type=MESH,
        )

    def pass_on(k):
        to_sibling(k).wait_recv()
        for m in range(4):
            rows = slice(m * 256, (m + 1) * 256)
            snd[k, m] = (part[k, own, :, rows].astype(F32) + rc[k, :, rows].astype(F32)).astype(BF16)
            to_owner(k, m).start()

    def chunk(c):
        return me.dy(table(ROWS, c // 8)), me.column(lax.rem(c, 8))

    slots()
    place_tiles(ROWS[0])
    bufs = (a0, a1)
    unpack(dense, *chunk(0), a0)

    def two_chunks(n, _):
        k, pair = n // 4, lax.rem(n, 4)
        for step in range(4):
            @pl.when(n == step)
            def _():
                arrive(step * 2)
                arrive(step * 2 + 1)

        for step in (1, 2):
            @pl.when(n == step * 4 - 1)
            def _():
                if step == 1:
                    send_parameters()
                place_tiles(ROWS[step])

        for h in range(2):
            unpack(dense, *chunk(jnp.minimum(n * 2 + h + 1, 31)), bufs[1 - h])
            prod = jnp.dot(g[me.column(pair * 2 + h)].reshape(256, 512), bufs[h][...], preferred_element_type=F32)
            if h == 0:
                acc[...] = jnp.where(pair == 0, 0.0, acc[...]) + prod
            else:
                acc[...] += prod

        @pl.when(pair == 3)
        def _():
            part[k, 0] = acc[0:128].astype(BF16)
            part[k, 1] = acc[128:256].astype(BF16)
            to_sibling(k).start()

        @pl.when(jnp.logical_and(pair == 0, k >= 1))
        def _():
            pass_on(k - 1)

        return 0

    lax.fori_loop(0, 16, two_chunks, 0)
    to_sibling(3).wait_recv()

    def finish_sum(m, out):
        for k in range(3):
            to_owner(k, m).wait_recv()
        rows = rows_of(m)
        total = part[3, own, :, rows].astype(F32) + rc[3, :, rows].astype(F32)
        for k in range(3):
            total = total + ry[k, m].astype(F32)
        total = total * row[0:1, rows]
        agg_t[:, rows] = total.astype(BF16)
        out[...] = total.T.astype(BF16)

    swaps = []
    peers = (xl_peer, xl_other, sibling)
    for n in range(3):
        finish_sum(peers[n][1], agg_s.at[n])
        swaps.append(copies.start(agg_s.at[n], agg.at[me.rep], peers[n]))
    finish_sum(me.rep, agg.at[me.rep])
    parameters()
    for copy in reversed(swaps):
        copy.wait_recv()

    for half in range(2):
        rows = slice(half * 128, (half + 1) * 128)
        hidden = jnp.dot(agg[0, rows, :], wc[0], preferred_element_type=F32)
        for q in range(1, 4):
            hidden = hidden + jnp.dot(agg[q, rows, :], wc[q], preferred_element_type=F32)
        hidden = hidden + bias[...]
        logistic = jax.nn.sigmoid(hidden)
        value = hidden * logistic
        factor = logistic * (1.0 + hidden * (1.0 - logistic))
        for q in range(4):
            lanes = slice(q * 128, (q + 1) * 128)
            act_s[q, rows, :] = value[:, lanes]
            slope[me.rep, rows, lanes] = (cotr[q, rows, :].astype(F32) * factor[:, lanes]).astype(BF16)

    def block(y, rep):
        return ball.at[pl.ds(pl.multiple_of(y * 1024 + rep * 256, 256), 256), :]

    def back_into(xl, out):
        for core in range(2):
            value = lax.dot_general(
                slope[me.rep], wc[xl * 2 + core], (((1,), (1,)), ((), ())), preferred_element_type=F32
            )
            out[:, core * 128:(core + 1) * 128] = (value * col[rows_of(me.rep), :]).astype(BF16)

    theirs = (1 - me.xl) * 2 + me.c
    back_into(1 - me.xl, back_s)
    from_xl = copies.start(back_s, block(me.y, me.rep), xl_peer)
    back_into(me.xl, block(me.y, me.rep))

    def send_block(rep):
        here = block(me.y, rep)
        return [copies.start(here, here, y_peers[n - 1]) for n in (2, 1, 3)] + [copies.start(here, here, sibling)]

    mine = send_block(me.rep)
    slope_far = copies.start(slope.at[me.rep], slope.at[me.rep], xl_peer)
    slope_near = copies.start(slope.at[me.rep], slope.at[me.rep], sibling)
    from_xl.wait_recv()
    passed = send_block(theirs)
    acts = [
        copies.start(act_s.at[peer[1]], act.at[rows_of(me.rep), :], peer)
        for peer in (xl_peer, xl_other, sibling)
    ]
    act_kept = pltpu.make_async_copy(act_s.at[me.rep], act.at[rows_of(me.rep), :], local)
    act_kept.start()
    slope_far.wait_recv()
    slope_relay = copies.start(slope.at[theirs], slope.at[theirs], sibling)

    relays = []
    for sent, rep in ((mine, me.rep), (passed, theirs)):
        if rep is theirs:
            slope_near.wait_recv()
            slope_relay.wait_recv()
            ones = jnp.ones((8, 256), BF16)
            grad = jnp.zeros((128, 512), F32)
            gb = jnp.zeros((8, 512), F32)
            for q in range(4):
                grad = grad + jnp.dot(agg_t[:, q * 256:(q + 1) * 256], slope[q], preferred_element_type=F32)
                gb = gb + jnp.dot(ones, slope[q], preferred_element_type=F32)
            for n in range(4):
                gwx[n, 0:32, :] = grad[n * 32:(n + 1) * 32]
                gwx[n, 32:40, :] = gb
        for n, copy in zip((2, 1, 3), sent):
            copy.wait_recv()
            here = block(me.dy(4 - n), rep)
            relays.append(copies.start(here, here, sibling))
    for copy in [mine[3], passed[3]] + relays:
        copy.wait_recv()

    def finish():
        for copy in acts:
            copy.wait_recv()
        act_kept.wait()
        copies.wait_sends()
        for k in range(3):
            for m in range(4):
                to_owner(k, m).wait_send()
        for k in range(4):
            to_sibling(k).wait_send()

    return finish


SPLIT = 192
BLOCKS = ((1, 2), (1, 1), (1, 3), (1, 0), (0, 2), (0, 1), (0, 3), (0, 0))
ORDER = {key: n for n, key in enumerate(BLOCKS)}


def settle(me, dense, col, ball, gwx, out, gw, a0, a1,
           acc, part_a, part_b, az, a_sum, ax, bx, b_sum, bz, hold, final, wy, wz, wx_send, wx, gw_own, send, recv, local):
    sibling = me.at(c=1 - me.c)
    x_peer = me.at(x=1 - me.x)
    z_peers = [me.at(z=me.dz(n)) for n in (1, 2, 3)]
    y_peers = [me.at(y=me.dy(n)) for n in (1, 2, 3)]

    def remote(n, src, dst, peer):
        return pltpu.make_async_remote_copy(
            src_ref=src, dst_ref=dst, send_sem=send.at[n], recv_sem=recv.at[n],
            device_id=peer, device_id_type=MESH,
        )

    x_first = {n: remote(n, part_b.at[ORDER[1, n]], bx.at[n], x_peer) for n in range(4)}
    z_first = {
        (side, n): remote(4 + side * 3 + n - 1, part_a.at[ORDER[side, n]], az.at[side, n - 1], z_peers[n - 1])
        for side in range(2) for n in (1, 2, 3)
    }
    z_second = {n: remote(9 + n, b_sum.at[n - 1], bz.at[n - 1], z_peers[n - 1]) for n in (1, 2, 3)}
    x_second = remote(13, a_sum, ax, x_peer)
    w_y = [remote(13 + n, gwx.at[me.dy(n)], wy.at[me.y], y_peers[n - 1]) for n in (1, 2, 3)]
    w_z = [remote(16 + n, wz.at[me.z], wz.at[me.z], z_peers[n - 1]) for n in (1, 2, 3)]
    w_x = remote(20, wx_send, wx, x_peer)
    w_back = [remote(20 + n, gw_own, gw.at[me.y], y_peers[n - 1]) for n in (1, 2, 3)]
    w_kept = pltpu.make_async_copy(gw_own, gw.at[me.y], local.at[0])

    def pass_b(n):
        x_first[n].wait_recv()
        b_sum[n - 1] = (part_b[ORDER[0, n]].astype(F32) + bx[n].astype(F32)).astype(BF16)
        z_second[n].start()

    def pass_a():
        total = part_a[ORDER[1, 0]].astype(F32)
        for n in (1, 2, 3):
            z_first[1, n].wait_recv()
            total = total + az[1, n - 1].astype(F32)
        a_sum[...] = total.astype(BF16)
        x_second.start()

    def weights_z():
        for copy in w_y:
            copy.wait_recv()
        wz[me.z] = (wy[0] + wy[1]) + (wy[2] + wy[3])
        for copy in w_z:
            copy.start()

    def weights_x():
        for copy in w_z:
            copy.wait_recv()
        wx_send[...] = (wz[0] + wz[1]) + (wz[2] + wz[3])
        w_x.start()

    def weights_back():
        w_x.wait_recv()
        gw_own[...] = wx_send[...] + wx[...]
        w_kept.start()
        for copy in w_back:
            copy.start()

    actions = {n: [] for n in range(8)}
    for n in range(4):
        actions[ORDER[1, n]].append(x_first[n].start)
    for n in (2, 1, 3):
        actions[ORDER[0, n]].append(functools.partial(pass_b, n))
    for key, copy in z_first.items():
        actions[ORDER[key]].append(copy.start)
    actions[3].append(weights_z)
    actions[4].append(pass_a)
    actions[5].append(weights_x)
    actions[6].append(weights_back)

    for copy in w_y:
        copy.start()
    wy[me.y] = gwx[me.y]

    def chunk(c):
        at = c // 4
        x = lax.rem(me.x + table([block[0] for block in BLOCKS], at), 2)
        z = lax.rem(me.z + table([block[1] for block in BLOCKS], at), 4)
        return lax.rem(c, 4), x * 4 + z

    bufs = (a0, a1)
    unpack(dense, *chunk(0), a0)

    def two_chunks(step, _):
        block, pair = step // 2, lax.rem(step, 2)
        for h in range(2):
            unpack(dense, *chunk(jnp.minimum(step * 2 + h + 1, 31)), bufs[1 - h])
            prod = jnp.dot(bufs[h][...], ball[pl.ds(pl.multiple_of((pair * 2 + h) * 1024, 1024), 1024), :], preferred_element_type=F32)
            if h == 0:
                acc[...] = jnp.where(pair == 0, 0.0, acc[...]) + prod
            else:
                acc[...] += prod

        @pl.when(pair == 1)
        def _():
            part_a[block] = acc[0:SPLIT].astype(BF16)
            part_b[block] = acc[SPLIT:512].astype(BF16)

        for at, calls in actions.items():
            if calls:
                @pl.when(step == at * 2 + 1)
                def _():
                    for call in calls:
                        call()

        return 0

    lax.fori_loop(0, 16, two_chunks, 0)

    def keep_rows(first, total):
        for q in range(2):
            hold[q * 512 + first:q * 512 + first + total.shape[0], :] = total[:, q * 128:(q + 1) * 128]

    def place(tile):
        here = slice(tile * 128, tile * 128 + 256)
        for t in range(tile, tile + 2):
            for w in range(16):
                first = t * 128 + w * 8
                scale = col[pl.ds(pl.multiple_of(me.c * 512 + first, 8), 8), :]
                for q in range(2):
                    final[q, first:first + 8, :] = hold[pl.ds(q * 512 + t * 128 + w, 8, stride=16), :] * scale
        at = tile // 2
        swap = remote(24 + at, final.at[1 - me.c, here], out.at[me.c, here], sibling)
        keep = pltpu.make_async_copy(final.at[me.c, here], out.at[me.c, here], local.at[1 + at])
        swap.start()
        keep.start()
        return swap, keep

    total = part_b[ORDER[0, 0]].astype(F32)
    x_first[0].wait_recv()
    total = total + bx[0].astype(F32)
    for n in (1, 2, 3):
        z_second[n].wait_recv()
        total = total + bz[n - 1].astype(F32)
    keep_rows(SPLIT, total)
    swaps = [place(2)]
    total = part_a[ORDER[0, 0]].astype(F32)
    for n in (1, 2, 3):
        z_first[0, n].wait_recv()
        total = total + az[0, n - 1].astype(F32)
    x_second.wait_recv()
    total = total + ax[...].astype(F32)
    keep_rows(0, total)
    swaps.append(place(0))
    for copy in w_back:
        copy.wait_recv()
    for swap, keep in swaps:
        swap.wait_recv()
        keep.wait()
    w_kept.wait()
    for copy in list(x_first.values()) + list(z_first.values()) + list(z_second.values()):
        copy.wait_send()
    for copy in [x_second, w_x] + [swap for swap, _ in swaps] + w_y + w_z + w_back:
        copy.wait_send()


PART_A, PART_B = (SPLIT, 256), (512 - SPLIT, 256)
HELD = (
    pltpu.VMEM((32, 4, 8, 16, 128), jnp.int16),
    pltpu.VMEM((8, 1024), F32),
    pltpu.VMEM((1024, 128), F32),
    pltpu.VMEM((8, 2, 128, 512), BF16),
    pltpu.VMEM((4, 128, 512), BF16),
    pltpu.VMEM((4, 256, 128), BF16),
    pltpu.VMEM((1, 512), F32),
    pltpu.VMEM((4096, 256), BF16),
    pltpu.VMEM((4, 40, 512), F32),
    pltpu.VMEM((512, 1024), BF16),
    pltpu.VMEM((512, 1024), BF16),
)
SPREAD = (
    pltpu.SMEM((4, 256), jnp.int32),
    pltpu.SMEM((1, 256), jnp.int32),
    pltpu.VMEM((1024, 128), BF16),
    pltpu.VMEM((8, 2, 128, 512), BF16),
    pltpu.VMEM((8, 128), F32),
    pltpu.VMEM((8, 8, 128), F32),
    pltpu.VMEM((8, 8, 16, 16, 128), jnp.int32),
    pltpu.VMEM((3, 8, 16, 16, 128), jnp.int16),
    pltpu.VMEM((4, 8, 16, 16, 128), jnp.int16),
    pltpu.SMEM((4, 1, 128), jnp.int32),
    pltpu.VMEM((4, 1, 128), jnp.int32),
    pltpu.VMEM((4, 1, 128), jnp.int32),
    pltpu.SMEM((4, 1, 128), jnp.int32),
    pltpu.VMEM((2, 128, 512), BF16),
    DMA((34,)),
    DMA((34,)),
    DMA((8,)),
    DMA((10,)),
)
LAYER = (
    pltpu.VMEM((256, 1024), F32),
    pltpu.VMEM((4, 2, 128, 1024), BF16),
    pltpu.VMEM((4, 128, 1024), BF16),
    pltpu.VMEM((3, 4, 128, 256), BF16),
    pltpu.VMEM((3, 4, 128, 256), BF16),
    pltpu.VMEM((3, 256, 128), BF16),
    pltpu.VMEM((4, 256, 128), BF16),
    pltpu.VMEM((128, 1024), BF16),
    pltpu.VMEM((4, 256, 512), BF16),
    pltpu.VMEM((4, 256, 128), F32),
    pltpu.VMEM((256, 256), BF16),
    DMA((4,)),
    DMA((4,)),
    DMA((12,)),
    DMA((12,)),
    DMA((24,)),
    DMA((24,)),
    DMA,
)
SETTLE = (
    pltpu.VMEM((512, 256), F32),
    pltpu.VMEM((8,) + PART_A, BF16),
    pltpu.VMEM((8,) + PART_B, BF16),
    pltpu.VMEM((2, 3) + PART_A, BF16),
    pltpu.VMEM(PART_A, BF16),
    pltpu.VMEM(PART_A, BF16),
    pltpu.VMEM((4,) + PART_B, BF16),
    pltpu.VMEM((3,) + PART_B, BF16),
    pltpu.VMEM((3,) + PART_B, BF16),
    pltpu.VMEM((1024, 128), F32),
    pltpu.VMEM((2, 512, 128), F32),
    pltpu.VMEM((4, 40, 512), F32),
    pltpu.VMEM((4, 40, 512), F32),
    pltpu.VMEM((40, 512), F32),
    pltpu.VMEM((40, 512), F32),
    pltpu.VMEM((40, 512), F32),
    DMA((26,)),
    DMA((26,)),
    DMA((3,)),
)


def all_kernel(*refs):
    groups, first = [], 0
    for size in (7, 3, len(HELD), len(SPREAD), len(LAYER), len(SETTLE)):
        groups.append(refs[first:first + size])
        first += size
    ins, (act, out, gw), held, spread_refs, layer_refs, settle_refs = groups
    dense, row, col, g, wc, cotr, bias, ball, gwx, a0, a1 = held
    me = Place()
    *arrivals, finish_spread = spread(me, *ins, dense, row, col, g, wc, cotr, bias, *spread_refs)
    finish_layer = layer(
        me, *arrivals, dense, g, row, col, wc, bias, cotr, act, ball, gwx, a0, a1, *layer_refs
    )
    settle(me, dense, col, ball, gwx, out, gw, a0, a1, *settle_refs)
    finish_layer()
    finish_spread()


def results_kernel(act, out, gw, act_out, feat_out, gw_out, gb_out, act_v, feat_v, gw_v, load, store):
    loads = [pltpu.make_async_copy(gw, gw_v, load.at[0])]
    for n in range(2):
        here = slice(n * 512, n * 512 + 512)
        loads.append(pltpu.make_async_copy(act.at[here], act_v.at[here], load.at[1 + n]))
        loads.append(pltpu.make_async_copy(out.at[here], feat_v.at[here], load.at[3 + n]))
    for copy in loads:
        copy.start()
    loads[0].wait()
    stores = [
        pltpu.make_async_copy(gw_v.at[:, 0:32], gw_out, store.at[0]),
        pltpu.make_async_copy(gw_v.at[0, 32:33], gb_out, store.at[1]),
    ]
    for copy in stores:
        copy.start()
    for n in range(2):
        here = slice(n * 512, n * 512 + 512)
        loads[1 + 2 * n].wait()
        stores.append(pltpu.make_async_copy(act_v.at[here], act_out.at[here], store.at[2 + n]))
        stores[-1].start()
        loads[2 + 2 * n].wait()
        stores.append(pltpu.make_async_copy(feat_v.at[here], feat_out.at[here], store.at[4 + n]))
        stores[-1].start()
    for copy in stores:
        copy.wait()


def body(features, weight, bias_vector, cotangent, tile_masks, tile_rows, tile_counts):
    masks = tile_masks.reshape(8, 4, 2, 16, 16, 128)
    act, out, gw = pl.pallas_call(
        all_kernel,
        out_shape=(
            jax.ShapeDtypeStruct((1024, 128), F32),
            jax.ShapeDtypeStruct((2, 512, 128), F32),
            jax.ShapeDtypeStruct((4, 40, 512), F32),
        ),
        in_specs=[HBM] * 7,
        out_specs=(HBM,) * 3,
        scratch_shapes=HELD + SPREAD + LAYER + SETTLE,
        compiler_params=pltpu.CompilerParams(
            collective_id=0, has_side_effects=True, vmem_limit_bytes=VMEM_MIB * MIB
        ),
        name="layer",
    )(tile_rows[0].T, tile_counts, masks, features, weight, bias_vector.reshape(1, 512), cotangent)
    act, out, gw, gb = pl.pallas_call(
        results_kernel,
        out_shape=(
            jax.ShapeDtypeStruct((1024, 128), F32),
            jax.ShapeDtypeStruct((1024, 128), F32),
            jax.ShapeDtypeStruct((4, 32, 512), F32),
            jax.ShapeDtypeStruct((1, 512), F32),
        ),
        in_specs=[HBM] * 3,
        out_specs=(HBM,) * 4,
        scratch_shapes=[
            pltpu.VMEM((1024, 128), F32),
            pltpu.VMEM((1024, 128), F32),
            pltpu.VMEM((4, 40, 512), F32),
            DMA((5,)),
            DMA((6,)),
        ],
        compiler_params=pltpu.CompilerParams(vmem_limit_bytes=VMEM_MIB * MIB),
        name="results",
    )(act, out.reshape(1024, 128), gw)
    return act, out, gw.reshape(128, 512), gb.reshape(512)


def solution(mesh):
    return jax.shard_map(
        body,
        mesh=mesh,
        in_specs=(
            P("blk", "rep"),
            P("rep", None),
            P(),
            P("blk", "rep"),
            P("blk", None, None, None, None),
            P("blk", None, None),
            P("blk", None),
        ),
        out_specs=(P("blk", "rep"), P("blk", "rep"), P("rep", None), P()),
        check_vma=False,
    )
```
